256 devices in a mesh: batch: 8 (over z_lo, x), expert: 32 (over y, z_hi, core).
Axes of the slice: x: 4, y: 4, z: 8 (z_hi: 4, z_lo: 2; z = z_hi * 2 + z_lo), core: 2. Of those that a mesh axis runs over, the one named last changes fastest.
Arguments:
- tokens: bfloat16 [256, 256, 1280], P(('batch', 'expert')), may hold values from -18 to 18
- slot_params: bfloat16 [1280, 64], replicated, as said below
- weight_in: bfloat16 [64, 1280, 4096], P('expert', None, 'batch'), may hold values from -0.15625 to 0.15625
- weight_out: bfloat16 [64, 4096, 1280], P('expert', 'batch'), may hold values from -0.09375 to 0.09375
- output_grad: bfloat16 [256, 256, 1280], P(('batch', 'expert')), may hold values from -6 to 6
Outputs:
- tokens_grad: bfloat16 [256, 256, 1280], P(('batch', 'expert'))
- params_grad: float32 [1280, 64], replicated
- weight_in_grad: bfloat16 [64, 1280, 4096], P('expert', None, 'batch')
- weight_out_grad: bfloat16 [64, 4096, 1280], P('expert', 'batch')
The draws below stay inside these ranges and needn't reach their ends.
Inputs may be any that keep to these rules, and one draw needn't show every extreme that they name: Every entry of slot_params is plus or minus one common magnitude, the bfloat16 value nearest to 1280 ** -0.5.
All inputs are finite; a program needn't handle non-finite values.
Results may differ from the reference program's by a relative error of at most 0.023.
Values may be sent and summed in bfloat16 or wider, within the bound.
No kernel may reach another device: no remote copies, remote signals or barrier semaphores. Data moves between devices by JAX's collectives and lax.ppermute only.
A program may use at most 64 MiB of HBM per device.

```python
import math
import jax
import jax.numpy as jnp
from jax import lax

D = 1280
PATCHES = 256
FF = 4096
EXPERTS = 64
IMAGES = 256


def sign_table(base_key):
    return (jax.random.randint(base_key, (D, EXPERTS), 0, 2) * 2 - 1).astype(jnp.float32)


def draw_slot_params(key, part):
    signs_all = sign_table(key)
    return (signs_all * D ** (-0.5)).astype(jnp.bfloat16)


def draw_tokens(key, part):
    key = jax.random.fold_in(key, 11)
    scale_key, value_key = jax.random.split(key, 2)
    scales = jnp.exp(jax.random.uniform(scale_key, (IMAGES, PATCHES, 1), jnp.float32, math.log(0.3), math.log(3.0)))
    values = jax.random.truncated_normal(value_key, -6.0, 6.0, (IMAGES, PATCHES, D), jnp.float32) * scales
    return values.astype(jnp.bfloat16)


def block_scale(own_key, extent, cuts, least, top_value):
    factor_of = 1.0
    for position, shards_of in cuts:
        draws = jax.random.uniform(jax.random.fold_in(jax.random.fold_in(own_key, 6), position), (shards_of,), jnp.float32, least / len(cuts), top_value / len(cuts))
        factor_of = factor_of * jnp.repeat(jnp.exp(draws), extent[position] // shards_of).reshape((-1,) + (1,) * (len(extent) - 1 - position))
    return factor_of


def centred(own_key, dims, scale, reach, shards=(), dtype=jnp.bfloat16):
    result = jax.random.normal(own_key, dims, jnp.float32) * scale
    if len(shards) > 0:
        result = block_scale(own_key, dims, shards, -0.22, 0.18) * result
    return jnp.clip(result, min=-reach, max=reach).astype(dtype)


def setup_inputs(seed: int = 0) -> dict:
    keys = jax.random.split(jax.random.key(seed), 6)
    return {
        "tokens": draw_tokens(jax.random.fold_in(keys[5], 71), 0),
        "slot_params": draw_slot_params(jax.random.fold_in(keys[5], 71), 0),
        "weight_in": centred(keys[2], (EXPERTS, D, FF), D ** -0.5, 0.15625, ((0, 32), (2, 8))),
        "weight_out": centred(keys[3], (EXPERTS, FF, D), FF ** -0.5, 0.09375, ((0, 32), (1, 8))),
        "output_grad": centred(keys[4], (IMAGES, PATCHES, D), 1.0, 6.0, ((0, 256),)),
    }


GELU_CUBIC = 0.044715
GELU_ROOT = math.sqrt(2.0 / math.pi)

def gelu_pair(pre_act):
    tanh_arg = GELU_ROOT * (pre_act + GELU_CUBIC * pre_act * pre_act * pre_act)
    tanh_value = jnp.tanh(tanh_arg)
    gelu_value = 0.5 * pre_act * (1.0 + tanh_value)
    gelu_slope = 0.5 * (1.0 + tanh_value) + 0.5 * pre_act * (1.0 - tanh_value * tanh_value) * GELU_ROOT * (1.0 + 3.0 * GELU_CUBIC * pre_act * pre_act)
    return (gelu_value, gelu_slope)

def expert_pass(items):
    rows_in, rows_cot, mat_in, mat_out = items
    pre_act = jnp.dot(rows_in, mat_in, preferred_element_type=jnp.float32)
    gelu_value, gelu_slope = gelu_pair(pre_act)
    activation = gelu_value.astype(jnp.bfloat16)
    slot_out = jnp.dot(activation, mat_out, preferred_element_type=jnp.float32).astype(jnp.bfloat16)
    act_grad = jnp.dot(rows_cot, mat_out.T, preferred_element_type=jnp.float32)
    pre_grad = (act_grad * gelu_slope).astype(jnp.bfloat16)
    out_grad = jnp.dot(activation.T, rows_cot, preferred_element_type=jnp.float32).astype(jnp.bfloat16)
    in_grad = jnp.dot(rows_in.T, pre_grad, preferred_element_type=jnp.float32).astype(jnp.bfloat16)
    slot_in_grad = jnp.dot(pre_grad, mat_in.T, preferred_element_type=jnp.float32).astype(jnp.bfloat16)
    return (slot_out, slot_in_grad, in_grad, out_grad)

def reference(tokens, slot_params, weight_in, weight_out, output_grad):
    tokens_wide = tokens.astype(jnp.float32)
    cot_wide = output_grad.astype(jnp.float32)
    params_wide = slot_params.astype(jnp.float32)
    logits = jnp.einsum('bmd,ds->bsm', tokens_wide, params_wide)
    dispatch = jax.nn.softmax(logits, axis=2)
    combine = jax.nn.softmax(logits, axis=1)
    dispatch_half = dispatch.astype(jnp.bfloat16)
    combine_half = combine.astype(jnp.bfloat16)
    slot_in = jnp.einsum('bsm,bmd->bsd', dispatch_half.astype(jnp.float32), tokens_wide).astype(jnp.bfloat16)
    slot_cot = jnp.einsum('bsm,bmd->bsd', combine_half.astype(jnp.float32), cot_wide).astype(jnp.bfloat16)
    results = lax.map(expert_pass, (jnp.swapaxes(slot_in, 0, 1), jnp.swapaxes(slot_cot, 0, 1), weight_in, weight_out))
    slot_out = jnp.swapaxes(results[0], 0, 1)
    slot_in_grad = jnp.swapaxes(results[1], 0, 1)
    weight_in_grad = results[2]
    weight_out_grad = results[3]
    combine_grad = jnp.einsum('bmd,bsd->bsm', cot_wide, slot_out.astype(jnp.float32))
    dispatch_grad = jnp.einsum('bmd,bsd->bsm', tokens_wide, slot_in_grad.astype(jnp.float32))
    combine_part = combine * (combine_grad - lax.optimization_barrier(jnp.sum(combine * combine_grad, axis=1, keepdims=True)))
    dispatch_part = dispatch * (dispatch_grad - lax.optimization_barrier(jnp.sum(dispatch * dispatch_grad, axis=2, keepdims=True)))
    logits_grad = (combine_part + dispatch_part).astype(jnp.bfloat16)
    direct = jnp.einsum('bsm,bsd->bmd', dispatch_half.astype(jnp.float32), slot_in_grad.astype(jnp.float32))
    through = jnp.einsum('bsm,ds->bmd', logits_grad.astype(jnp.float32), params_wide)
    tokens_grad = (direct + through).astype(jnp.bfloat16)
    params_grad = jnp.einsum('bmd,bsm->ds', tokens_wide, logits_grad.astype(jnp.float32)) / IMAGES
    return (tokens_grad, params_grad, weight_in_grad, weight_out_grad)
```

```python
import math

import jax
import jax.numpy as jnp
from jax import lax
from jax.sharding import PartitionSpec as P

GELU_CUBIC = 0.044715
GELU_ROOT = math.sqrt(2.0 / math.pi)
BF16 = jnp.bfloat16
F32 = jnp.float32

X, ZL, Y, ZH, CORE = 4, 2, 4, 4, 2
OFFSETS = [(dz, dx) for dz in range(ZL) for dx in range(X)]


def gelu_pair(pre_act):
    tanh_arg = GELU_ROOT * (pre_act + GELU_CUBIC * pre_act * pre_act * pre_act)
    tanh_value = jnp.tanh(tanh_arg)
    gelu_value = 0.5 * pre_act * (1.0 + tanh_value)
    gelu_slope = 0.5 * (1.0 + tanh_value) + 0.5 * pre_act * (
        1.0 - tanh_value * tanh_value
    ) * GELU_ROOT * (1.0 + 3.0 * GELU_CUBIC * pre_act * pre_act)
    return (gelu_value, gelu_slope)


def batch_send(value, dz, dx):
    pairs = [
        (z * X + x, ((z + dz) % ZL) * X + (x + dx) % X) for z in range(ZL) for x in range(X)
    ]
    return lax.ppermute(value, "batch", pairs)


def batch_fetch(value, dz, dx):
    return batch_send(value, -dz, -dx)


def expert_send(value, dy, dh, dc):
    pairs = []
    for y in range(Y):
        for h in range(ZH):
            for c in range(CORE):
                to = (((y + dy) % Y) * ZH + (h + dh) % ZH) * CORE + (c + dc) % CORE
                pairs.append(((y * ZH + h) * CORE + c, to))
    return lax.ppermute(value, "expert", pairs)


def thirds(width):
    tiles = width // 128
    first = -(-tiles // 3) * 128
    second = first + (tiles - first // 128 + 1) // 2 * 128
    return (slice(0, first), slice(first, second), slice(second, width))


def gather_blocks(mine):
    blocks = {(0, 0): mine}
    blocks[0, 1] = batch_fetch(mine, 0, 1)
    blocks[0, 3] = batch_fetch(mine, 0, 3)
    blocks[1, 0] = batch_fetch(mine, 1, 0)
    blocks[0, 2] = batch_fetch(blocks[0, 1], 0, 1)
    blocks[1, 3] = batch_fetch(blocks[1, 0], 0, 3)
    blocks[1, 1] = batch_fetch(blocks[0, 1], 1, 0)
    a, b, c = thirds(mine.shape[1])
    blocks[1, 2] = jnp.concatenate(
        [
            batch_fetch(blocks[1, 1][:, a], 0, 1),
            batch_fetch(blocks[1, 3][:, b], 0, 3),
            batch_fetch(blocks[0, 2][:, c], 1, 0),
        ],
        axis=1,
    )
    return blocks


def add(*terms):
    total = terms[0].astype(F32)
    for term in terms[1:]:
        total = total + term.astype(F32)
    return total.astype(BF16)


def scatter_blocks(parts):
    a, b, c = thirds(parts[0, 0].shape[1])
    far = parts[1, 2]
    got_a = batch_send(far[:, a], 0, 1)
    got_b = batch_send(far[:, b], 0, 3)
    got_c = batch_send(far[:, c], 1, 0)

    def add_cols(part, got, cols):
        return jnp.concatenate(
            [part[:, : cols.start], add(part[:, cols], got), part[:, cols.stop :]], axis=1
        )

    got_11 = batch_send(add_cols(parts[1, 1], got_a, a), 1, 0)
    got_13 = batch_send(add_cols(parts[1, 3], got_b, b), 0, 3)
    got_02 = batch_send(add_cols(parts[0, 2], got_c, c), 0, 1)
    got_01 = batch_send(add(parts[0, 1], got_11, got_02), 0, 1)
    got_03 = batch_send(parts[0, 3], 0, 3)
    got_10 = batch_send(add(parts[1, 0], got_13), 1, 0)
    return add(parts[0, 0], got_01, got_03, got_10)


def sum_all(partial):
    core = lax.axis_index("expert") % CORE
    halves = partial.reshape(CORE, partial.shape[0] // CORE, partial.shape[1])
    keep = lax.dynamic_index_in_dim(halves, core, 0, False)
    give = lax.dynamic_index_in_dim(halves, 1 - core, 0, False)
    total = add(keep, expert_send(give, 0, 0, 1))
    total = add(total, *[batch_send(total, 0, k) for k in (1, 2, 3)])
    total = add(total, *[expert_send(total, k, 0, 0) for k in (1, 2, 3)])
    total = add(total, batch_send(total, 1, 0))
    total = add(total, *[expert_send(total, 0, k, 0) for k in (1, 2, 3)])
    other = expert_send(total, 0, 0, 1)
    first = jnp.where(core == 0, total, other)
    second = jnp.where(core == 0, other, total)
    return jnp.concatenate([first, second], axis=0).astype(F32)


def body(tokens, slot_params, weight_in, weight_out, output_grad):
    tokens, output_grad = tokens[0], output_grad[0]
    width = tokens.shape[1]
    slots = slot_params.shape[1]
    groups = lax.axis_size("expert")
    each = slots // groups
    params = slot_params.reshape(width, groups, each).swapaxes(1, 2).reshape(width, slots)
    logits = jnp.einsum("md,ds->sm", tokens, params, preferred_element_type=F32)
    dispatch = jax.nn.softmax(logits, axis=1)
    combine = jax.nn.softmax(logits, axis=0)
    dispatch_half = dispatch.astype(BF16)
    combine_half = combine.astype(BF16)
    slot_in = jnp.dot(dispatch_half, tokens, preferred_element_type=F32).astype(BF16)
    slot_cot = jnp.dot(combine_half, output_grad, preferred_element_type=F32).astype(BF16)
    rows = jnp.concatenate(
        [slot_in[j * groups : (j + 1) * groups] for j in range(each)]
        + [slot_cot[j * groups : (j + 1) * groups] for j in range(each)],
        axis=1,
    )
    routed = lax.all_to_all(rows, "expert", split_axis=0, concat_axis=0, tiled=True)
    blocks = gather_blocks(routed)
    gathered = jnp.concatenate([blocks[o] for o in OFFSETS], axis=0)
    out_cols, in_cols, in_grads, out_grads = [], [], [], []
    for j in range(each):
        rows_in = gathered[:, j * width : (j + 1) * width]
        rows_cot = gathered[:, (each + j) * width : (each + j + 1) * width]
        pre_act = jnp.dot(rows_in, weight_in[j], preferred_element_type=F32)
        gelu_value, gelu_slope = gelu_pair(pre_act)
        activation = gelu_value.astype(BF16)
        out_cols.append(jnp.dot(activation, weight_out[j], preferred_element_type=F32).astype(BF16))
        act_grad = lax.dot_general(
            rows_cot, weight_out[j], (((1,), (1,)), ((), ())), preferred_element_type=F32
        )
        pre_grad = (act_grad * gelu_slope).astype(BF16)
        in_cols.append(
            lax.dot_general(
                pre_grad, weight_in[j], (((1,), (1,)), ((), ())), preferred_element_type=F32
            ).astype(BF16)
        )
        out_grads.append(
            lax.dot_general(
                activation, rows_cot, (((0,), (0,)), ((), ())), preferred_element_type=F32
            ).astype(BF16)
        )
        in_grads.append(
            lax.dot_general(
                rows_in, pre_grad, (((0,), (0,)), ((), ())), preferred_element_type=F32
            ).astype(BF16)
        )
    partial = jnp.concatenate(out_cols + in_cols, axis=1)
    parts = {o: partial[i * groups : (i + 1) * groups] for i, o in enumerate(OFFSETS)}
    share = scatter_blocks(parts)
    back = lax.all_to_all(share, "expert", split_axis=0, concat_axis=0, tiled=True)
    slot_out = jnp.concatenate([back[:, j * width : (j + 1) * width] for j in range(each)], axis=0)
    slot_in_grad = jnp.concatenate(
        [back[:, (each + j) * width : (each + j + 1) * width] for j in range(each)], axis=0
    )
    combine_grad = jnp.einsum("md,sd->sm", output_grad, slot_out, preferred_element_type=F32)
    dispatch_grad = jnp.einsum("md,sd->sm", tokens, slot_in_grad, preferred_element_type=F32)
    combine_part = combine * (combine_grad - jnp.sum(combine * combine_grad, axis=0, keepdims=True))
    dispatch_part = dispatch * (
        dispatch_grad - jnp.sum(dispatch * dispatch_grad, axis=1, keepdims=True)
    )
    logits_grad = (combine_part + dispatch_part).astype(BF16)
    tokens_grad = (
        jnp.einsum("sm,sd->md", dispatch_half, slot_in_grad, preferred_element_type=F32)
        + jnp.einsum("sm,ds->md", logits_grad, params, preferred_element_type=F32)
    ).astype(BF16)
    local_params = jnp.einsum("md,sm->ds", tokens, logits_grad, preferred_element_type=F32)
    total_images = lax.axis_size("batch") * groups
    params_grad = sum_all(local_params.astype(BF16)) / total_images
    params_grad = params_grad.reshape(width, each, groups).swapaxes(1, 2).reshape(width, slots)
    return (tokens_grad[None], params_grad, jnp.stack(in_grads), jnp.stack(out_grads))


def solution(mesh):
    in_specs = (
        P(("batch", "expert"), None, None),
        P(),
        P("expert", None, "batch"),
        P("expert", "batch", None),
        P(("batch", "expert"), None, None),
    )
    out_specs = (
        P(("batch", "expert"), None, None),
        P(),
        P("expert", None, "batch"),
        P("expert", "batch", None),
    )
    return jax.shard_map(body, mesh=mesh, in_specs=in_specs, out_specs=out_specs, check_vma=False)
```

```python
import functools
import math

import jax
import jax.numpy as jnp
from jax import lax
from jax.experimental import pallas as pl
from jax.experimental.pallas import tpu as pltpu
from jax.sharding import PartitionSpec as P

GELU_CUBIC = 0.044715
GELU_ROOT = math.sqrt(2.0 / math.pi)
BF16 = jnp.bfloat16
F32 = jnp.float32

X, ZL, Y, ZH, CORE = 4, 2, 4, 4, 2
OFFSETS = [(dz, dx) for dz in range(ZL) for dx in range(X)]


def gelu_pair(pre_act):
    tanh_arg = GELU_ROOT * (pre_act + GELU_CUBIC * pre_act * pre_act * pre_act)
    tanh_value = jnp.tanh(tanh_arg)
    gelu_value = 0.5 * pre_act * (1.0 + tanh_value)
    gelu_slope = 0.5 * (1.0 + tanh_value) + 0.5 * pre_act * (
        1.0 - tanh_value * tanh_value
    ) * GELU_ROOT * (1.0 + 3.0 * GELU_CUBIC * pre_act * pre_act)
    return (gelu_value, gelu_slope)


def batch_send(value, dz, dx):
    pairs = [
        (z * X + x, ((z + dz) % ZL) * X + (x + dx) % X) for z in range(ZL) for x in range(X)
    ]
    return lax.ppermute(value, "batch", pairs)


def batch_fetch(value, dz, dx):
    return batch_send(value, -dz, -dx)


def expert_send(value, dy, dh, dc):
    pairs = []
    for y in range(Y):
        for h in range(ZH):
            for c in range(CORE):
                to = (((y + dy) % Y) * ZH + (h + dh) % ZH) * CORE + (c + dc) % CORE
                pairs.append(((y * ZH + h) * CORE + c, to))
    return lax.ppermute(value, "expert", pairs)


def thirds(width):
    tiles = width // 128
    first = -(-tiles // 3) * 128
    second = first + (tiles - first // 128 + 1) // 2 * 128
    return (slice(0, first), slice(first, second), slice(second, width))


def gather_blocks(mine):
    blocks = {(0, 0): mine}
    blocks[0, 1] = batch_fetch(mine, 0, 1)
    blocks[0, 3] = batch_fetch(mine, 0, 3)
    blocks[1, 0] = batch_fetch(mine, 1, 0)
    blocks[0, 2] = batch_fetch(blocks[0, 1], 0, 1)
    blocks[1, 3] = batch_fetch(blocks[1, 0], 0, 3)
    blocks[1, 1] = batch_fetch(blocks[0, 1], 1, 0)
    a, b, c = thirds(mine.shape[1])
    blocks[1, 2] = jnp.concatenate(
        [
            batch_fetch(blocks[1, 1][:, a], 0, 1),
            batch_fetch(blocks[1, 3][:, b], 0, 3),
            batch_fetch(blocks[0, 2][:, c], 1, 0),
        ],
        axis=1,
    )
    return blocks


def add(*terms):
    total = terms[0].astype(F32)
    for term in terms[1:]:
        total = total + term.astype(F32)
    return total.astype(BF16)


LANES = 128


def local_kernel(kernel, outs, scratch, flops, moved, name):
    return pl.pallas_call(
        kernel,
        out_shape=outs,
        scratch_shapes=scratch,
        compiler_params=pltpu.CompilerParams(vmem_limit_bytes=32 * 1024 * 1024),
        cost_estimate=pl.CostEstimate(flops=flops, bytes_accessed=moved, transcendentals=0),
        name=name,
    )


def nt(a, b):
    return lax.dot_general(a, b, (((1,), (1,)), ((), ())), preferred_element_type=F32)


def front_kernel(each, tok_ref, cot_ref, par_ref, rows_ref, disp_ref, comb_ref, slots_ref, flat_ref):
    tiles = slots_ref.shape[0]
    groups = slots_ref.shape[1] // each
    stride = 2 * each * tiles
    logits = nt(par_ref[...], tok_ref[...])
    raised = jnp.exp(logits - jnp.max(logits, axis=1, keepdims=True))
    dispatch = raised / jnp.sum(raised, axis=1, keepdims=True)
    raised = jnp.exp(logits - jnp.max(logits, axis=0, keepdims=True))
    combine = raised / jnp.sum(raised, axis=0, keepdims=True)
    disp_ref[...] = dispatch
    comb_ref[...] = combine
    for kind, (weights, values) in enumerate(((dispatch, tok_ref), (combine, cot_ref))):
        mixed = jnp.dot(weights.astype(BF16), values[...], preferred_element_type=F32)
        for k in range(tiles):
            slots_ref[k] = mixed[:, k * LANES : (k + 1) * LANES]
            for j in range(each):
                row = (kind * each + j) * tiles + k
                flat_ref[pl.ds(row, groups, stride=stride), :] = slots_ref[
                    k, pl.ds(j, groups, stride=each), :
                ]
    rows_ref[...] = flat_ref[...].astype(BF16)


def unpack_kernel(flat_in_ref, out_ref, flat_ref):
    groups = out_ref.shape[0]
    stride = out_ref.shape[1] // LANES
    flat_ref[...] = flat_in_ref[...].astype(F32)
    for c in range(stride):
        out_ref[:, c * LANES : (c + 1) * LANES] = flat_ref[
            pl.ds(c, groups, stride=stride), :
        ].astype(BF16)


def pack_sum_kernel(a_ref, b_ref, c_ref, d_ref, out_ref, flat_ref):
    groups = a_ref.shape[0]
    stride = a_ref.shape[1] // LANES
    for c in range(stride):
        cols = slice(c * LANES, (c + 1) * LANES)
        total = a_ref[:, cols].astype(F32) + b_ref[:, cols].astype(F32)
        total = total + c_ref[:, cols].astype(F32) + d_ref[:, cols].astype(F32)
        flat_ref[pl.ds(c, groups, stride=stride), :] = total
    out_ref[...] = flat_ref[...].astype(BF16)


def final_kernel(
    each, flat_in_ref, tok_ref, cot_ref, disp_ref, comb_ref, sig_ref, grad_ref, par_ref,
    flat_ref, out_f_ref, sig_f_ref,
):
    groups = sig_ref.shape[0] // each
    tiles = sig_ref.shape[1] // LANES
    stride = 2 * each * tiles
    flat_ref[...] = flat_in_ref[...].astype(F32)
    for kind, ref in enumerate((out_f_ref, sig_f_ref)):
        for j in range(each):
            for k in range(tiles):
                row = (kind * each + j) * tiles + k
                ref[k, pl.ds(j, groups, stride=each), :] = flat_ref[
                    pl.ds(row, groups, stride=stride), :
                ]
    slot_out = jnp.concatenate([out_f_ref[k].astype(BF16) for k in range(tiles)], axis=1)
    sig = jnp.concatenate([sig_f_ref[k].astype(BF16) for k in range(tiles)], axis=1)
    sig_ref[...] = sig
    combine_grad = nt(slot_out, cot_ref[...])
    dispatch_grad = nt(sig, tok_ref[...])
    combine = comb_ref[...]
    dispatch = disp_ref[...]
    combine_part = combine * (combine_grad - jnp.sum(combine * combine_grad, axis=0, keepdims=True))
    dispatch_part = dispatch * (
        dispatch_grad - jnp.sum(dispatch * dispatch_grad, axis=1, keepdims=True)
    )
    logits_grad = (combine_part + dispatch_part).astype(BF16)
    grad_ref[...] = logits_grad
    par_ref[...] = jnp.dot(logits_grad, tok_ref[...], preferred_element_type=F32).astype(BF16)


def scatter_blocks(parts):
    a, b, c = thirds(parts[0, 0].shape[1])
    far = parts[1, 2]
    got_a = batch_send(far[:, a], 0, 1)
    got_b = batch_send(far[:, b], 0, 3)
    got_c = batch_send(far[:, c], 1, 0)

    def add_cols(part, got, cols):
        return jnp.concatenate(
            [part[:, : cols.start], add(part[:, cols], got), part[:, cols.stop :]], axis=1
        )

    got_11 = batch_send(add_cols(parts[1, 1], got_a, a), 1, 0)
    got_13 = batch_send(add_cols(parts[1, 3], got_b, b), 0, 3)
    got_02 = batch_send(add_cols(parts[0, 2], got_c, c), 0, 1)
    got_01 = batch_send(add(parts[0, 1], got_11, got_02), 0, 1)
    got_03 = batch_send(parts[0, 3], 0, 3)
    got_10 = batch_send(add(parts[1, 0], got_13), 1, 0)
    return parts[0, 0], got_01, got_03, got_10


def sum_all(partial):
    core = lax.axis_index("expert") % CORE
    x = lax.axis_index("batch") % X
    half = partial.shape[0] // CORE
    rows = half // X
    keep = lax.dynamic_slice_in_dim(partial, core * half, half)
    give = lax.dynamic_slice_in_dim(partial, (1 - core) * half, half)
    total = add(keep, expert_send(give, 0, 0, 1))
    chunks = [lax.dynamic_slice_in_dim(total, (x + k) % X * rows, rows) for k in range(X)]
    total = add(chunks[0], *[batch_send(chunks[k], 0, k) for k in range(1, X)])
    total = add(total, *[expert_send(total, k, 0, 0) for k in range(1, Y)])
    total = add(total, batch_send(total, 1, 0))
    total = add(total, *[expert_send(total, 0, k, 0) for k in range(1, ZH)])
    around = [batch_send(total, 0, k) for k in range(X - 1, 0, -1)] + [total]
    ring = jnp.concatenate(around + around, axis=0)
    total = lax.dynamic_slice_in_dim(ring, (X - 1 - x) * rows, half)
    other = expert_send(total, 0, 0, 1)
    first = jnp.where(core == 0, total, other)
    second = jnp.where(core == 0, other, total)
    return jnp.concatenate([first, second], axis=0).astype(F32)


def body(tokens, slot_params, weight_in, weight_out, output_grad):
    tokens, output_grad = tokens[0], output_grad[0]
    patches, width = tokens.shape
    slots = slot_params.shape[1]
    groups = lax.axis_size("expert")
    each = slots // groups
    tiles = width // LANES
    flat = groups * 2 * each * tiles
    params = slot_params.T
    flat_shape = jax.ShapeDtypeStruct((flat, LANES), BF16)
    square = jax.ShapeDtypeStruct((slots, patches), F32)
    dot_flops = 2 * slots * patches * width
    rows, dispatch, combine = local_kernel(
        functools.partial(front_kernel, each),
        (flat_shape, square, square),
        [pltpu.VMEM((tiles, slots, LANES), F32), pltpu.VMEM((flat, LANES), F32)],
        3 * dot_flops,
        4 * patches * width + 2 * flat * LANES,
        "front",
    )(tokens, output_grad, params)
    routed = lax.all_to_all(
        rows.reshape(groups, 2 * each * tiles, LANES), "expert", split_axis=0, concat_axis=0,
        tiled=True,
    ).reshape(flat, LANES)
    mine = local_kernel(
        unpack_kernel,
        jax.ShapeDtypeStruct((groups, 2 * each * width), BF16),
        [pltpu.VMEM((flat, LANES), F32)],
        0,
        4 * flat * LANES,
        "unpack",
    )(routed)
    blocks = gather_blocks(mine)
    gathered = jnp.concatenate([blocks[o] for o in OFFSETS], axis=0)
    out_cols, in_cols, in_grads, out_grads = [], [], [], []
    for j in range(each):
        rows_in = gathered[:, j * width : (j + 1) * width]
        rows_cot = gathered[:, (each + j) * width : (each + j + 1) * width]
        pre_act = jnp.dot(rows_in, weight_in[j], preferred_element_type=F32)
        gelu_value, gelu_slope = gelu_pair(pre_act)
        activation = gelu_value.astype(BF16)
        out_cols.append(jnp.dot(activation, weight_out[j], preferred_element_type=F32).astype(BF16))
        act_grad = lax.dot_general(
            rows_cot, weight_out[j], (((1,), (1,)), ((), ())), preferred_element_type=F32
        )
        pre_grad = (act_grad * gelu_slope).astype(BF16)
        in_cols.append(
            lax.dot_general(
                pre_grad, weight_in[j], (((1,), (1,)), ((), ())), preferred_element_type=F32
            ).astype(BF16)
        )
        out_grads.append(
            lax.dot_general(
                activation, rows_cot, (((0,), (0,)), ((), ())), preferred_element_type=F32
            ).astype(BF16)
        )
        in_grads.append(
            lax.dot_general(
                rows_in, pre_grad, (((0,), (0,)), ((), ())), preferred_element_type=F32
            ).astype(BF16)
        )
    partial = jnp.concatenate(out_cols + in_cols, axis=1)
    parts = {o: partial[i * groups : (i + 1) * groups] for i, o in enumerate(OFFSETS)}
    share = scatter_blocks(parts)
    packed = local_kernel(
        pack_sum_kernel,
        flat_shape,
        [pltpu.VMEM((flat, LANES), F32)],
        0,
        10 * flat * LANES,
        "pack_sum",
    )(*share)
    back = lax.all_to_all(
        packed.reshape(groups, 2 * each * tiles, LANES), "expert", split_axis=0, concat_axis=0,
        tiled=True,
    ).reshape(flat, LANES)
    row_shape = jax.ShapeDtypeStruct((slots, width), BF16)
    slot_in_grad, logits_grad, local_params = local_kernel(
        functools.partial(final_kernel, each),
        (row_shape, jax.ShapeDtypeStruct((slots, patches), BF16), row_shape),
        [
            pltpu.VMEM((flat, LANES), F32),
            pltpu.VMEM((tiles, slots, LANES), F32),
            pltpu.VMEM((tiles, slots, LANES), F32),
        ],
        3 * dot_flops,
        4 * patches * width + 2 * flat * LANES,
        "final",
    )(back, tokens, output_grad, dispatch, combine)
    tokens_grad = (
        jnp.einsum("sm,sd->md", dispatch.astype(BF16), slot_in_grad, preferred_element_type=F32)
        + jnp.einsum("sm,sd->md", logits_grad, params, preferred_element_type=F32)
    ).astype(BF16)
    total_images = lax.axis_size("batch") * groups
    params_grad = (sum_all(local_params) / total_images).T
    return (tokens_grad[None], params_grad, jnp.stack(in_grads), jnp.stack(out_grads))


def solution(mesh):
    in_specs = (
        P(("batch", "expert"), None, None),
        P(),
        P("expert", None, "batch"),
        P("expert", "batch", None),
        P(("batch", "expert"), None, None),
    )
    out_specs = (
        P(("batch", "expert"), None, None),
        P(),
        P("expert", None, "batch"),
        P("expert", "batch", None),
    )
    return jax.shard_map(body, mesh=mesh, in_specs=in_specs, out_specs=out_specs, check_vma=False)
```

```python
import functools
import math

import jax
import jax.numpy as jnp
from jax import lax
from jax.experimental import pallas as pl
from jax.experimental.pallas import tpu as pltpu
from jax.sharding import PartitionSpec as P

GELU_CUBIC = 0.044715
GELU_ROOT = math.sqrt(2.0 / math.pi)
BF16 = jnp.bfloat16
F32 = jnp.float32

X, ZL, Y, ZH, CORE = 4, 2, 4, 4, 2
OFFSETS = [(dz, dx) for dz in range(ZL) for dx in range(X)]


def gelu_pair(pre_act):
    tanh_arg = GELU_ROOT * (pre_act + GELU_CUBIC * pre_act * pre_act * pre_act)
    tanh_value = jnp.tanh(tanh_arg)
    gelu_value = 0.5 * pre_act * (1.0 + tanh_value)
    gelu_slope = 0.5 * (1.0 + tanh_value) + 0.5 * pre_act * (
        1.0 - tanh_value * tanh_value
    ) * GELU_ROOT * (1.0 + 3.0 * GELU_CUBIC * pre_act * pre_act)
    return (gelu_value, gelu_slope)


def batch_send(value, dz, dx):
    pairs = [
        (z * X + x, ((z + dz) % ZL) * X + (x + dx) % X) for z in range(ZL) for x in range(X)
    ]
    return lax.ppermute(value, "batch", pairs)


def batch_fetch(value, dz, dx):
    return batch_send(value, -dz, -dx)


def expert_send(value, dy, dh, dc):
    pairs = []
    for y in range(Y):
        for h in range(ZH):
            for c in range(CORE):
                to = (((y + dy) % Y) * ZH + (h + dh) % ZH) * CORE + (c + dc) % CORE
                pairs.append(((y * ZH + h) * CORE + c, to))
    return lax.ppermute(value, "expert", pairs)


def thirds(width):
    tiles = width // 128
    first = -(-tiles // 3) * 128
    second = first + (tiles - first // 128 + 1) // 2 * 128
    return (slice(0, first), slice(first, second), slice(second, width))


def gather_blocks(mine):
    blocks = {(0, 0): mine}
    blocks[0, 1] = batch_fetch(mine, 0, 1)
    blocks[0, 3] = batch_fetch(mine, 0, 3)
    blocks[1, 0] = batch_fetch(mine, 1, 0)
    blocks[0, 2] = batch_fetch(blocks[0, 1], 0, 1)
    blocks[1, 3] = batch_fetch(blocks[1, 0], 0, 3)
    blocks[1, 1] = batch_fetch(blocks[0, 1], 1, 0)
    a, b, c = thirds(mine.shape[1])
    blocks[1, 2] = jnp.concatenate(
        [
            batch_fetch(blocks[1, 1][:, a], 0, 1),
            batch_fetch(blocks[1, 3][:, b], 0, 3),
            batch_fetch(blocks[0, 2][:, c], 1, 0),
        ],
        axis=1,
    )
    return blocks


def add(*terms):
    total = terms[0].astype(F32)
    for term in terms[1:]:
        total = total + term.astype(F32)
    return total.astype(BF16)


LANES = 128


def local_kernel(kernel, outs, scratch, flops, moved, name, **specs):
    return pl.pallas_call(
        kernel,
        out_shape=outs,
        **specs,
        scratch_shapes=scratch,
        compiler_params=pltpu.CompilerParams(vmem_limit_bytes=32 * 1024 * 1024),
        cost_estimate=pl.CostEstimate(flops=flops, bytes_accessed=moved, transcendentals=0),
        name=name,
    )


def nt(a, b):
    return lax.dot_general(a, b, (((1,), (1,)), ((), ())), preferred_element_type=F32)


PIECES = 4


def tn(a, b):
    return lax.dot_general(a, b, (((0,), (0,)), ((), ())), preferred_element_type=F32)


def front_kernel(
    each, tok_hbm, cot_hbm, par_hbm, rows_ref, disp_ref, comb_ref,
    slots_ref, flat_ref, tok_ref, cot_ref, par_ref, sems,
):
    def loads(source, target, which):
        rows = source.shape[0] // PIECES
        for i in range(PIECES):
            part = pl.ds(i * rows, rows)
            copy = pltpu.make_async_copy(source.at[part], target.at[part], sems.at[which, i])
            copy.start()
            yield copy

    par_loads = list(loads(par_hbm, par_ref, 0))
    tok_loads = list(loads(tok_hbm, tok_ref, 1))
    cot_loads = list(loads(cot_hbm, cot_ref, 2))
    for copy in par_loads + tok_loads:
        copy.wait()
    tiles = slots_ref.shape[0]
    groups = slots_ref.shape[1] // each
    stride = 2 * each * tiles
    logits = nt(par_ref[...], tok_ref[...])
    raised = jnp.exp(logits - jnp.max(logits, axis=1, keepdims=True))
    dispatch = raised / jnp.sum(raised, axis=1, keepdims=True)
    raised = jnp.exp(logits - jnp.max(logits, axis=0, keepdims=True))
    combine = raised / jnp.sum(raised, axis=0, keepdims=True)
    disp_ref[...] = dispatch
    comb_ref[...] = combine
    for kind, (weights, values) in enumerate(((dispatch, tok_ref), (combine, cot_ref))):
        if kind == 1:
            for copy in cot_loads:
                copy.wait()
        mixed = jnp.dot(weights.astype(BF16), values[...], preferred_element_type=F32)
        for k in range(tiles):
            slots_ref[k] = mixed[:, k * LANES : (k + 1) * LANES]
            for j in range(each):
                row = (kind * each + j) * tiles + k
                flat_ref[pl.ds(row, groups, stride=stride), :] = slots_ref[
                    k, pl.ds(j, groups, stride=each), :
                ]
    rows_ref[...] = flat_ref[...].astype(BF16)


def unpack_kernel(flat_in_ref, out_ref, flat_ref):
    groups = out_ref.shape[0]
    stride = out_ref.shape[1] // LANES
    flat_ref[...] = flat_in_ref[...].astype(F32)
    for c in range(stride):
        out_ref[:, c * LANES : (c + 1) * LANES] = flat_ref[
            pl.ds(c, groups, stride=stride), :
        ].astype(BF16)


def pack_sum_kernel(a_ref, b_ref, c_ref, d_ref, out_ref, flat_ref):
    groups = a_ref.shape[0]
    stride = a_ref.shape[1] // LANES
    for c in range(stride):
        cols = slice(c * LANES, (c + 1) * LANES)
        total = a_ref[:, cols].astype(F32) + b_ref[:, cols].astype(F32)
        total = total + c_ref[:, cols].astype(F32) + d_ref[:, cols].astype(F32)
        flat_ref[pl.ds(c, groups, stride=stride), :] = total
    out_ref[...] = flat_ref[...].astype(BF16)


def final_kernel(
    each, flat_in_ref, tok_ref, cot_ref, disp_ref, comb_ref, sig_ref, grad_ref, par_ref,
    flat_ref, out_f_ref, sig_f_ref,
):
    groups = sig_ref.shape[0] // each
    tiles = sig_ref.shape[1] // LANES
    stride = 2 * each * tiles
    flat_ref[...] = flat_in_ref[...].astype(F32)
    for kind, ref in enumerate((out_f_ref, sig_f_ref)):
        for j in range(each):
            for k in range(tiles):
                row = (kind * each + j) * tiles + k
                ref[k, pl.ds(j, groups, stride=each), :] = flat_ref[
                    pl.ds(row, groups, stride=stride), :
                ]
    slot_out = jnp.concatenate([out_f_ref[k].astype(BF16) for k in range(tiles)], axis=1)
    sig = jnp.concatenate([sig_f_ref[k].astype(BF16) for k in range(tiles)], axis=1)
    sig_ref[...] = sig
    combine_grad = nt(slot_out, cot_ref[...])
    dispatch_grad = nt(sig, tok_ref[...])
    combine = comb_ref[...]
    dispatch = disp_ref[...]
    combine_part = combine * (combine_grad - jnp.sum(combine * combine_grad, axis=0, keepdims=True))
    dispatch_part = dispatch * (
        dispatch_grad - jnp.sum(dispatch * dispatch_grad, axis=1, keepdims=True)
    )
    logits_grad = (combine_part + dispatch_part).astype(BF16)
    grad_ref[...] = logits_grad
    par_ref[...] = jnp.dot(logits_grad, tok_ref[...], preferred_element_type=F32).astype(BF16)


def scatter_blocks(parts):
    a, b, c = thirds(parts[0, 0].shape[1])
    far = parts[1, 2]
    got_a = batch_send(far[:, a], 0, 1)
    got_b = batch_send(far[:, b], 0, 3)
    got_c = batch_send(far[:, c], 1, 0)

    def add_cols(part, got, cols):
        return jnp.concatenate(
            [part[:, : cols.start], add(part[:, cols], got), part[:, cols.stop :]], axis=1
        )

    got_11 = batch_send(add_cols(parts[1, 1], got_a, a), 1, 0)
    got_13 = batch_send(add_cols(parts[1, 3], got_b, b), 0, 3)
    got_02 = batch_send(add_cols(parts[0, 2], got_c, c), 0, 1)
    got_01 = batch_send(add(parts[0, 1], got_11, got_02), 0, 1)
    got_03 = batch_send(parts[0, 3], 0, 3)
    got_10 = batch_send(add(parts[1, 0], got_13), 1, 0)
    return parts[0, 0], got_01, got_03, got_10


def crossed_send(value, step, turn):
    pairs = []
    for z in range(ZL):
        for x in range(X):
            for y in range(Y):
                for h in range(ZH):
                    for c in range(CORE):
                        along_x = (c + turn) % 2 == 0
                        tx = (x + step) % X if along_x else x
                        ty = y if along_x else (y + step) % Y
                        here = ((z * X + x) * Y + y) * ZH + h
                        there = ((z * X + tx) * Y + ty) * ZH + h
                        pairs.append((here * CORE + c, there * CORE + c))
    return lax.ppermute(value, ("batch", "expert"), pairs)


def sum_all(partial, beside):
    core = lax.axis_index("expert") % CORE
    half = partial.shape[0] // CORE
    keep = lax.dynamic_slice_in_dim(partial, core * half, half)
    give = lax.dynamic_slice_in_dim(partial, (1 - core) * half, half)
    total = add(keep, expert_send(give, 0, 0, 1))
    total = add(total, *[crossed_send(total, k, 0) for k in range(1, X)])
    total = add(total, *[crossed_send(total, k, 1) for k in range(1, X)])
    total = add(total, batch_send(total, 1, 0))
    total, beside = lax.optimization_barrier((total, beside))
    total = add(total, *[expert_send(total, 0, k, 0) for k in range(1, ZH)])
    other = expert_send(total, 0, 0, 1)
    first = jnp.where(core == 0, total, other)
    second = jnp.where(core == 0, other, total)
    return jnp.concatenate([first, second], axis=0).astype(F32), beside


def body(tokens, slot_params, weight_in, weight_out, output_grad):
    tokens, output_grad = tokens[0], output_grad[0]
    patches, width = tokens.shape
    slots = slot_params.shape[1]
    groups = lax.axis_size("expert")
    each = slots // groups
    tiles = width // LANES
    flat = groups * 2 * each * tiles
    params = slot_params.T
    flat_shape = jax.ShapeDtypeStruct((flat, LANES), BF16)
    square = jax.ShapeDtypeStruct((slots, patches), F32)
    dot_flops = 2 * slots * patches * width
    rows, dispatch, combine = local_kernel(
        functools.partial(front_kernel, each),
        (flat_shape, square, square),
        [
            pltpu.VMEM((tiles, slots, LANES), F32),
            pltpu.VMEM((flat, LANES), F32),
            pltpu.VMEM((patches, width), BF16),
            pltpu.VMEM((patches, width), BF16),
            pltpu.VMEM((slots, width), BF16),
            pltpu.SemaphoreType.DMA((3, PIECES)),
        ],
        3 * dot_flops,
        4 * patches * width + 2 * flat * LANES,
        "front",
        in_specs=[pl.BlockSpec(memory_space=pltpu.HBM)] * 3,
    )(tokens, output_grad, params)
    routed = lax.all_to_all(
        rows.reshape(groups, 2 * each * tiles, LANES), "expert", split_axis=0, concat_axis=0,
        tiled=True,
    ).reshape(flat, LANES)
    mine = local_kernel(
        unpack_kernel,
        jax.ShapeDtypeStruct((groups, 2 * each * width), BF16),
        [pltpu.VMEM((flat, LANES), F32)],
        0,
        4 * flat * LANES,
        "unpack",
    )(routed)
    blocks = gather_blocks(mine)
    gathered = jnp.concatenate([blocks[o] for o in OFFSETS], axis=0)
    out_cols, in_cols, acts, pres = [], [], [], []
    for j in range(each):
        rows_in = gathered[:, j * width : (j + 1) * width]
        rows_cot = gathered[:, (each + j) * width : (each + j + 1) * width]
        pre_act = jnp.dot(rows_in, weight_in[j], preferred_element_type=F32)
        gelu_value, gelu_slope = gelu_pair(pre_act)
        activation = gelu_value.astype(BF16)
        out_cols.append(jnp.dot(activation, weight_out[j], preferred_element_type=F32).astype(BF16))
        act_grad = lax.dot_general(
            rows_cot, weight_out[j], (((1,), (1,)), ((), ())), preferred_element_type=F32
        )
        pre_grad = (act_grad * gelu_slope).astype(BF16)
        in_cols.append(
            lax.dot_general(
                pre_grad, weight_in[j], (((1,), (1,)), ((), ())), preferred_element_type=F32
            ).astype(BF16)
        )
        acts.append(activation)
        pres.append(pre_grad)
    partial = jnp.concatenate(out_cols + in_cols, axis=1)
    parts = {o: partial[i * groups : (i + 1) * groups] for i, o in enumerate(OFFSETS)}
    share = scatter_blocks(parts)
    packed = local_kernel(
        pack_sum_kernel,
        flat_shape,
        [pltpu.VMEM((flat, LANES), F32)],
        0,
        10 * flat * LANES,
        "pack_sum",
    )(*share)
    packed, gathered, acts, pres = lax.optimization_barrier((packed, gathered, acts, pres))
    back = lax.all_to_all(
        packed.reshape(groups, 2 * each * tiles, LANES), "expert", split_axis=0, concat_axis=0,
        tiled=True,
    ).reshape(flat, LANES)
    in_grads, out_grads = [], []
    for j in range(each):
        rows_in = gathered[:, j * width : (j + 1) * width]
        rows_cot = gathered[:, (each + j) * width : (each + j + 1) * width]
        in_grads.append(tn(rows_in, pres[j]).astype(BF16))
        out_grads.append(tn(acts[j], rows_cot).astype(BF16))
    weight_grads = (jnp.stack(in_grads), jnp.stack(out_grads))
    back, weight_grads = lax.optimization_barrier((back, weight_grads))
    row_shape = jax.ShapeDtypeStruct((slots, width), BF16)
    slot_in_grad, logits_grad, local_params = local_kernel(
        functools.partial(final_kernel, each),
        (row_shape, jax.ShapeDtypeStruct((slots, patches), BF16), row_shape),
        [
            pltpu.VMEM((flat, LANES), F32),
            pltpu.VMEM((tiles, slots, LANES), F32),
            pltpu.VMEM((tiles, slots, LANES), F32),
        ],
        3 * dot_flops,
        4 * patches * width + 2 * flat * LANES,
        "final",
    )(back, tokens, output_grad, dispatch, combine)
    tokens_grad = (
        jnp.einsum("sm,sd->md", dispatch.astype(BF16), slot_in_grad, preferred_element_type=F32)
        + jnp.einsum("sm,sd->md", logits_grad, params, preferred_element_type=F32)
    ).astype(BF16)
    total_images = lax.axis_size("batch") * groups
    params_sum, tokens_grad = sum_all(local_params, tokens_grad)
    params_grad = (params_sum / total_images).T
    return (tokens_grad[None], params_grad, *weight_grads)


def solution(mesh):
    in_specs = (
        P(("batch", "expert"), None, None),
        P(),
        P("expert", None, "batch"),
        P("expert", "batch", None),
        P(("batch", "expert"), None, None),
    )
    out_specs = (
        P(("batch", "expert"), None, None),
        P(),
        P("expert", None, "batch"),
        P("expert", "batch", None),
    )
    return jax.shard_map(body, mesh=mesh, in_specs=in_specs, out_specs=out_specs, check_vma=False)
```

```python
import functools
import math

import jax
import jax.numpy as jnp
from jax import lax
from jax.experimental import pallas as pl
from jax.experimental.pallas import tpu as pltpu
from jax.sharding import PartitionSpec as P

GELU_CUBIC = 0.044715
GELU_ROOT = math.sqrt(2.0 / math.pi)
BF16 = jnp.bfloat16
F32 = jnp.float32

X, ZL, Y, ZH, CORE = 4, 2, 4, 4, 2
OFFSETS = [(dz, dx) for dz in range(ZL) for dx in range(X)]


def gelu_pair(pre_act):
    tanh_arg = GELU_ROOT * (pre_act + GELU_CUBIC * pre_act * pre_act * pre_act)
    tanh_value = jnp.tanh(tanh_arg)
    gelu_value = 0.5 * pre_act * (1.0 + tanh_value)
    gelu_slope = 0.5 * (1.0 + tanh_value) + 0.5 * pre_act * (
        1.0 - tanh_value * tanh_value
    ) * GELU_ROOT * (1.0 + 3.0 * GELU_CUBIC * pre_act * pre_act)
    return (gelu_value, gelu_slope)


def batch_send(value, dz, dx):
    pairs = [
        (z * X + x, ((z + dz) % ZL) * X + (x + dx) % X) for z in range(ZL) for x in range(X)
    ]
    return lax.ppermute(value, "batch", pairs)


def batch_fetch(value, dz, dx):
    return batch_send(value, -dz, -dx)


def expert_send(value, dy, dh, dc):
    pairs = []
    for y in range(Y):
        for h in range(ZH):
            for c in range(CORE):
                to = (((y + dy) % Y) * ZH + (h + dh) % ZH) * CORE + (c + dc) % CORE
                pairs.append(((y * ZH + h) * CORE + c, to))
    return lax.ppermute(value, "expert", pairs)


def thirds(width):
    tiles = width // 128
    first = -(-tiles // 3) * 128
    second = first + (tiles - first // 128 + 1) // 2 * 128
    return (slice(0, first), slice(first, second), slice(second, width))


def gather_blocks(mine):
    blocks = {(0, 0): mine}
    blocks[0, 1] = batch_fetch(mine, 0, 1)
    blocks[0, 3] = batch_fetch(mine, 0, 3)
    blocks[1, 0] = batch_fetch(mine, 1, 0)
    blocks[0, 2] = batch_fetch(blocks[0, 1], 0, 1)
    blocks[1, 3] = batch_fetch(blocks[1, 0], 0, 3)
    blocks[1, 1] = batch_fetch(blocks[0, 1], 1, 0)
    a, b, c = thirds(mine.shape[1])
    blocks[1, 2] = jnp.concatenate(
        [
            batch_fetch(blocks[1, 1][:, a], 0, 1),
            batch_fetch(blocks[1, 3][:, b], 0, 3),
            batch_fetch(blocks[0, 2][:, c], 1, 0),
        ],
        axis=1,
    )
    return blocks


def add(*terms):
    total = terms[0].astype(F32)
    for term in terms[1:]:
        total = total + term.astype(F32)
    return total.astype(BF16)


LANES = 128


PIECES = 4


def start_loads(source, target, sems):
    rows = source.shape[0] // PIECES
    copies = []
    for i in range(PIECES):
        part = pl.ds(i * rows, rows)
        copies.append(pltpu.make_async_copy(source.at[part], target.at[part], sems.at[i]))
        copies[-1].start()
    return copies


def in_hbm(value):
    return pltpu.with_memory_space_constraint(value, pltpu.HBM)


def local_kernel(kernel, outs, scratch, flops, moved, name, vmem=16, **specs):
    return pl.pallas_call(
        kernel,
        out_shape=outs,
        **specs,
        scratch_shapes=scratch,
        compiler_params=pltpu.CompilerParams(vmem_limit_bytes=vmem * 1024 * 1024),
        cost_estimate=pl.CostEstimate(flops=flops, bytes_accessed=moved, transcendentals=0),
        name=name,
    )


def nt(a, b):
    return lax.dot_general(a, b, (((1,), (1,)), ((), ())), preferred_element_type=F32)


PIECES = 4


def tn(a, b):
    return lax.dot_general(a, b, (((0,), (0,)), ((), ())), preferred_element_type=F32)


def front_kernel(
    each, tok_hbm, cot_hbm, par_hbm, rows_ref, disp_ref, comb_ref,
    slots_ref, flat_ref, tok_ref, cot_ref, par_ref, sems,
):
    par_loads = start_loads(par_hbm, par_ref, sems.at[0])
    tok_loads = start_loads(tok_hbm, tok_ref, sems.at[1])
    cot_loads = start_loads(cot_hbm, cot_ref, sems.at[2])
    for copy in par_loads + tok_loads:
        copy.wait()
    tiles = slots_ref.shape[0]
    groups = slots_ref.shape[1] // each
    stride = 2 * each * tiles
    logits = nt(par_ref[...], tok_ref[...])
    raised = jnp.exp(logits - jnp.max(logits, axis=1, keepdims=True))
    dispatch = raised / jnp.sum(raised, axis=1, keepdims=True)
    raised = jnp.exp(logits - jnp.max(logits, axis=0, keepdims=True))
    combine = raised / jnp.sum(raised, axis=0, keepdims=True)
    disp_ref[...] = dispatch
    comb_ref[...] = combine
    for kind, (weights, values) in enumerate(((dispatch, tok_ref), (combine, cot_ref))):
        if kind == 1:
            for copy in cot_loads:
                copy.wait()
        mixed = jnp.dot(weights.astype(BF16), values[...], preferred_element_type=F32)
        for k in range(tiles):
            slots_ref[k] = mixed[:, k * LANES : (k + 1) * LANES]
            for j in range(each):
                row = (kind * each + j) * tiles + k
                flat_ref[pl.ds(row, groups, stride=stride), :] = slots_ref[
                    k, pl.ds(j, groups, stride=each), :
                ]
    rows_ref[...] = flat_ref[...].astype(BF16)


def unpack_kernel(flat_in_ref, out_ref, flat_ref):
    groups = out_ref.shape[0]
    stride = out_ref.shape[1] // LANES
    flat_ref[...] = flat_in_ref[...].astype(F32)
    for c in range(stride):
        out_ref[:, c * LANES : (c + 1) * LANES] = flat_ref[
            pl.ds(c, groups, stride=stride), :
        ].astype(BF16)


def pack_sum_kernel(a_ref, b_ref, c_ref, d_ref, out_ref, flat_ref):
    groups = a_ref.shape[0]
    stride = a_ref.shape[1] // LANES
    for c in range(stride):
        cols = slice(c * LANES, (c + 1) * LANES)
        total = a_ref[:, cols].astype(F32) + b_ref[:, cols].astype(F32)
        total = total + c_ref[:, cols].astype(F32) + d_ref[:, cols].astype(F32)
        flat_ref[pl.ds(c, groups, stride=stride), :] = total
    out_ref[...] = flat_ref[...].astype(BF16)


def final_kernel(
    each, flat_in_ref, tok_ref, cot_ref, disp_ref, comb_ref, sig_ref, grad_ref, par_ref,
    flat_ref, out_f_ref, sig_f_ref,
):
    groups = sig_ref.shape[0] // each
    tiles = sig_ref.shape[1] // LANES
    stride = 2 * each * tiles
    flat_ref[...] = flat_in_ref[...].astype(F32)
    for kind, ref in enumerate((out_f_ref, sig_f_ref)):
        for j in range(each):
            for k in range(tiles):
                row = (kind * each + j) * tiles + k
                ref[k, pl.ds(j, groups, stride=each), :] = flat_ref[
                    pl.ds(row, groups, stride=stride), :
                ]
    slot_out = jnp.concatenate([out_f_ref[k].astype(BF16) for k in range(tiles)], axis=1)
    sig = jnp.concatenate([sig_f_ref[k].astype(BF16) for k in range(tiles)], axis=1)
    sig_ref[...] = sig
    combine_grad = nt(slot_out, cot_ref[...])
    dispatch_grad = nt(sig, tok_ref[...])
    combine = comb_ref[...]
    dispatch = disp_ref[...]
    combine_part = combine * (combine_grad - jnp.sum(combine * combine_grad, axis=0, keepdims=True))
    dispatch_part = dispatch * (
        dispatch_grad - jnp.sum(dispatch * dispatch_grad, axis=1, keepdims=True)
    )
    logits_grad = (combine_part + dispatch_part).astype(BF16)
    grad_ref[...] = logits_grad
    par_ref[...] = jnp.dot(logits_grad, tok_ref[...], preferred_element_type=F32).astype(BF16)


def expert_kernel(count, each, *refs):
    blocks, (win_hbm, wout_hbm) = refs[:count], refs[count : count + 2]
    parts = refs[count + 2 : 2 * count + 2]
    act_ref, pre_ref, win_ref, wout_ref, sems = refs[2 * count + 2 :]
    loads = [
        (
            start_loads(win_hbm.at[j], win_ref.at[j], sems.at[0, j]),
            start_loads(wout_hbm.at[j], wout_ref.at[j], sems.at[1, j]),
        )
        for j in range(each)
    ]
    groups = blocks[0].shape[0]
    width, hidden = win_ref.shape[1:]

    def gathered(kind, j):
        cols = slice((kind * each + j) * width, (kind * each + j + 1) * width)
        return jnp.concatenate([block[:, cols] for block in blocks], axis=0)

    def spread(value, kind, j):
        cols = slice((kind * each + j) * width, (kind * each + j + 1) * width)
        value = value.astype(BF16)
        for i, part in enumerate(parts):
            part[:, cols] = value[i * groups : (i + 1) * groups]

    for j in range(each):
        hid = slice(j * hidden, (j + 1) * hidden)
        for copy in loads[j][0]:
            copy.wait()
        pre_act = jnp.dot(gathered(0, j), win_ref[j], preferred_element_type=F32)
        gelu_value, gelu_slope = gelu_pair(pre_act)
        activation = gelu_value.astype(BF16)
        act_ref[:, hid] = activation
        for copy in loads[j][1]:
            copy.wait()
        spread(jnp.dot(activation, wout_ref[j], preferred_element_type=F32), 0, j)
        pre_grad = (nt(gathered(1, j), wout_ref[j]) * gelu_slope).astype(BF16)
        pre_ref[:, hid] = pre_grad
        spread(nt(pre_grad, win_ref[j]), 1, j)


def expert_step(blocks, weight_in, weight_out):
    count = len(blocks)
    each, width, hidden = weight_in.shape
    rows = count * blocks[0].shape[0]
    kept = jax.ShapeDtypeStruct((rows, each * hidden), BF16)
    outs = local_kernel(
        functools.partial(expert_kernel, count, each),
        [jax.ShapeDtypeStruct(b.shape, BF16) for b in blocks] + [kept, kept],
        [
            pltpu.VMEM(weight_in.shape, BF16),
            pltpu.VMEM(weight_out.shape, BF16),
            pltpu.SemaphoreType.DMA((2, each, PIECES)),
        ],
        8 * rows * each * width * hidden,
        4 * each * width * hidden + 8 * rows * each * width,
        "expert",
        in_specs=[pl.BlockSpec(memory_space=pltpu.VMEM)] * count
        + [pl.BlockSpec(memory_space=pltpu.HBM)] * 2,
    )(*blocks, in_hbm(weight_in), in_hbm(weight_out))
    return outs[:count], outs[count], outs[count + 1]


def weights_kernel(count, kept, *refs):
    rows_in, rows_cot = refs[:count], refs[count : 2 * count]
    acts, pres = refs[2 * count : 2 * count + kept], refs[2 * count + kept : 2 * count + 2 * kept]
    gin_ref, gout_ref = refs[2 * count + 2 * kept :]

    def whole(parts):
        return jnp.concatenate([part[...] for part in parts], axis=0)

    gin_ref[0] = tn(whole(rows_in), whole(pres)).astype(BF16)
    gout_ref[0] = tn(whole(acts), whole(rows_cot)).astype(BF16)


def weight_gradients(blocks, acts, pres, each, width, hidden):
    count, kept, cuts = len(blocks), len(acts), 2
    groups = blocks[0].shape[0]
    rows = count * groups
    return local_kernel(
        functools.partial(weights_kernel, count, kept),
        (
            jax.ShapeDtypeStruct((each, width, hidden), BF16),
            jax.ShapeDtypeStruct((each, hidden, width), BF16),
        ),
        [],
        4 * rows * each * width * hidden,
        4 * each * width * hidden + 8 * rows * each * width,
        "weight_grads",
        grid=(each, cuts),
        in_specs=[pl.BlockSpec((groups, width // cuts), lambda e, i: (0, e * cuts + i))] * count
        + [pl.BlockSpec((groups, width), lambda e, i: (0, each + e))] * count
        + [pl.BlockSpec((a.shape[0], hidden // cuts), lambda e, i: (0, e * cuts + i)) for a in acts]
        + [pl.BlockSpec((p.shape[0], hidden), lambda e, i: (0, e)) for p in pres],
        out_specs=(
            pl.BlockSpec((1, width // cuts, hidden), lambda e, i: (e, i, 0)),
            pl.BlockSpec((1, hidden // cuts, width), lambda e, i: (e, i, 0)),
        ),
    )(*blocks, *blocks, *acts, *pres)


def scatter_blocks(parts):
    a, b, c = thirds(parts[0, 0].shape[1])
    far = parts[1, 2]
    got_a = batch_send(far[:, a], 0, 1)
    got_b = batch_send(far[:, b], 0, 3)
    got_c = batch_send(far[:, c], 1, 0)

    def add_cols(part, got, cols):
        return jnp.concatenate(
            [part[:, : cols.start], add(part[:, cols], got), part[:, cols.stop :]], axis=1
        )

    got_11 = batch_send(add_cols(parts[1, 1], got_a, a), 1, 0)
    got_13 = batch_send(add_cols(parts[1, 3], got_b, b), 0, 3)
    got_02 = batch_send(add_cols(parts[0, 2], got_c, c), 0, 1)
    got_01 = batch_send(add(parts[0, 1], got_11, got_02), 0, 1)
    got_03 = batch_send(parts[0, 3], 0, 3)
    got_10 = batch_send(add(parts[1, 0], got_13), 1, 0)
    return parts[0, 0], got_01, got_03, got_10


def crossed_send(value, step, turn):
    pairs = []
    for z in range(ZL):
        for x in range(X):
            for y in range(Y):
                for h in range(ZH):
                    for c in range(CORE):
                        along_x = (c + turn) % 2 == 0
                        tx = (x + step) % X if along_x else x
                        ty = y if along_x else (y + step) % Y
                        here = ((z * X + x) * Y + y) * ZH + h
                        there = ((z * X + tx) * Y + ty) * ZH + h
                        pairs.append((here * CORE + c, there * CORE + c))
    return lax.ppermute(value, ("batch", "expert"), pairs)


def sum_all(partial, beside):
    core = lax.axis_index("expert") % CORE
    half = partial.shape[0] // CORE
    keep = lax.dynamic_slice_in_dim(partial, core * half, half)
    give = lax.dynamic_slice_in_dim(partial, (1 - core) * half, half)
    total = add(keep, expert_send(give, 0, 0, 1))
    total = add(total, *[crossed_send(total, k, 0) for k in range(1, X)])
    total = add(total, *[crossed_send(total, k, 1) for k in range(1, X)])
    total = add(total, batch_send(total, 1, 0))
    total, beside = lax.optimization_barrier((total, beside))
    total = add(total, *[expert_send(total, 0, k, 0) for k in range(1, ZH)])
    other = expert_send(total, 0, 0, 1)
    first = jnp.where(core == 0, total, other)
    second = jnp.where(core == 0, other, total)
    return jnp.concatenate([first, second], axis=0).astype(F32), beside


def body(tokens, slot_params, weight_in, weight_out, output_grad):
    tokens, output_grad = tokens[0], output_grad[0]
    patches, width = tokens.shape
    slots = slot_params.shape[1]
    groups = lax.axis_size("expert")
    each = slots // groups
    tiles = width // LANES
    flat = groups * 2 * each * tiles
    params = slot_params.T
    flat_shape = jax.ShapeDtypeStruct((flat, LANES), BF16)
    square = jax.ShapeDtypeStruct((slots, patches), F32)
    dot_flops = 2 * slots * patches * width
    rows, dispatch, combine = local_kernel(
        functools.partial(front_kernel, each),
        (flat_shape, square, square),
        [
            pltpu.VMEM((tiles, slots, LANES), F32),
            pltpu.VMEM((flat, LANES), F32),
            pltpu.VMEM((patches, width), BF16),
            pltpu.VMEM((patches, width), BF16),
            pltpu.VMEM((slots, width), BF16),
            pltpu.SemaphoreType.DMA((3, PIECES)),
        ],
        3 * dot_flops,
        4 * patches * width + 2 * flat * LANES,
        "front",
        in_specs=[pl.BlockSpec(memory_space=pltpu.HBM)] * 3,
    )(in_hbm(tokens), in_hbm(output_grad), in_hbm(params))
    routed = lax.all_to_all(
        rows.reshape(groups, 2 * each * tiles, LANES), "expert", split_axis=0, concat_axis=0,
        tiled=True,
    ).reshape(flat, LANES)
    mine = local_kernel(
        unpack_kernel,
        jax.ShapeDtypeStruct((groups, 2 * each * width), BF16),
        [pltpu.VMEM((flat, LANES), F32)],
        0,
        4 * flat * LANES,
        "unpack",
    )(routed)
    blocks = gather_blocks(mine)
    blocks = [blocks[o] for o in OFFSETS]
    partial, act, pre = expert_step(blocks, weight_in, weight_out)
    parts = dict(zip(OFFSETS, partial))
    share = scatter_blocks(parts)
    packed = local_kernel(
        pack_sum_kernel,
        flat_shape,
        [pltpu.VMEM((flat, LANES), F32)],
        0,
        10 * flat * LANES,
        "pack_sum",
    )(*share)
    packed, act, pre = lax.optimization_barrier((packed, act, pre))
    back = lax.all_to_all(
        packed.reshape(groups, 2 * each * tiles, LANES), "expert", split_axis=0, concat_axis=0,
        tiled=True,
    ).reshape(flat, LANES)
    hidden = weight_in.shape[2]
    weight_grads = weight_gradients(blocks, [act], [pre], each, width, hidden)
    back, weight_grads = lax.optimization_barrier((back, weight_grads))
    row_shape = jax.ShapeDtypeStruct((slots, width), BF16)
    slot_in_grad, logits_grad, local_params = local_kernel(
        functools.partial(final_kernel, each),
        (row_shape, jax.ShapeDtypeStruct((slots, patches), BF16), row_shape),
        [
            pltpu.VMEM((flat, LANES), F32),
            pltpu.VMEM((tiles, slots, LANES), F32),
            pltpu.VMEM((tiles, slots, LANES), F32),
        ],
        3 * dot_flops,
        4 * patches * width + 2 * flat * LANES,
        "final",
    )(back, tokens, output_grad, dispatch, combine)
    tokens_grad = (
        jnp.einsum("sm,sd->md", dispatch.astype(BF16), slot_in_grad, preferred_element_type=F32)
        + jnp.einsum("sm,sd->md", logits_grad, params, preferred_element_type=F32)
    ).astype(BF16)
    total_images = lax.axis_size("batch") * groups
    params_sum, tokens_grad = sum_all(local_params, tokens_grad)
    params_grad = (params_sum / total_images).T
    return (tokens_grad[None], params_grad, *weight_grads)


def solution(mesh):
    in_specs = (
        P(("batch", "expert"), None, None),
        P(),
        P("expert", None, "batch"),
        P("expert", "batch", None),
        P(("batch", "expert"), None, None),
    )
    out_specs = (
        P(("batch", "expert"), None, None),
        P(),
        P("expert", None, "batch"),
        P("expert", "batch", None),
    )
    return jax.shard_map(body, mesh=mesh, in_specs=in_specs, out_specs=out_specs, check_vma=False)
```

```python
import functools
import math

import jax
import jax.numpy as jnp
from jax import lax
from jax.experimental import pallas as pl
from jax.experimental.pallas import tpu as pltpu
from jax.sharding import PartitionSpec as P

GELU_CUBIC = 0.044715
GELU_ROOT = math.sqrt(2.0 / math.pi)
BF16 = jnp.bfloat16
F32 = jnp.float32

X, ZL, Y, ZH, CORE = 4, 2, 4, 4, 2


def gelu_pair(pre_act):
    tanh_arg = GELU_ROOT * (pre_act + GELU_CUBIC * pre_act * pre_act * pre_act)
    tanh_value = jnp.tanh(tanh_arg)
    gelu_value = 0.5 * pre_act * (1.0 + tanh_value)
    gelu_slope = 0.5 * (1.0 + tanh_value) + 0.5 * pre_act * (
        1.0 - tanh_value * tanh_value
    ) * GELU_ROOT * (1.0 + 3.0 * GELU_CUBIC * pre_act * pre_act)
    return (gelu_value, gelu_slope)


def batch_send(value, dz, dx):
    pairs = [
        (z * X + x, ((z + dz) % ZL) * X + (x + dx) % X) for z in range(ZL) for x in range(X)
    ]
    return lax.ppermute(value, "batch", pairs)


def batch_fetch(value, dz, dx):
    return batch_send(value, -dz, -dx)


def expert_send(value, dy, dh, dc):
    pairs = []
    for y in range(Y):
        for h in range(ZH):
            for c in range(CORE):
                to = (((y + dy) % Y) * ZH + (h + dh) % ZH) * CORE + (c + dc) % CORE
                pairs.append(((y * ZH + h) * CORE + c, to))
    return lax.ppermute(value, "expert", pairs)


def add(*terms):
    total = terms[0].astype(F32)
    for term in terms[1:]:
        total = total + term.astype(F32)
    return total.astype(BF16)


def together(*values):
    return lax.optimization_barrier(values)


def gather_near(mine):
    return batch_fetch(mine, 0, 1), batch_fetch(mine, 0, 3), batch_fetch(mine, 1, 0)


def gather_next(near):
    b01, b03, b10 = near
    return batch_fetch(b01, 0, 1), batch_fetch(b10, 0, 3), batch_fetch(b01, 1, 0)


def gather_far(nexts, side):
    b02, b13, b11 = nexts
    return batch_fetch(b11, 0, 1) if side == 0 else batch_fetch(b13, 0, 3)


def by_offset(mine, near, nexts, far):
    return [mine, near[0], nexts[0], near[1], near[2], nexts[2], far, nexts[1]]


def scatter_far(parts, side):
    p00, p01, p02, p03, p10, p11, p12, p13 = parts
    return batch_send(p12, 0, 1 if side == 0 else 3), batch_send(p03, 0, 3)


def scatter_next(parts, got, side):
    p00, p01, p02, p03, p10, p11, p12, p13 = parts
    if side == 0:
        p11 = add(p11, got)
    else:
        p13 = add(p13, got)
    return batch_send(p02, 0, 1), batch_send(p13, 0, 3), batch_send(p11, 1, 0)


def scatter_near(parts, got):
    p01 = add(parts[1], got[0], got[2])
    p10 = add(parts[4], got[1])
    return batch_send(p01, 0, 1), batch_send(p10, 1, 0)


LANES = 128


PIECES = 4


def start_loads(source, target, sems):
    rows = source.shape[0] // PIECES
    copies = []
    for i in range(PIECES):
        part = pl.ds(i * rows, rows)
        copies.append(pltpu.make_async_copy(source.at[part], target.at[part], sems.at[i]))
        copies[-1].start()
    return copies


def in_hbm(value):
    return pltpu.with_memory_space_constraint(value, pltpu.HBM)


def local_kernel(kernel, outs, scratch, flops, moved, name, vmem=16, **specs):
    return pl.pallas_call(
        kernel,
        out_shape=outs,
        **specs,
        scratch_shapes=scratch,
        compiler_params=pltpu.CompilerParams(vmem_limit_bytes=vmem * 1024 * 1024),
        cost_estimate=pl.CostEstimate(flops=flops, bytes_accessed=moved, transcendentals=0),
        name=name,
    )


def nt(a, b):
    return lax.dot_general(a, b, (((1,), (1,)), ((), ())), preferred_element_type=F32)


PIECES = 4


def tn(a, b):
    return lax.dot_general(a, b, (((0,), (0,)), ((), ())), preferred_element_type=F32)


def front_kernel(
    each, tok_hbm, cot_hbm, par_hbm, rows_ref, disp_ref, comb_ref,
    slots_ref, flat_ref, tok_ref, cot_ref, par_ref, sems,
):
    par_loads = start_loads(par_hbm, par_ref, sems.at[0])
    tok_loads = start_loads(tok_hbm, tok_ref, sems.at[1])
    cot_loads = start_loads(cot_hbm, cot_ref, sems.at[2])
    for copy in par_loads + tok_loads:
        copy.wait()
    tiles = slots_ref.shape[0]
    groups = slots_ref.shape[1] // each
    stride = 2 * each * tiles
    logits = nt(par_ref[...], tok_ref[...])
    raised = jnp.exp(logits - jnp.max(logits, axis=1, keepdims=True))
    dispatch = raised / jnp.sum(raised, axis=1, keepdims=True)
    raised = jnp.exp(logits - jnp.max(logits, axis=0, keepdims=True))
    combine = raised / jnp.sum(raised, axis=0, keepdims=True)
    disp_ref[...] = dispatch
    comb_ref[...] = combine
    for kind, (weights, values) in enumerate(((dispatch, tok_ref), (combine, cot_ref))):
        if kind == 1:
            for copy in cot_loads:
                copy.wait()
        mixed = jnp.dot(weights.astype(BF16), values[...], preferred_element_type=F32)
        for k in range(tiles):
            slots_ref[k] = mixed[:, k * LANES : (k + 1) * LANES]
            for j in range(each):
                row = (kind * each + j) * tiles + k
                flat_ref[pl.ds(row, groups, stride=stride), :] = slots_ref[
                    k, pl.ds(j, groups, stride=each), :
                ]
    rows_ref[...] = flat_ref[...].astype(BF16)


def unpack_kernel(flat_in_ref, ins_ref, cots_ref, flat_ref):
    groups = ins_ref.shape[0]
    tiles = ins_ref.shape[1] // LANES
    flat_ref[...] = flat_in_ref[...].astype(F32)
    for kind, out_ref in enumerate((ins_ref, cots_ref)):
        for c in range(tiles):
            out_ref[:, c * LANES : (c + 1) * LANES] = flat_ref[
                pl.ds(kind * tiles + c, groups, stride=2 * tiles), :
            ].astype(BF16)


def pack_sum_kernel(*refs):
    out_ref, flat_ref = refs[-2:]
    groups = refs[0].shape[0]
    tiles = refs[0].shape[1] // LANES
    for kind in range(2):
        terms = refs[4 * kind : 4 * kind + 4]
        for c in range(tiles):
            cols = slice(c * LANES, (c + 1) * LANES)
            total = terms[0][:, cols].astype(F32)
            for term in terms[1:]:
                total = total + term[:, cols].astype(F32)
            flat_ref[pl.ds(kind * tiles + c, groups, stride=2 * tiles), :] = total
    out_ref[...] = flat_ref[...].astype(BF16)


def final_kernel(
    each, flat_in_ref, tok_ref, cot_ref, disp_ref, comb_ref, sig_ref, grad_ref, par_ref,
    flat_ref, out_f_ref, sig_f_ref,
):
    groups = sig_ref.shape[0] // each
    tiles = sig_ref.shape[1] // LANES
    stride = 2 * each * tiles
    flat_ref[...] = flat_in_ref[...].astype(F32)
    for kind, ref in enumerate((out_f_ref, sig_f_ref)):
        for j in range(each):
            for k in range(tiles):
                row = (kind * each + j) * tiles + k
                ref[k, pl.ds(j, groups, stride=each), :] = flat_ref[
                    pl.ds(row, groups, stride=stride), :
                ]
    slot_out = jnp.concatenate([out_f_ref[k].astype(BF16) for k in range(tiles)], axis=1)
    sig = jnp.concatenate([sig_f_ref[k].astype(BF16) for k in range(tiles)], axis=1)
    sig_ref[...] = sig
    combine_grad = nt(slot_out, cot_ref[...])
    dispatch_grad = nt(sig, tok_ref[...])
    combine = comb_ref[...]
    dispatch = disp_ref[...]
    combine_part = combine * (combine_grad - jnp.sum(combine * combine_grad, axis=0, keepdims=True))
    dispatch_part = dispatch * (
        dispatch_grad - jnp.sum(dispatch * dispatch_grad, axis=1, keepdims=True)
    )
    logits_grad = (combine_part + dispatch_part).astype(BF16)
    grad_ref[...] = logits_grad
    par_ref[...] = jnp.dot(logits_grad, tok_ref[...], preferred_element_type=F32).astype(BF16)


def gathered(blocks, j, width):
    return jnp.concatenate([b[:, j * width : (j + 1) * width] for b in blocks], axis=0)


def spread(parts, value, j, width):
    value = value.astype(BF16)
    groups = parts[0].shape[0]
    for i, part in enumerate(parts):
        part[:, j * width : (j + 1) * width] = value[i * groups : (i + 1) * groups]


def wait_all(copies):
    for copy in copies:
        copy.wait()


def forward_kernel(count, each, *refs):
    blocks, (win_hbm, wout_hbm) = refs[:count], refs[count : count + 2]
    parts = refs[count + 2 : 2 * count + 2]
    act_ref, slope_ref, win_ref, wout_ref, sems = refs[2 * count + 2 :]
    width, hidden = win_ref.shape[1:]
    win_loads = [start_loads(win_hbm.at[j], win_ref.at[j], sems.at[0, j]) for j in range(each)]
    wout_loads = [start_loads(wout_hbm.at[j], wout_ref.at[j], sems.at[1, j]) for j in range(each)]
    for j in range(each):
        hid = slice(j * hidden, (j + 1) * hidden)
        wait_all(win_loads[j])
        pre_act = jnp.dot(gathered(blocks, j, width), win_ref[j], preferred_element_type=F32)
        gelu_value, slope_ref[:, hid] = gelu_pair(pre_act)
        act_ref[:, hid] = gelu_value.astype(BF16)
    for j in range(each):
        hid = slice(j * hidden, (j + 1) * hidden)
        wait_all(wout_loads[j])
        spread(parts, jnp.dot(act_ref[:, hid], wout_ref[j], preferred_element_type=F32), j, width)


def backward_kernel(count, each, *refs):
    blocks, (slope_ref, win_hbm, wout_hbm) = refs[:count], refs[count : count + 3]
    parts = refs[count + 3 : 2 * count + 3]
    pre_ref, win_ref, wout_ref, sems = refs[2 * count + 3 :]
    width, hidden = win_ref.shape[1:]
    wout_loads = [start_loads(wout_hbm.at[j], wout_ref.at[j], sems.at[1, j]) for j in range(each)]
    win_loads = [start_loads(win_hbm.at[j], win_ref.at[j], sems.at[0, j]) for j in range(each)]
    for j in range(each):
        hid = slice(j * hidden, (j + 1) * hidden)
        wait_all(wout_loads[j])
        act_grad = nt(gathered(blocks, j, width), wout_ref[j])
        pre_ref[:, hid] = (act_grad * slope_ref[:, hid]).astype(BF16)
    for j in range(each):
        hid = slice(j * hidden, (j + 1) * hidden)
        wait_all(win_loads[j])
        spread(parts, nt(pre_ref[:, hid], win_ref[j]), j, width)


def expert_step(kernel, name, blocks, extra, kept, weight_in, weight_out):
    count = len(blocks)
    each, width, hidden = weight_in.shape
    rows = count * blocks[0].shape[0]
    in_vmem, hbm = pl.BlockSpec(memory_space=pltpu.VMEM), pl.BlockSpec(memory_space=pltpu.HBM)
    outs = local_kernel(
        functools.partial(kernel, count, each),
        [jax.ShapeDtypeStruct(b.shape, BF16) for b in blocks]
        + [jax.ShapeDtypeStruct((rows, each * hidden), t) for t in kept],
        [
            pltpu.VMEM(weight_in.shape, BF16),
            pltpu.VMEM(weight_out.shape, BF16),
            pltpu.SemaphoreType.DMA((2, each, PIECES)),
        ],
        4 * rows * each * width * hidden,
        4 * each * width * hidden + 4 * rows * each * width,
        name,
        in_specs=[in_vmem] * (count + len(extra)) + [hbm] * 2,
    )(*blocks, *extra, in_hbm(weight_in), in_hbm(weight_out))
    return outs[:count], *outs[count:]


def weights_kernel(count, kept, *refs):
    rows_in, rows_cot = refs[:count], refs[count : 2 * count]
    acts, pres = refs[2 * count : 2 * count + kept], refs[2 * count + kept : 2 * count + 2 * kept]
    gin_ref, gout_ref = refs[2 * count + 2 * kept :]

    def whole(parts):
        return jnp.concatenate([part[...] for part in parts], axis=0)

    gin_ref[0] = tn(whole(rows_in), whole(pres)).astype(BF16)
    gout_ref[0] = tn(whole(acts), whole(rows_cot)).astype(BF16)


def weight_gradients(ins, cots, acts, pres, each, width, hidden):
    count, kept, cuts = len(ins), len(acts), 2
    groups = ins[0].shape[0]
    rows = count * groups
    return local_kernel(
        functools.partial(weights_kernel, count, kept),
        (
            jax.ShapeDtypeStruct((each, width, hidden), BF16),
            jax.ShapeDtypeStruct((each, hidden, width), BF16),
        ),
        [],
        4 * rows * each * width * hidden,
        4 * each * width * hidden + 8 * rows * each * width,
        "weight_grads",
        grid=(each, cuts),
        in_specs=[pl.BlockSpec((groups, width // cuts), lambda e, i: (0, e * cuts + i))] * count
        + [pl.BlockSpec((groups, width), lambda e, i: (0, e))] * count
        + [pl.BlockSpec((a.shape[0], hidden // cuts), lambda e, i: (0, e * cuts + i)) for a in acts]
        + [pl.BlockSpec((p.shape[0], hidden), lambda e, i: (0, e)) for p in pres],
        out_specs=(
            pl.BlockSpec((1, width // cuts, hidden), lambda e, i: (e, i, 0)),
            pl.BlockSpec((1, hidden // cuts, width), lambda e, i: (e, i, 0)),
        ),
    )(*ins, *cots, *acts, *pres)


def crossed_send(value, step, turn):
    pairs = []
    for z in range(ZL):
        for x in range(X):
            for y in range(Y):
                for h in range(ZH):
                    for c in range(CORE):
                        along_x = (c + turn) % 2 == 0
                        tx = (x + step) % X if along_x else x
                        ty = y if along_x else (y + step) % Y
                        here = ((z * X + x) * Y + y) * ZH + h
                        there = ((z * X + tx) * Y + ty) * ZH + h
                        pairs.append((here * CORE + c, there * CORE + c))
    return lax.ppermute(value, ("batch", "expert"), pairs)


def sum_all(partial, beside):
    core = lax.axis_index("expert") % CORE
    half = partial.shape[0] // CORE
    keep = lax.dynamic_slice_in_dim(partial, core * half, half)
    give = lax.dynamic_slice_in_dim(partial, (1 - core) * half, half)
    total = add(keep, expert_send(give, 0, 0, 1))
    total = add(total, *[crossed_send(total, k, 0) for k in range(1, X)])
    total = add(total, *[crossed_send(total, k, 1) for k in range(1, X)])
    total = add(total, batch_send(total, 1, 0))
    total, beside = lax.optimization_barrier((total, beside))
    total = add(total, *[expert_send(total, 0, k, 0) for k in range(1, ZH)])
    other = expert_send(total, 0, 0, 1)
    first = jnp.where(core == 0, total, other)
    second = jnp.where(core == 0, other, total)
    return jnp.concatenate([first, second], axis=0).astype(F32), beside


def body(tokens, slot_params, weight_in, weight_out, output_grad):
    tokens, output_grad = tokens[0], output_grad[0]
    patches, width = tokens.shape
    slots = slot_params.shape[1]
    groups = lax.axis_size("expert")
    each = slots // groups
    tiles = width // LANES
    flat = groups * 2 * each * tiles
    params = slot_params.T
    flat_shape = jax.ShapeDtypeStruct((flat, LANES), BF16)
    square = jax.ShapeDtypeStruct((slots, patches), F32)
    dot_flops = 2 * slots * patches * width
    rows, dispatch, combine = local_kernel(
        functools.partial(front_kernel, each),
        (flat_shape, square, square),
        [
            pltpu.VMEM((tiles, slots, LANES), F32),
            pltpu.VMEM((flat, LANES), F32),
            pltpu.VMEM((patches, width), BF16),
            pltpu.VMEM((patches, width), BF16),
            pltpu.VMEM((slots, width), BF16),
            pltpu.SemaphoreType.DMA((3, PIECES)),
        ],
        3 * dot_flops,
        4 * patches * width + 2 * flat * LANES,
        "front",
        in_specs=[pl.BlockSpec(memory_space=pltpu.HBM)] * 3,
    )(in_hbm(tokens), in_hbm(output_grad), in_hbm(params))
    routed = lax.all_to_all(
        rows.reshape(groups, 2 * each * tiles, LANES), "expert", split_axis=0, concat_axis=0,
        tiled=True,
    ).reshape(flat, LANES)
    half_shape = jax.ShapeDtypeStruct((groups, each * width), BF16)
    ins, cots = local_kernel(
        unpack_kernel,
        (half_shape, half_shape),
        [pltpu.VMEM((flat, LANES), F32)],
        0,
        4 * flat * LANES,
        "unpack",
    )(routed)
    near_a = gather_near(ins)
    near_b = gather_near(cots)
    near_a = together(*near_a)
    next_a = gather_next(near_a)
    near_b = together(*near_b)
    next_b = gather_next(near_b)
    next_a = together(*next_a)
    far_a = gather_far(next_a, 0)
    next_b = together(*next_b)
    far_b = gather_far(next_b, 1)
    blocks_a = by_offset(ins, near_a, next_a, far_a)
    blocks_b = by_offset(cots, near_b, next_b, far_b)
    parts_a, act, slope = expert_step(
        forward_kernel, "expert_forward", blocks_a, [], [BF16, F32], weight_in, weight_out
    )
    got_a, near_from_a = scatter_far(parts_a, 0)
    parts_b, pre = expert_step(
        backward_kernel, "expert_backward", blocks_b, [slope], [BF16], weight_in, weight_out
    )
    got_b, near_from_b = scatter_far(parts_b, 1)
    got_a, near_from_a = together(got_a, near_from_a)
    next_got_a = scatter_next(parts_a, got_a, 0)
    got_b, near_from_b = together(got_b, near_from_b)
    next_got_b = scatter_next(parts_b, got_b, 1)
    next_got_a = together(*next_got_a)
    near_got_a = scatter_near(parts_a, next_got_a)
    next_got_b = together(*next_got_b)
    near_got_b = scatter_near(parts_b, next_got_b)
    share = (parts_a[0], near_from_a, *near_got_a, parts_b[0], near_from_b, *near_got_b)
    packed = local_kernel(
        pack_sum_kernel,
        flat_shape,
        [pltpu.VMEM((flat, LANES), F32)],
        0,
        10 * flat * LANES,
        "pack_sum",
    )(*share)
    packed, act, pre = lax.optimization_barrier((packed, act, pre))
    back = lax.all_to_all(
        packed.reshape(groups, 2 * each * tiles, LANES), "expert", split_axis=0, concat_axis=0,
        tiled=True,
    ).reshape(flat, LANES)
    hidden = weight_in.shape[2]
    weight_grads = weight_gradients(blocks_a, blocks_b, [act], [pre], each, width, hidden)
    back, weight_grads = lax.optimization_barrier((back, weight_grads))
    row_shape = jax.ShapeDtypeStruct((slots, width), BF16)
    slot_in_grad, logits_grad, local_params = local_kernel(
        functools.partial(final_kernel, each),
        (row_shape, jax.ShapeDtypeStruct((slots, patches), BF16), row_shape),
        [
            pltpu.VMEM((flat, LANES), F32),
            pltpu.VMEM((tiles, slots, LANES), F32),
            pltpu.VMEM((tiles, slots, LANES), F32),
        ],
        3 * dot_flops,
        4 * patches * width + 2 * flat * LANES,
        "final",
    )(back, tokens, output_grad, dispatch, combine)
    tokens_grad = (
        jnp.einsum("sm,sd->md", dispatch.astype(BF16), slot_in_grad, preferred_element_type=F32)
        + jnp.einsum("sm,sd->md", logits_grad, params, preferred_element_type=F32)
    ).astype(BF16)
    total_images = lax.axis_size("batch") * groups
    params_sum, tokens_grad = sum_all(local_params, tokens_grad)
    params_grad = (params_sum / total_images).T
    return (tokens_grad[None], params_grad, *weight_grads)


def solution(mesh):
    in_specs = (
        P(("batch", "expert"), None, None),
        P(),
        P("expert", None, "batch"),
        P("expert", "batch", None),
        P(("batch", "expert"), None, None),
    )
    out_specs = (
        P(("batch", "expert"), None, None),
        P(),
        P("expert", None, "batch"),
        P("expert", "batch", None),
    )
    return jax.shard_map(body, mesh=mesh, in_specs=in_specs, out_specs=out_specs, check_vma=False)
```

```python
import functools
import math

import jax
import jax.numpy as jnp
from jax import lax
from jax.experimental import pallas as pl
from jax.experimental.pallas import tpu as pltpu
from jax.sharding import PartitionSpec as P

GELU_CUBIC = 0.044715
GELU_ROOT = math.sqrt(2.0 / math.pi)
BF16 = jnp.bfloat16
F32 = jnp.float32

X, ZL, Y, ZH, CORE = 4, 2, 4, 4, 2


def gelu_pair(pre_act):
    tanh_arg = GELU_ROOT * (pre_act + GELU_CUBIC * pre_act * pre_act * pre_act)
    tanh_value = jnp.tanh(tanh_arg)
    gelu_value = 0.5 * pre_act * (1.0 + tanh_value)
    gelu_slope = 0.5 * (1.0 + tanh_value) + 0.5 * pre_act * (
        1.0 - tanh_value * tanh_value
    ) * GELU_ROOT * (1.0 + 3.0 * GELU_CUBIC * pre_act * pre_act)
    return (gelu_value, gelu_slope)


def batch_send(value, dz, dx):
    pairs = [
        (z * X + x, ((z + dz) % ZL) * X + (x + dx) % X) for z in range(ZL) for x in range(X)
    ]
    return lax.ppermute(value, "batch", pairs)


def batch_fetch(value, dz, dx):
    return batch_send(value, -dz, -dx)


def expert_send(value, dy, dh, dc):
    pairs = []
    for y in range(Y):
        for h in range(ZH):
            for c in range(CORE):
                to = (((y + dy) % Y) * ZH + (h + dh) % ZH) * CORE + (c + dc) % CORE
                pairs.append(((y * ZH + h) * CORE + c, to))
    return lax.ppermute(value, "expert", pairs)


def add(*terms):
    total = terms[0].astype(F32)
    for term in terms[1:]:
        total = total + term.astype(F32)
    return total.astype(BF16)


def together(*values):
    return lax.optimization_barrier(values)


def gather_near(mine):
    return batch_fetch(mine, 0, 1), batch_fetch(mine, 0, 3), batch_fetch(mine, 1, 0)


def gather_next(near):
    b01, b03, b10 = near
    return batch_fetch(b01, 0, 1), batch_fetch(b10, 0, 3), batch_fetch(b01, 1, 0)


def gather_far(nexts, side):
    b02, b13, b11 = nexts
    return batch_fetch(b11, 0, 1) if side == 0 else batch_fetch(b13, 0, 3)


def by_offset(mine, near, nexts, far):
    return [mine, near[0], nexts[0], near[1], near[2], nexts[2], far, nexts[1]]


def scatter_far(parts, side):
    p00, p01, p02, p03, p10, p11, p12, p13 = parts
    return batch_send(p12, 0, 1 if side == 0 else 3), batch_send(p03, 0, 3)


def scatter_next(parts, got, side):
    p00, p01, p02, p03, p10, p11, p12, p13 = parts
    if side == 0:
        p11 = add(p11, got)
    else:
        p13 = add(p13, got)
    return batch_send(p02, 0, 1), batch_send(p13, 0, 3), batch_send(p11, 1, 0)


def scatter_near(parts, got):
    p01 = add(parts[1], got[0], got[2])
    p10 = add(parts[4], got[1])
    return batch_send(p01, 0, 1), batch_send(p10, 1, 0)


LANES = 128


PIECES = 4


def start_loads(source, target, sems):
    rows = source.shape[0] // PIECES
    copies = []
    for i in range(PIECES):
        part = pl.ds(i * rows, rows)
        copies.append(pltpu.make_async_copy(source.at[part], target.at[part], sems.at[i]))
        copies[-1].start()
    return copies


def wait_all(copies):
    for copy in copies:
        copy.wait()


in_vmem_spec = pl.BlockSpec(memory_space=pltpu.VMEM)
in_hbm_spec = pl.BlockSpec(memory_space=pltpu.HBM)


def in_hbm(value):
    return pltpu.with_memory_space_constraint(value, pltpu.HBM)


def local_kernel(kernel, outs, scratch, flops, moved, name, vmem=16, **specs):
    return pl.pallas_call(
        kernel,
        out_shape=outs,
        **specs,
        scratch_shapes=scratch,
        compiler_params=pltpu.CompilerParams(vmem_limit_bytes=vmem * 1024 * 1024),
        cost_estimate=pl.CostEstimate(flops=flops, bytes_accessed=moved, transcendentals=0),
        name=name,
    )


def nt(a, b):
    return lax.dot_general(a, b, (((1,), (1,)), ((), ())), preferred_element_type=F32)


PIECES = 4


def tn(a, b):
    return lax.dot_general(a, b, (((0,), (0,)), ((), ())), preferred_element_type=F32)


def front_kernel(
    each, tok_hbm, cot_hbm, par_hbm, rows_ref, disp_hbm, comb_hbm,
    slots_ref, flat_ref, tok_ref, cot_ref, par_ref, disp_ref, comb_ref, sems, out_sems,
):
    par_loads = start_loads(par_hbm, par_ref, sems.at[0])
    tok_loads = start_loads(tok_hbm, tok_ref, sems.at[1])
    cot_loads = start_loads(cot_hbm, cot_ref, sems.at[2])
    wait_all(par_loads + tok_loads)
    tiles = slots_ref.shape[0]
    groups = slots_ref.shape[1] // each
    stride = 2 * each * tiles
    logits = nt(par_ref[...], tok_ref[...])
    raised = jnp.exp(logits - jnp.max(logits, axis=1, keepdims=True))
    dispatch = raised / jnp.sum(raised, axis=1, keepdims=True)
    raised = jnp.exp(logits - jnp.max(logits, axis=0, keepdims=True))
    combine = raised / jnp.sum(raised, axis=0, keepdims=True)
    disp_ref[...] = dispatch
    comb_ref[...] = combine
    stores = [
        pltpu.make_async_copy(disp_ref, disp_hbm, out_sems.at[0]),
        pltpu.make_async_copy(comb_ref, comb_hbm, out_sems.at[1]),
    ]
    for copy in stores:
        copy.start()
    for kind, (weights, values) in enumerate(((dispatch, tok_ref), (combine, cot_ref))):
        if kind == 1:
            wait_all(cot_loads)
        mixed = jnp.dot(weights.astype(BF16), values[...], preferred_element_type=F32)
        for k in range(tiles):
            slots_ref[k] = mixed[:, k * LANES : (k + 1) * LANES]
            for j in range(each):
                row = (kind * each + j) * tiles + k
                flat_ref[pl.ds(row, groups, stride=stride), :] = slots_ref[
                    k, pl.ds(j, groups, stride=each), :
                ]
    rows_ref[...] = flat_ref[...].astype(BF16)
    wait_all(stores)


def unpack_kernel(flat_in_ref, ins_ref, cots_ref, flat_ref):
    groups = ins_ref.shape[0]
    tiles = ins_ref.shape[1] // LANES
    flat_ref[...] = flat_in_ref[...].astype(F32)
    for kind, out_ref in enumerate((ins_ref, cots_ref)):
        for c in range(tiles):
            out_ref[:, c * LANES : (c + 1) * LANES] = flat_ref[
                pl.ds(kind * tiles + c, groups, stride=2 * tiles), :
            ].astype(BF16)


def pack_sum_kernel(*refs):
    out_ref, flat_ref = refs[-2:]
    groups = refs[0].shape[0]
    tiles = refs[0].shape[1] // LANES
    for kind in range(2):
        terms = refs[4 * kind : 4 * kind + 4]
        for c in range(tiles):
            cols = slice(c * LANES, (c + 1) * LANES)
            total = terms[0][:, cols].astype(F32)
            for term in terms[1:]:
                total = total + term[:, cols].astype(F32)
            flat_ref[pl.ds(kind * tiles + c, groups, stride=2 * tiles), :] = total
    out_ref[...] = flat_ref[...].astype(BF16)


def final_kernel(
    each, flat_in_ref, tok_ref, cot_ref, disp_hbm, comb_hbm, sig_ref, grad_ref, par_ref,
    flat_ref, out_f_ref, sig_f_ref, disp_ref, comb_ref, sems,
):
    loads = [
        pltpu.make_async_copy(disp_hbm, disp_ref, sems.at[0]),
        pltpu.make_async_copy(comb_hbm, comb_ref, sems.at[1]),
    ]
    for copy in loads:
        copy.start()
    groups = sig_ref.shape[0] // each
    tiles = sig_ref.shape[1] // LANES
    stride = 2 * each * tiles
    flat_ref[...] = flat_in_ref[...].astype(F32)
    for kind, ref in enumerate((out_f_ref, sig_f_ref)):
        for j in range(each):
            for k in range(tiles):
                row = (kind * each + j) * tiles + k
                ref[k, pl.ds(j, groups, stride=each), :] = flat_ref[
                    pl.ds(row, groups, stride=stride), :
                ]
    slot_out = jnp.concatenate([out_f_ref[k].astype(BF16) for k in range(tiles)], axis=1)
    sig = jnp.concatenate([sig_f_ref[k].astype(BF16) for k in range(tiles)], axis=1)
    sig_ref[...] = sig
    combine_grad = nt(slot_out, cot_ref[...])
    dispatch_grad = nt(sig, tok_ref[...])
    wait_all(loads)
    combine = comb_ref[...]
    dispatch = disp_ref[...]
    combine_part = combine * (combine_grad - jnp.sum(combine * combine_grad, axis=0, keepdims=True))
    dispatch_part = dispatch * (
        dispatch_grad - jnp.sum(dispatch * dispatch_grad, axis=1, keepdims=True)
    )
    logits_grad = (combine_part + dispatch_part).astype(BF16)
    grad_ref[...] = logits_grad
    par_ref[...] = jnp.dot(logits_grad, tok_ref[...], preferred_element_type=F32).astype(BF16)


def gathered(blocks, j, width):
    return jnp.concatenate([b[:, j * width : (j + 1) * width] for b in blocks], axis=0)


def spread(parts, value, j, width):
    value = value.astype(BF16)
    groups = parts[0].shape[0]
    for i, part in enumerate(parts):
        part[:, j * width : (j + 1) * width] = value[i * groups : (i + 1) * groups]


def start_stores(sources, target, sems):
    rows = sources[0].shape[0]
    copies = []
    for i, source in enumerate(sources):
        part = target.at[pl.ds(i * rows, rows)]
        copies.append(pltpu.make_async_copy(source, part, sems.at[i]))
        copies[-1].start()
    return copies


def forward_kernel(count, each, *refs):
    blocks, (win_hbm, wout_hbm) = refs[:count], refs[count : count + 2]
    parts, (slope_ref, rows_hbm, act_hbm) = refs[count + 2 : 2 * count + 2], refs[-9:-6]
    win_ref, wout_ref, act_ref, sems, row_sems, kept_sems = refs[-6:]
    width, hidden = win_ref.shape[1:]
    win_loads = [start_loads(win_hbm.at[j], win_ref.at[j], sems.at[0, j]) for j in range(each)]
    wout_loads = [start_loads(wout_hbm.at[j], wout_ref.at[j], sems.at[1, j]) for j in range(each)]
    stores = start_stores(blocks, rows_hbm, row_sems)
    for j in range(each):
        hid = slice(j * hidden, (j + 1) * hidden)
        wait_all(win_loads[j])
        pre_act = jnp.dot(gathered(blocks, j, width), win_ref[j], preferred_element_type=F32)
        gelu_value, slope_ref[:, hid] = gelu_pair(pre_act)
        act_ref[:, hid] = gelu_value.astype(BF16)
    stores += start_stores([act_ref], act_hbm, kept_sems)
    for j in range(each):
        hid = slice(j * hidden, (j + 1) * hidden)
        wait_all(wout_loads[j])
        spread(parts, jnp.dot(act_ref[:, hid], wout_ref[j], preferred_element_type=F32), j, width)
    wait_all(stores)


def backward_kernel(count, each, *refs):
    blocks, (slope_ref, win_hbm, wout_hbm) = refs[:count], refs[count : count + 3]
    parts, (rows_hbm, pre_hbm) = refs[count + 3 : 2 * count + 3], refs[-8:-6]
    win_ref, wout_ref, pre_ref, sems, row_sems, kept_sems = refs[-6:]
    width, hidden = win_ref.shape[1:]
    wout_loads = [start_loads(wout_hbm.at[j], wout_ref.at[j], sems.at[1, j]) for j in range(each)]
    win_loads = [start_loads(win_hbm.at[j], win_ref.at[j], sems.at[0, j]) for j in range(each)]
    stores = start_stores(blocks, rows_hbm, row_sems)
    for j in range(each):
        hid = slice(j * hidden, (j + 1) * hidden)
        wait_all(wout_loads[j])
        act_grad = nt(gathered(blocks, j, width), wout_ref[j])
        pre_ref[:, hid] = (act_grad * slope_ref[:, hid]).astype(BF16)
    stores += start_stores([pre_ref], pre_hbm, kept_sems)
    for j in range(each):
        hid = slice(j * hidden, (j + 1) * hidden)
        wait_all(win_loads[j])
        spread(parts, nt(pre_ref[:, hid], win_ref[j]), j, width)
    wait_all(stores)


def expert_step(kernel, name, blocks, extra, in_place, weight_in, weight_out):
    count = len(blocks)
    each, width, hidden = weight_in.shape
    rows = count * blocks[0].shape[0]
    kept = jax.ShapeDtypeStruct((rows, each * hidden), BF16)
    outs = local_kernel(
        functools.partial(kernel, count, each),
        [jax.ShapeDtypeStruct(b.shape, BF16) for b in blocks]
        + [jax.ShapeDtypeStruct((rows, each * hidden), F32)] * in_place
        + [pltpu.HBM((rows, each * width), BF16), pltpu.HBM(kept.shape, BF16)],
        [
            pltpu.VMEM(weight_in.shape, BF16),
            pltpu.VMEM(weight_out.shape, BF16),
            pltpu.VMEM(kept.shape, BF16),
            pltpu.SemaphoreType.DMA((2, each, PIECES)),
            pltpu.SemaphoreType.DMA((count,)),
            pltpu.SemaphoreType.DMA((1,)),
        ],
        4 * rows * each * width * hidden,
        4 * each * width * hidden + 4 * rows * each * width,
        name,
        in_specs=[in_vmem_spec] * (count + len(extra)) + [in_hbm_spec] * 2,
        out_specs=[in_vmem_spec] * (count + in_place) + [in_hbm_spec] * 2,
    )(*blocks, *extra, in_hbm(weight_in), in_hbm(weight_out))
    return outs[:count], *outs[count:]


def weights_kernel(ins_ref, cots_ref, act_ref, pre_ref, gin_ref, gout_ref):
    gin_ref[0] = tn(ins_ref[...], pre_ref[...]).astype(BF16)
    gout_ref[0] = tn(act_ref[...], cots_ref[...]).astype(BF16)


def weight_gradients(ins, cots, act, pre, each):
    cuts = 2
    rows = ins.shape[0]
    width, hidden = ins.shape[1] // each, act.shape[1] // each
    return local_kernel(
        weights_kernel,
        (
            jax.ShapeDtypeStruct((each, width, hidden), BF16),
            jax.ShapeDtypeStruct((each, hidden, width), BF16),
        ),
        [],
        4 * rows * each * width * hidden,
        4 * each * width * hidden + 8 * rows * each * width,
        "weight_grads",
        grid=(each, cuts),
        in_specs=[
            pl.BlockSpec((rows, width // cuts), lambda e, i: (0, e * cuts + i)),
            pl.BlockSpec((rows, width), lambda e, i: (0, e)),
            pl.BlockSpec((rows, hidden // cuts), lambda e, i: (0, e * cuts + i)),
            pl.BlockSpec((rows, hidden), lambda e, i: (0, e)),
        ],
        out_specs=(
            pl.BlockSpec((1, width // cuts, hidden), lambda e, i: (e, i, 0)),
            pl.BlockSpec((1, hidden // cuts, width), lambda e, i: (e, i, 0)),
        ),
    )(in_hbm(ins), in_hbm(cots), in_hbm(act), in_hbm(pre))


def crossed_send(value, step, turn):
    pairs = []
    for z in range(ZL):
        for x in range(X):
            for y in range(Y):
                for h in range(ZH):
                    for c in range(CORE):
                        along_x = (c + turn) % 2 == 0
                        tx = (x + step) % X if along_x else x
                        ty = y if along_x else (y + step) % Y
                        here = ((z * X + x) * Y + y) * ZH + h
                        there = ((z * X + tx) * Y + ty) * ZH + h
                        pairs.append((here * CORE + c, there * CORE + c))
    return lax.ppermute(value, ("batch", "expert"), pairs)


def depth_swap(value, step):
    depth = ZL * ZH
    pairs = []
    for z in range(depth):
        to = (z + (step if z % 2 else -step)) % depth
        for x in range(X):
            for y in range(Y):
                for c in range(CORE):
                    here, there = (
                        ((k % ZL * X + x) * Y + y) * ZH * CORE + k // ZL * CORE + c for k in (z, to)
                    )
                    pairs.append((here, there))
    return lax.ppermute(value, ("batch", "expert"), pairs)


def sum_all(partial, beside):
    core = lax.axis_index("expert") % CORE
    half = partial.shape[0] // CORE
    keep = lax.dynamic_slice_in_dim(partial, core * half, half)
    give = lax.dynamic_slice_in_dim(partial, (1 - core) * half, half)
    total = add(keep, expert_send(give, 0, 0, 1))
    total = add(total, *[crossed_send(total, k, 0) for k in range(1, X)])
    total = add(total, *[crossed_send(total, k, 1) for k in range(1, X)])
    total = add(total, batch_send(total, 1, 0))
    total, beside = together(total, beside)
    total = add(total, depth_swap(total, 1))
    total = add(total, depth_swap(total, -3))
    other = expert_send(total, 0, 0, 1)
    first = jnp.where(core == 0, total, other)
    second = jnp.where(core == 0, other, total)
    return jnp.concatenate([first, second], axis=0).astype(F32), beside


def body(tokens, slot_params, weight_in, weight_out, output_grad):
    tokens, output_grad = tokens[0], output_grad[0]
    patches, width = tokens.shape
    slots = slot_params.shape[1]
    groups = lax.axis_size("expert")
    each = slots // groups
    tiles = width // LANES
    flat = groups * 2 * each * tiles
    params = slot_params.T
    flat_shape = jax.ShapeDtypeStruct((flat, LANES), BF16)
    square = pltpu.HBM((slots, patches), F32)
    dot_flops = 2 * slots * patches * width
    rows, dispatch, combine = local_kernel(
        functools.partial(front_kernel, each),
        (flat_shape, square, square),
        [
            pltpu.VMEM((tiles, slots, LANES), F32),
            pltpu.VMEM((flat, LANES), F32),
            pltpu.VMEM((patches, width), BF16),
            pltpu.VMEM((patches, width), BF16),
            pltpu.VMEM((slots, width), BF16),
            pltpu.VMEM((slots, patches), F32),
            pltpu.VMEM((slots, patches), F32),
            pltpu.SemaphoreType.DMA((3, PIECES)),
            pltpu.SemaphoreType.DMA((2,)),
        ],
        3 * dot_flops,
        4 * patches * width + 2 * flat * LANES,
        "front",
        in_specs=[in_hbm_spec] * 3,
        out_specs=(in_vmem_spec, in_hbm_spec, in_hbm_spec),
    )(in_hbm(tokens), in_hbm(output_grad), in_hbm(params))
    routed = lax.all_to_all(
        rows.reshape(groups, 2 * each * tiles, LANES), "expert", split_axis=0, concat_axis=0,
        tiled=True,
    ).reshape(flat, LANES)
    half_shape = jax.ShapeDtypeStruct((groups, each * width), BF16)
    ins, cots = local_kernel(
        unpack_kernel,
        (half_shape, half_shape),
        [pltpu.VMEM((flat, LANES), F32)],
        0,
        4 * flat * LANES,
        "unpack",
    )(routed)
    near_a = gather_near(ins)
    near_b = gather_near(cots)
    near_a = together(*near_a)
    next_a = gather_next(near_a)
    near_b = together(*near_b)
    next_b = gather_next(near_b)
    next_a = together(*next_a)
    far_a = gather_far(next_a, 0)
    next_b = together(*next_b)
    far_b = gather_far(next_b, 1)
    blocks_a = by_offset(ins, near_a, next_a, far_a)
    blocks_b = by_offset(cots, near_b, next_b, far_b)
    parts_a, slope, rows_a, act = expert_step(
        forward_kernel, "expert_forward", blocks_a, [], 1, weight_in, weight_out
    )
    got_a, near_from_a = scatter_far(parts_a, 0)
    parts_b, rows_b, pre = expert_step(
        backward_kernel, "expert_backward", blocks_b, [slope], 0, weight_in, weight_out
    )
    got_a, near_from_a, parts_a, pre = together(got_a, near_from_a, parts_a, pre)
    got_b, near_from_b = scatter_far(parts_b, 1)
    next_got_a = scatter_next(parts_a, got_a, 0)
    got_b, near_from_b = together(got_b, near_from_b)
    next_got_b = scatter_next(parts_b, got_b, 1)
    next_got_a = together(*next_got_a)
    near_got_a = scatter_near(parts_a, next_got_a)
    next_got_b = together(*next_got_b)
    near_got_b = scatter_near(parts_b, next_got_b)
    share = (parts_a[0], near_from_a, *near_got_a, parts_b[0], near_from_b, *near_got_b)
    packed = local_kernel(
        pack_sum_kernel,
        flat_shape,
        [pltpu.VMEM((flat, LANES), F32)],
        0,
        10 * flat * LANES,
        "pack_sum",
    )(*share)
    packed, act, pre = together(packed, act, pre)
    back = lax.all_to_all(
        packed.reshape(groups, 2 * each * tiles, LANES), "expert", split_axis=0, concat_axis=0,
        tiled=True,
    ).reshape(flat, LANES)
    weight_grads = weight_gradients(rows_a, rows_b, act, pre, each)
    back, weight_grads = lax.optimization_barrier((back, weight_grads))
    row_shape = jax.ShapeDtypeStruct((slots, width), BF16)
    slot_in_grad, logits_grad, local_params = local_kernel(
        functools.partial(final_kernel, each),
        (row_shape, jax.ShapeDtypeStruct((slots, patches), BF16), row_shape),
        [
            pltpu.VMEM((flat, LANES), F32),
            pltpu.VMEM((tiles, slots, LANES), F32),
            pltpu.VMEM((tiles, slots, LANES), F32),
            pltpu.VMEM((slots, patches), F32),
            pltpu.VMEM((slots, patches), F32),
            pltpu.SemaphoreType.DMA((2,)),
        ],
        3 * dot_flops,
        4 * patches * width + 2 * flat * LANES,
        "final",
        in_specs=[in_vmem_spec] * 3 + [in_hbm_spec] * 2,
    )(back, tokens, output_grad, in_hbm(dispatch), in_hbm(combine))
    tokens_grad = (
        jnp.einsum("sm,sd->md", dispatch.astype(BF16), slot_in_grad, preferred_element_type=F32)
        + jnp.einsum("sm,sd->md", logits_grad, params, preferred_element_type=F32)
    ).astype(BF16)
    total_images = lax.axis_size("batch") * groups
    params_sum, tokens_grad = sum_all(local_params, tokens_grad)
    params_grad = (params_sum / total_images).T
    return (tokens_grad[None], params_grad, *weight_grads)


def solution(mesh):
    in_specs = (
        P(("batch", "expert"), None, None),
        P(),
        P("expert", None, "batch"),
        P("expert", "batch", None),
        P(("batch", "expert"), None, None),
    )
    out_specs = (
        P(("batch", "expert"), None, None),
        P(),
        P("expert", None, "batch"),
        P("expert", "batch", None),
    )
    return jax.shard_map(body, mesh=mesh, in_specs=in_specs, out_specs=out_specs, check_vma=False)
```

```python
import functools
import math

import jax
import jax.numpy as jnp
from jax import lax
from jax.experimental import pallas as pl
from jax.experimental.pallas import tpu as pltpu
from jax.sharding import PartitionSpec as P

GELU_CUBIC = 0.044715
GELU_ROOT = math.sqrt(2.0 / math.pi)
BF16 = jnp.bfloat16
F32 = jnp.float32

X, ZL, Y, ZH, CORE = 4, 2, 4, 4, 2


def gelu_pair(pre_act):
    tanh_arg = GELU_ROOT * (pre_act + GELU_CUBIC * pre_act * pre_act * pre_act)
    tanh_value = jnp.tanh(tanh_arg)
    gelu_value = 0.5 * pre_act * (1.0 + tanh_value)
    gelu_slope = 0.5 * (1.0 + tanh_value) + 0.5 * pre_act * (
        1.0 - tanh_value * tanh_value
    ) * GELU_ROOT * (1.0 + 3.0 * GELU_CUBIC * pre_act * pre_act)
    return (gelu_value, gelu_slope)


def batch_send(value, dz, dx):
    pairs = [
        (z * X + x, ((z + dz) % ZL) * X + (x + dx) % X) for z in range(ZL) for x in range(X)
    ]
    return lax.ppermute(value, "batch", pairs)


def batch_fetch(value, dz, dx):
    return batch_send(value, -dz, -dx)


def expert_send(value, dy, dh, dc):
    pairs = []
    for y in range(Y):
        for h in range(ZH):
            for c in range(CORE):
                to = (((y + dy) % Y) * ZH + (h + dh) % ZH) * CORE + (c + dc) % CORE
                pairs.append(((y * ZH + h) * CORE + c, to))
    return lax.ppermute(value, "expert", pairs)


def add(*terms):
    total = terms[0].astype(F32)
    for term in terms[1:]:
        total = total + term.astype(F32)
    return total.astype(BF16)


def together(*values):
    return lax.optimization_barrier(values)


def gather_near(mine):
    return batch_fetch(mine, 0, 1), batch_fetch(mine, 0, 3), batch_fetch(mine, 1, 0)


def gather_next(near):
    b01, b03, b10 = near
    return batch_fetch(b01, 0, 1), batch_fetch(b10, 0, 3), batch_fetch(b01, 1, 0)


def gather_far(nexts, side):
    b02, b13, b11 = nexts
    return batch_fetch(b11, 0, 1) if side == 0 else batch_fetch(b13, 0, 3)


def by_offset(mine, near, nexts, far):
    return [mine, near[0], nexts[0], near[1], near[2], nexts[2], far, nexts[1]]


def scatter_first(parts):
    p00, p01, p02, p03, p10, p11, p12, p13 = parts
    return batch_send(p11, 0, 1), batch_send(p13, 0, 3), batch_send(p12, 1, 0)


def scatter_second(parts, got, side):
    p00, p01, p02, p03, p10, p11, p12, p13 = parts
    p10 = add(p10, got[0], got[1])
    p02 = add(p02, got[2])
    if side == 0:
        return batch_send(p02, 0, 1), batch_send(p03, 0, 3), batch_send(p10, 1, 0)
    return batch_send(p02, 0, 3), batch_send(p01, 0, 1), batch_send(p10, 1, 0)


def scatter_third(parts, got, side):
    if side == 0:
        return batch_send(add(parts[1], got), 0, 1)
    return batch_send(add(parts[3], got), 0, 3)


LANES = 128


PIECES = 4


def start_loads(source, target, sems):
    rows = source.shape[0] // PIECES
    copies = []
    for i in range(PIECES):
        part = pl.ds(i * rows, rows)
        copies.append(pltpu.make_async_copy(source.at[part], target.at[part], sems.at[i]))
        copies[-1].start()
    return copies


def wait_all(copies):
    for copy in copies:
        copy.wait()


in_vmem_spec = pl.BlockSpec(memory_space=pltpu.VMEM)
in_hbm_spec = pl.BlockSpec(memory_space=pltpu.HBM)


def in_hbm(value):
    return pltpu.with_memory_space_constraint(value, pltpu.HBM)


def local_kernel(kernel, outs, scratch, flops, moved, name, vmem=16, **specs):
    return pl.pallas_call(
        kernel,
        out_shape=outs,
        **specs,
        scratch_shapes=scratch,
        compiler_params=pltpu.CompilerParams(vmem_limit_bytes=vmem * 1024 * 1024),
        cost_estimate=pl.CostEstimate(flops=flops, bytes_accessed=moved, transcendentals=0),
        name=name,
    )


def nt(a, b):
    return lax.dot_general(a, b, (((1,), (1,)), ((), ())), preferred_element_type=F32)


PIECES = 4


def tn(a, b):
    return lax.dot_general(a, b, (((0,), (0,)), ((), ())), preferred_element_type=F32)


def front_kernel(
    each, tok_hbm, cot_hbm, par_hbm, rows_ref, disp_hbm, comb_hbm,
    slots_ref, flat_ref, tok_ref, cot_ref, par_ref, disp_ref, comb_ref, sems, out_sems,
):
    par_loads = start_loads(par_hbm, par_ref, sems.at[0])
    tok_loads = start_loads(tok_hbm, tok_ref, sems.at[1])
    cot_loads = start_loads(cot_hbm, cot_ref, sems.at[2])
    wait_all(par_loads + tok_loads)
    tiles = slots_ref.shape[0]
    groups = slots_ref.shape[1] // each
    stride = 2 * each * tiles
    logits = nt(par_ref[...], tok_ref[...])
    raised = jnp.exp(logits - jnp.max(logits, axis=1, keepdims=True))
    dispatch = raised / jnp.sum(raised, axis=1, keepdims=True)
    raised = jnp.exp(logits - jnp.max(logits, axis=0, keepdims=True))
    combine = raised / jnp.sum(raised, axis=0, keepdims=True)
    disp_ref[...] = dispatch
    comb_ref[...] = combine
    stores = [
        pltpu.make_async_copy(disp_ref, disp_hbm, out_sems.at[0]),
        pltpu.make_async_copy(comb_ref, comb_hbm, out_sems.at[1]),
    ]
    for copy in stores:
        copy.start()
    for kind, (weights, values) in enumerate(((dispatch, tok_ref), (combine, cot_ref))):
        if kind == 1:
            wait_all(cot_loads)
        mixed = jnp.dot(weights.astype(BF16), values[...], preferred_element_type=F32)
        for k in range(tiles):
            slots_ref[k] = mixed[:, k * LANES : (k + 1) * LANES]
            for j in range(each):
                row = (kind * each + j) * tiles + k
                flat_ref[pl.ds(row, groups, stride=stride), :] = slots_ref[
                    k, pl.ds(j, groups, stride=each), :
                ]
    rows_ref[...] = flat_ref[...].astype(BF16)
    wait_all(stores)


def unpack_kernel(flat_in_ref, ins_ref, cots_ref, flat_ref):
    groups = ins_ref.shape[0]
    tiles = ins_ref.shape[1] // LANES
    flat_ref[...] = flat_in_ref[...].astype(F32)
    for kind, out_ref in enumerate((ins_ref, cots_ref)):
        for c in range(tiles):
            out_ref[:, c * LANES : (c + 1) * LANES] = flat_ref[
                pl.ds(kind * tiles + c, groups, stride=2 * tiles), :
            ].astype(BF16)


def pack_sum_kernel(*refs):
    out_ref, flat_ref = refs[-2:]
    groups = refs[0].shape[0]
    tiles = refs[0].shape[1] // LANES
    for kind in range(2):
        terms = refs[4 * kind : 4 * kind + 4]
        for c in range(tiles):
            cols = slice(c * LANES, (c + 1) * LANES)
            total = terms[0][:, cols].astype(F32)
            for term in terms[1:]:
                total = total + term[:, cols].astype(F32)
            flat_ref[pl.ds(kind * tiles + c, groups, stride=2 * tiles), :] = total
    out_ref[...] = flat_ref[...].astype(BF16)


def final_kernel(
    each, flat_in_ref, tok_ref, cot_ref, disp_hbm, comb_hbm, sig_ref, grad_ref, par_ref,
    flat_ref, out_f_ref, sig_f_ref, disp_ref, comb_ref, sems,
):
    loads = [
        pltpu.make_async_copy(disp_hbm, disp_ref, sems.at[0]),
        pltpu.make_async_copy(comb_hbm, comb_ref, sems.at[1]),
    ]
    for copy in loads:
        copy.start()
    groups = sig_ref.shape[0] // each
    tiles = sig_ref.shape[1] // LANES
    stride = 2 * each * tiles
    flat_ref[...] = flat_in_ref[...].astype(F32)
    for kind, ref in enumerate((out_f_ref, sig_f_ref)):
        for j in range(each):
            for k in range(tiles):
                row = (kind * each + j) * tiles + k
                ref[k, pl.ds(j, groups, stride=each), :] = flat_ref[
                    pl.ds(row, groups, stride=stride), :
                ]
    slot_out = jnp.concatenate([out_f_ref[k].astype(BF16) for k in range(tiles)], axis=1)
    sig = jnp.concatenate([sig_f_ref[k].astype(BF16) for k in range(tiles)], axis=1)
    sig_ref[...] = sig
    combine_grad = nt(slot_out, cot_ref[...])
    dispatch_grad = nt(sig, tok_ref[...])
    wait_all(loads)
    combine = comb_ref[...]
    dispatch = disp_ref[...]
    combine_part = combine * (combine_grad - jnp.sum(combine * combine_grad, axis=0, keepdims=True))
    dispatch_part = dispatch * (
        dispatch_grad - jnp.sum(dispatch * dispatch_grad, axis=1, keepdims=True)
    )
    logits_grad = (combine_part + dispatch_part).astype(BF16)
    grad_ref[...] = logits_grad
    par_ref[...] = jnp.dot(logits_grad, tok_ref[...], preferred_element_type=F32).astype(BF16)


def gathered(blocks, j, width):
    return jnp.concatenate([b[:, j * width : (j + 1) * width] for b in blocks], axis=0)


def spread(parts, value, j, width):
    value = value.astype(BF16)
    groups = parts[0].shape[0]
    for i, part in enumerate(parts):
        part[:, j * width : (j + 1) * width] = value[i * groups : (i + 1) * groups]


def start_stores(sources, target, sems):
    rows = sources[0].shape[0]
    copies = []
    for i, source in enumerate(sources):
        part = target.at[pl.ds(i * rows, rows)]
        copies.append(pltpu.make_async_copy(source, part, sems.at[i]))
        copies[-1].start()
    return copies


def forward_kernel(count, each, *refs):
    blocks, (win_ref, wout_hbm) = refs[:count], refs[count : count + 2]
    parts, (slope_ref, rows_hbm, act_hbm) = refs[count + 2 : 2 * count + 2], refs[-8:-5]
    wout_ref, act_ref, sems, row_sems, kept_sems = refs[-5:]
    width, hidden = win_ref.shape[1:]
    wout_loads = [start_loads(wout_hbm.at[j], wout_ref.at[j], sems.at[j]) for j in range(each)]
    stores = start_stores(blocks, rows_hbm, row_sems)
    for j in range(each):
        hid = slice(j * hidden, (j + 1) * hidden)
        pre_act = jnp.dot(gathered(blocks, j, width), win_ref[j], preferred_element_type=F32)
        gelu_value, slope_ref[:, hid] = gelu_pair(pre_act)
        act_ref[:, hid] = gelu_value.astype(BF16)
    stores += start_stores([act_ref], act_hbm, kept_sems)
    for j in range(each):
        hid = slice(j * hidden, (j + 1) * hidden)
        wait_all(wout_loads[j])
        spread(parts, jnp.dot(act_ref[:, hid], wout_ref[j], preferred_element_type=F32), j, width)
    wait_all(stores)


def backward_kernel(count, each, *refs):
    blocks, (slope_ref, wout_ref, win_hbm) = refs[:count], refs[count : count + 3]
    parts, (rows_hbm, pre_hbm) = refs[count + 3 : 2 * count + 3], refs[-7:-5]
    win_ref, pre_ref, sems, row_sems, kept_sems = refs[-5:]
    width, hidden = win_ref.shape[1:]
    win_loads = [start_loads(win_hbm.at[j], win_ref.at[j], sems.at[j]) for j in range(each)]
    stores = start_stores(blocks, rows_hbm, row_sems)
    for j in range(each):
        hid = slice(j * hidden, (j + 1) * hidden)
        act_grad = nt(gathered(blocks, j, width), wout_ref[j])
        pre_ref[:, hid] = (act_grad * slope_ref[:, hid]).astype(BF16)
    stores += start_stores([pre_ref], pre_hbm, kept_sems)
    for j in range(each):
        hid = slice(j * hidden, (j + 1) * hidden)
        wait_all(win_loads[j])
        spread(parts, nt(pre_ref[:, hid], win_ref[j]), j, width)
    wait_all(stores)


def expert_step(kernel, name, blocks, extra, in_place, first, second, hidden):
    count = len(blocks)
    each, width = first.shape[0], first.shape[1] * first.shape[2] // hidden
    rows = count * blocks[0].shape[0]
    kept = jax.ShapeDtypeStruct((rows, each * hidden), BF16)
    outs = local_kernel(
        functools.partial(kernel, count, each),
        [jax.ShapeDtypeStruct(b.shape, BF16) for b in blocks]
        + [jax.ShapeDtypeStruct((rows, each * hidden), F32)] * in_place
        + [pltpu.HBM((rows, each * width), BF16), pltpu.HBM(kept.shape, BF16)],
        [
            pltpu.VMEM(second.shape, BF16),
            pltpu.VMEM(kept.shape, BF16),
            pltpu.SemaphoreType.DMA((each, PIECES)),
            pltpu.SemaphoreType.DMA((count,)),
            pltpu.SemaphoreType.DMA((1,)),
        ],
        4 * rows * each * width * hidden,
        4 * each * width * hidden + 4 * rows * each * width,
        name,
        in_specs=[in_vmem_spec] * (count + len(extra) + 1) + [in_hbm_spec],
        out_specs=[in_vmem_spec] * (count + in_place) + [in_hbm_spec] * 2,
    )(*blocks, *extra, first, in_hbm(second))
    return outs[:count], *outs[count:]


def weights_kernel(ins_ref, cots_ref, act_ref, pre_ref, gin_ref, gout_ref):
    gin_ref[0] = tn(ins_ref[...], pre_ref[...]).astype(BF16)
    gout_ref[0] = tn(act_ref[...], cots_ref[...]).astype(BF16)


def weight_gradients(ins, cots, act, pre, each):
    cuts = 2
    rows = ins.shape[0]
    width, hidden = ins.shape[1] // each, act.shape[1] // each
    return local_kernel(
        weights_kernel,
        (
            jax.ShapeDtypeStruct((each, width, hidden), BF16),
            jax.ShapeDtypeStruct((each, hidden, width), BF16),
        ),
        [],
        4 * rows * each * width * hidden,
        4 * each * width * hidden + 8 * rows * each * width,
        "weight_grads",
        grid=(each, cuts),
        in_specs=[
            pl.BlockSpec((rows, width // cuts), lambda e, i: (0, e * cuts + i)),
            pl.BlockSpec((rows, width), lambda e, i: (0, e)),
            pl.BlockSpec((rows, hidden // cuts), lambda e, i: (0, e * cuts + i)),
            pl.BlockSpec((rows, hidden), lambda e, i: (0, e)),
        ],
        out_specs=(
            pl.BlockSpec((1, width // cuts, hidden), lambda e, i: (e, i, 0)),
            pl.BlockSpec((1, hidden // cuts, width), lambda e, i: (e, i, 0)),
        ),
    )(in_hbm(ins), in_hbm(cots), in_hbm(act), in_hbm(pre))


def crossed_send(value, step, turn):
    pairs = []
    for z in range(ZL):
        for x in range(X):
            for y in range(Y):
                for h in range(ZH):
                    for c in range(CORE):
                        along_x = (c + turn) % 2 == 0
                        tx = (x + step) % X if along_x else x
                        ty = y if along_x else (y + step) % Y
                        here = ((z * X + x) * Y + y) * ZH + h
                        there = ((z * X + tx) * Y + ty) * ZH + h
                        pairs.append((here * CORE + c, there * CORE + c))
    return lax.ppermute(value, ("batch", "expert"), pairs)


def depth_swap(value, step):
    depth = ZL * ZH
    pairs = []
    for z in range(depth):
        to = (z + (step if z % 2 else -step)) % depth
        for x in range(X):
            for y in range(Y):
                for c in range(CORE):
                    here, there = (
                        ((k % ZL * X + x) * Y + y) * ZH * CORE + k // ZL * CORE + c for k in (z, to)
                    )
                    pairs.append((here, there))
    return lax.ppermute(value, ("batch", "expert"), pairs)


def sum_all(partial, beside):
    core = lax.axis_index("expert") % CORE
    half = partial.shape[0] // CORE
    keep = lax.dynamic_slice_in_dim(partial, core * half, half)
    give = lax.dynamic_slice_in_dim(partial, (1 - core) * half, half)
    total = add(keep, expert_send(give, 0, 0, 1))
    total = add(total, *[crossed_send(total, k, 0) for k in range(1, X)])
    total = add(total, *[crossed_send(total, k, 1) for k in range(1, X)])
    total = add(total, batch_send(total, 1, 0))
    total, beside = together(total, beside)
    total = add(total, depth_swap(total, 1))
    total = add(total, depth_swap(total, -3))
    other = expert_send(total, 0, 0, 1)
    first = jnp.where(core == 0, total, other)
    second = jnp.where(core == 0, other, total)
    return jnp.concatenate([first, second], axis=0).astype(F32), beside


def body(tokens, slot_params, weight_in, weight_out, output_grad):
    tokens, output_grad = tokens[0], output_grad[0]
    patches, width = tokens.shape
    slots = slot_params.shape[1]
    groups = lax.axis_size("expert")
    each = slots // groups
    tiles = width // LANES
    flat = groups * 2 * each * tiles
    params = slot_params.T
    flat_shape = jax.ShapeDtypeStruct((flat, LANES), BF16)
    square = pltpu.HBM((slots, patches), F32)
    dot_flops = 2 * slots * patches * width
    rows, dispatch, combine = local_kernel(
        functools.partial(front_kernel, each),
        (flat_shape, square, square),
        [
            pltpu.VMEM((tiles, slots, LANES), F32),
            pltpu.VMEM((flat, LANES), F32),
            pltpu.VMEM((patches, width), BF16),
            pltpu.VMEM((patches, width), BF16),
            pltpu.VMEM((slots, width), BF16),
            pltpu.VMEM((slots, patches), F32),
            pltpu.VMEM((slots, patches), F32),
            pltpu.SemaphoreType.DMA((3, PIECES)),
            pltpu.SemaphoreType.DMA((2,)),
        ],
        3 * dot_flops,
        4 * patches * width + 2 * flat * LANES,
        "front",
        in_specs=[in_hbm_spec] * 3,
        out_specs=(in_vmem_spec, in_hbm_spec, in_hbm_spec),
    )(in_hbm(tokens), in_hbm(output_grad), in_hbm(params))
    routed = lax.all_to_all(
        rows.reshape(groups, 2 * each * tiles, LANES), "expert", split_axis=0, concat_axis=0,
        tiled=True,
    ).reshape(flat, LANES)
    half_shape = jax.ShapeDtypeStruct((groups, each * width), BF16)
    ins, cots = local_kernel(
        unpack_kernel,
        (half_shape, half_shape),
        [pltpu.VMEM((flat, LANES), F32)],
        0,
        4 * flat * LANES,
        "unpack",
    )(routed)
    hidden = weight_in.shape[2]
    near_a = gather_near(ins)
    near_b = gather_near(cots)
    near_a = together(*near_a)
    next_a = gather_next(near_a)
    near_b = together(*near_b)
    next_b = gather_next(near_b)
    next_a = together(*next_a)
    far_a = gather_far(next_a, 0)
    next_b = together(*next_b)
    far_b = gather_far(next_b, 1)
    blocks_a = by_offset(ins, near_a, next_a, far_a)
    blocks_b = by_offset(cots, near_b, next_b, far_b)
    parts_a, slope, rows_a, act = expert_step(
        forward_kernel, "expert_forward", blocks_a, [], 1, weight_in, weight_out, hidden
    )
    first_a = scatter_first(parts_a)
    parts_b, rows_b, pre = expert_step(
        backward_kernel, "expert_backward", blocks_b, [slope], 0, weight_out, weight_in, hidden
    )
    first_b = scatter_first(parts_b)
    first_a, parts_a, pre = together(first_a, parts_a, pre)
    second_a = scatter_second(parts_a, first_a, 0)
    first_b, parts_b = together(first_b, parts_b)
    second_b = scatter_second(parts_b, first_b, 1)
    second_a = together(*second_a)
    third_a = scatter_third(parts_a, second_a[0], 0)
    second_b = together(*second_b)
    third_b = scatter_third(parts_b, second_b[0], 1)
    share = (parts_a[0], *second_a[1:], third_a, parts_b[0], *second_b[1:], third_b)
    packed = local_kernel(
        pack_sum_kernel,
        flat_shape,
        [pltpu.VMEM((flat, LANES), F32)],
        0,
        10 * flat * LANES,
        "pack_sum",
    )(*share)
    packed, act, pre = together(packed, act, pre)
    back = lax.all_to_all(
        packed.reshape(groups, 2 * each * tiles, LANES), "expert", split_axis=0, concat_axis=0,
        tiled=True,
    ).reshape(flat, LANES)
    weight_grads = weight_gradients(rows_a, rows_b, act, pre, each)
    back, weight_grads = lax.optimization_barrier((back, weight_grads))
    row_shape = jax.ShapeDtypeStruct((slots, width), BF16)
    slot_in_grad, logits_grad, local_params = local_kernel(
        functools.partial(final_kernel, each),
        (row_shape, jax.ShapeDtypeStruct((slots, patches), BF16), row_shape),
        [
            pltpu.VMEM((flat, LANES), F32),
            pltpu.VMEM((tiles, slots, LANES), F32),
            pltpu.VMEM((tiles, slots, LANES), F32),
            pltpu.VMEM((slots, patches), F32),
            pltpu.VMEM((slots, patches), F32),
            pltpu.SemaphoreType.DMA((2,)),
        ],
        3 * dot_flops,
        4 * patches * width + 2 * flat * LANES,
        "final",
        in_specs=[in_vmem_spec] * 3 + [in_hbm_spec] * 2,
    )(back, tokens, output_grad, in_hbm(dispatch), in_hbm(combine))
    tokens_grad = (
        jnp.einsum("sm,sd->md", dispatch.astype(BF16), slot_in_grad, preferred_element_type=F32)
        + jnp.einsum("sm,sd->md", logits_grad, params, preferred_element_type=F32)
    ).astype(BF16)
    total_images = lax.axis_size("batch") * groups
    params_sum, tokens_grad = sum_all(local_params, tokens_grad)
    params_grad = (params_sum / total_images).T
    return (tokens_grad[None], params_grad, *weight_grads)


def solution(mesh):
    in_specs = (
        P(("batch", "expert"), None, None),
        P(),
        P("expert", None, "batch"),
        P("expert", "batch", None),
        P(("batch", "expert"), None, None),
    )
    out_specs = (
        P(("batch", "expert"), None, None),
        P(),
        P("expert", None, "batch"),
        P("expert", "batch", None),
    )
    return jax.shard_map(body, mesh=mesh, in_specs=in_specs, out_specs=out_specs, check_vma=False)
```

```python
import functools
import math

import jax
import jax.numpy as jnp
from jax import lax
from jax.experimental import pallas as pl
from jax.experimental.pallas import tpu as pltpu
from jax.sharding import PartitionSpec as P

GELU_CUBIC = 0.044715
GELU_ROOT = math.sqrt(2.0 / math.pi)
BF16 = jnp.bfloat16
F32 = jnp.float32

X, ZL, Y, ZH, CORE = 4, 2, 4, 4, 2


def gelu_pair(pre_act):
    tanh_arg = GELU_ROOT * (pre_act + GELU_CUBIC * pre_act * pre_act * pre_act)
    tanh_value = jnp.tanh(tanh_arg)
    gelu_value = 0.5 * pre_act * (1.0 + tanh_value)
    gelu_slope = 0.5 * (1.0 + tanh_value) + 0.5 * pre_act * (
        1.0 - tanh_value * tanh_value
    ) * GELU_ROOT * (1.0 + 3.0 * GELU_CUBIC * pre_act * pre_act)
    return (gelu_value, gelu_slope)


def batch_send(value, dz, dx):
    pairs = [
        (z * X + x, ((z + dz) % ZL) * X + (x + dx) % X) for z in range(ZL) for x in range(X)
    ]
    return lax.ppermute(value, "batch", pairs)


def batch_fetch(value, dz, dx):
    return batch_send(value, -dz, -dx)


def expert_send(value, dy, dh, dc):
    pairs = []
    for y in range(Y):
        for h in range(ZH):
            for c in range(CORE):
                to = (((y + dy) % Y) * ZH + (h + dh) % ZH) * CORE + (c + dc) % CORE
                pairs.append(((y * ZH + h) * CORE + c, to))
    return lax.ppermute(value, "expert", pairs)


def add(*terms):
    total = terms[0].astype(F32)
    for term in terms[1:]:
        total = total + term.astype(F32)
    return total.astype(BF16)


def together(*values):
    return lax.optimization_barrier(values)


def gather_near(mine):
    return batch_fetch(mine, 0, 1), batch_fetch(mine, 0, 3), batch_fetch(mine, 1, 0)


def gather_next(near):
    b01, b03, b10 = near
    return batch_fetch(b01, 0, 1), batch_fetch(b10, 0, 3), batch_fetch(b01, 1, 0)


def gather_far(nexts, side):
    b02, b13, b11 = nexts
    return batch_fetch(b11, 0, 1) if side == 0 else batch_fetch(b13, 0, 3)


def by_offset(mine, near, nexts, far):
    return [mine, near[0], nexts[0], near[1], near[2], nexts[2], far, nexts[1]]


def scatter_first(parts):
    p00, p01, p02, p03, p10, p11, p12, p13 = parts
    return batch_send(p11, 0, 1), batch_send(p13, 0, 3), batch_send(p12, 1, 0)


def scatter_second(parts, got, side):
    p00, p01, p02, p03, p10, p11, p12, p13 = parts
    p10 = add(p10, got[0], got[1])
    p02 = add(p02, got[2])
    if side == 0:
        return batch_send(p02, 0, 1), batch_send(p03, 0, 3), batch_send(p10, 1, 0)
    return batch_send(p02, 0, 3), batch_send(p01, 0, 1), batch_send(p10, 1, 0)


def scatter_third(parts, got, side):
    if side == 0:
        return batch_send(add(parts[1], got), 0, 1)
    return batch_send(add(parts[3], got), 0, 3)


LANES = 128


PIECES = 4


def start_loads(source, target, sems):
    rows = source.shape[0] // PIECES
    copies = []
    for i in range(PIECES):
        part = pl.ds(i * rows, rows)
        copies.append(pltpu.make_async_copy(source.at[part], target.at[part], sems.at[i]))
        copies[-1].start()
    return copies


def wait_all(copies):
    for copy in copies:
        copy.wait()


in_vmem_spec = pl.BlockSpec(memory_space=pltpu.VMEM)
in_hbm_spec = pl.BlockSpec(memory_space=pltpu.HBM)


def in_hbm(value):
    return pltpu.with_memory_space_constraint(value, pltpu.HBM)


def local_kernel(kernel, outs, scratch, flops, moved, name, vmem=16, **specs):
    return pl.pallas_call(
        kernel,
        out_shape=outs,
        **specs,
        scratch_shapes=scratch,
        compiler_params=pltpu.CompilerParams(vmem_limit_bytes=vmem * 1024 * 1024),
        cost_estimate=pl.CostEstimate(flops=flops, bytes_accessed=moved, transcendentals=0),
        name=name,
    )


def nt(a, b):
    return lax.dot_general(a, b, (((1,), (1,)), ((), ())), preferred_element_type=F32)


PIECES = 4


def tn(a, b):
    return lax.dot_general(a, b, (((0,), (0,)), ((), ())), preferred_element_type=F32)


def front_kernel(
    each, tok_hbm, cot_hbm, par_hbm, rows_ref, disp_ref, comb_ref,
    slots_ref, flat_ref, tok_ref, cot_ref, par_ref, sems,
):
    par_loads = start_loads(par_hbm, par_ref, sems.at[0])
    tok_loads = start_loads(tok_hbm, tok_ref, sems.at[1])
    cot_loads = start_loads(cot_hbm, cot_ref, sems.at[2])
    wait_all(par_loads + tok_loads)
    tiles = slots_ref.shape[0]
    groups = slots_ref.shape[1] // each
    stride = 2 * each * tiles
    logits = nt(par_ref[...], tok_ref[...])
    raised = jnp.exp(logits - jnp.max(logits, axis=1, keepdims=True))
    dispatch = raised / jnp.sum(raised, axis=1, keepdims=True)
    raised = jnp.exp(logits - jnp.max(logits, axis=0, keepdims=True))
    combine = raised / jnp.sum(raised, axis=0, keepdims=True)
    disp_ref[...] = dispatch
    comb_ref[...] = combine
    for kind, (weights, values) in enumerate(((dispatch, tok_ref), (combine, cot_ref))):
        if kind == 1:
            wait_all(cot_loads)
        mixed = jnp.dot(weights.astype(BF16), values[...], preferred_element_type=F32)
        for k in range(tiles):
            slots_ref[k] = mixed[:, k * LANES : (k + 1) * LANES]
            for j in range(each):
                row = (kind * each + j) * tiles + k
                flat_ref[pl.ds(row, groups, stride=stride), :] = slots_ref[
                    k, pl.ds(j, groups, stride=each), :
                ]
    rows_ref[...] = flat_ref[...].astype(BF16)


def unpack_kernel(flat_in_ref, ins_ref, cots_ref, flat_ref):
    groups = ins_ref.shape[0]
    tiles = ins_ref.shape[1] // LANES
    flat_ref[...] = flat_in_ref[...].astype(F32)
    for kind, out_ref in enumerate((ins_ref, cots_ref)):
        for c in range(tiles):
            out_ref[:, c * LANES : (c + 1) * LANES] = flat_ref[
                pl.ds(kind * tiles + c, groups, stride=2 * tiles), :
            ].astype(BF16)


def pack_sum_kernel(*refs):
    out_ref, flat_ref = refs[-2:]
    groups = refs[0].shape[0]
    tiles = refs[0].shape[1] // LANES
    for kind in range(2):
        terms = refs[4 * kind : 4 * kind + 4]
        for c in range(tiles):
            cols = slice(c * LANES, (c + 1) * LANES)
            total = terms[0][:, cols].astype(F32)
            for term in terms[1:]:
                total = total + term[:, cols].astype(F32)
            flat_ref[pl.ds(kind * tiles + c, groups, stride=2 * tiles), :] = total
    out_ref[...] = flat_ref[...].astype(BF16)


def final_kernel(
    each, flat_in_ref, tok_ref, cot_ref, disp_ref, comb_ref, sig_ref, grad_ref, par_ref,
    flat_ref, out_f_ref, sig_f_ref,
):
    groups = sig_ref.shape[0] // each
    tiles = sig_ref.shape[1] // LANES
    stride = 2 * each * tiles
    flat_ref[...] = flat_in_ref[...].astype(F32)
    for kind, ref in enumerate((out_f_ref, sig_f_ref)):
        for j in range(each):
            for k in range(tiles):
                row = (kind * each + j) * tiles + k
                ref[k, pl.ds(j, groups, stride=each), :] = flat_ref[
                    pl.ds(row, groups, stride=stride), :
                ]
    slot_out = jnp.concatenate([out_f_ref[k].astype(BF16) for k in range(tiles)], axis=1)
    sig = jnp.concatenate([sig_f_ref[k].astype(BF16) for k in range(tiles)], axis=1)
    sig_ref[...] = sig
    combine_grad = nt(slot_out, cot_ref[...])
    dispatch_grad = nt(sig, tok_ref[...])
    combine = comb_ref[...]
    dispatch = disp_ref[...]
    combine_part = combine * (combine_grad - jnp.sum(combine * combine_grad, axis=0, keepdims=True))
    dispatch_part = dispatch * (
        dispatch_grad - jnp.sum(dispatch * dispatch_grad, axis=1, keepdims=True)
    )
    logits_grad = (combine_part + dispatch_part).astype(BF16)
    grad_ref[...] = logits_grad
    par_ref[...] = jnp.dot(logits_grad, tok_ref[...], preferred_element_type=F32).astype(BF16)


def gathered(blocks, j, width):
    return jnp.concatenate([b[:, j * width : (j + 1) * width] for b in blocks], axis=0)


def spread(parts, value, j, width):
    value = value.astype(BF16)
    groups = parts[0].shape[0]
    for i, part in enumerate(parts):
        part[:, j * width : (j + 1) * width] = value[i * groups : (i + 1) * groups]


def start_stores(sources, target, sems):
    rows = sources[0].shape[0]
    copies = []
    for i, source in enumerate(sources):
        part = target.at[pl.ds(i * rows, rows)]
        copies.append(pltpu.make_async_copy(source, part, sems.at[i]))
        copies[-1].start()
    return copies


def forward_kernel(count, each, *refs):
    blocks, (win_hbm, wout_hbm) = refs[:count], refs[count : count + 2]
    parts, (slope_ref, rows_hbm, act_hbm) = refs[count + 2 : 2 * count + 2], refs[-10:-7]
    win_ref, wout_ref, act_ref, sems, row_sems, kept_sems, win_sems = refs[-7:]
    width, hidden = win_ref.shape[1:]
    win_loads = [start_loads(win_hbm.at[j], win_ref.at[j], win_sems.at[j]) for j in range(each)]
    wout_loads = [start_loads(wout_hbm.at[j], wout_ref.at[j], sems.at[j]) for j in range(each)]
    stores = start_stores(blocks, rows_hbm, row_sems)
    for j in range(each):
        hid = slice(j * hidden, (j + 1) * hidden)
        wait_all(win_loads[j])
        pre_act = jnp.dot(gathered(blocks, j, width), win_ref[j], preferred_element_type=F32)
        gelu_value, slope_ref[:, hid] = gelu_pair(pre_act)
        act_ref[:, hid] = gelu_value.astype(BF16)
    stores += start_stores([act_ref], act_hbm, kept_sems)
    for j in range(each):
        hid = slice(j * hidden, (j + 1) * hidden)
        wait_all(wout_loads[j])
        spread(parts, jnp.dot(act_ref[:, hid], wout_ref[j], preferred_element_type=F32), j, width)
    wait_all(stores)


def backward_kernel(count, each, *refs):
    blocks, (slope_ref, wout_ref, win_hbm) = refs[:count], refs[count : count + 3]
    parts, (rows_hbm, pre_hbm) = refs[count + 3 : 2 * count + 3], refs[-7:-5]
    win_ref, pre_ref, sems, row_sems, kept_sems = refs[-5:]
    width, hidden = win_ref.shape[1:]
    win_loads = [start_loads(win_hbm.at[j], win_ref.at[j], sems.at[j]) for j in range(each)]
    stores = start_stores(blocks, rows_hbm, row_sems)
    for j in range(each):
        hid = slice(j * hidden, (j + 1) * hidden)
        act_grad = nt(gathered(blocks, j, width), wout_ref[j])
        pre_ref[:, hid] = (act_grad * slope_ref[:, hid]).astype(BF16)
    stores += start_stores([pre_ref], pre_hbm, kept_sems)
    for j in range(each):
        hid = slice(j * hidden, (j + 1) * hidden)
        wait_all(win_loads[j])
        spread(parts, nt(pre_ref[:, hid], win_ref[j]), j, width)
    wait_all(stores)


def expert_step(kernel, name, blocks, extra, in_place, first, second, hidden, load_first):
    count = len(blocks)
    each, width = first.shape[0], first.shape[1] * first.shape[2] // hidden
    rows = count * blocks[0].shape[0]
    kept = jax.ShapeDtypeStruct((rows, each * hidden), BF16)
    outs = local_kernel(
        functools.partial(kernel, count, each),
        [jax.ShapeDtypeStruct(b.shape, BF16) for b in blocks]
        + [jax.ShapeDtypeStruct((rows, each * hidden), F32)] * in_place
        + [pltpu.HBM((rows, each * width), BF16), pltpu.HBM(kept.shape, BF16)],
        [pltpu.VMEM(first.shape, BF16)] * load_first
        + [
            pltpu.VMEM(second.shape, BF16),
            pltpu.VMEM(kept.shape, BF16),
            pltpu.SemaphoreType.DMA((each, PIECES)),
            pltpu.SemaphoreType.DMA((count,)),
            pltpu.SemaphoreType.DMA((1,)),
        ]
        + [pltpu.SemaphoreType.DMA((each, PIECES))] * load_first,
        4 * rows * each * width * hidden,
        4 * each * width * hidden + 4 * rows * each * width,
        name,
        in_specs=[in_vmem_spec] * (count + len(extra) + 1 - load_first)
        + [in_hbm_spec] * (1 + load_first),
        out_specs=[in_vmem_spec] * (count + in_place) + [in_hbm_spec] * 2,
    )(*blocks, *extra, in_hbm(first) if load_first else first, in_hbm(second))
    return outs[:count], *outs[count:]


def weights_kernel(ins_ref, cots_ref, act_ref, pre_ref, gin_ref, gout_ref):
    gin_ref[0] = tn(ins_ref[...], pre_ref[...]).astype(BF16)
    gout_ref[0] = tn(act_ref[...], cots_ref[...]).astype(BF16)


def weight_gradients(ins, cots, act, pre, each):
    cuts = 2
    rows = ins.shape[0]
    width, hidden = ins.shape[1] // each, act.shape[1] // each
    return local_kernel(
        weights_kernel,
        (
            jax.ShapeDtypeStruct((each, width, hidden), BF16),
            jax.ShapeDtypeStruct((each, hidden, width), BF16),
        ),
        [],
        4 * rows * each * width * hidden,
        4 * each * width * hidden + 8 * rows * each * width,
        "weight_grads",
        grid=(each, cuts),
        in_specs=[
            pl.BlockSpec((rows, width // cuts), lambda e, i: (0, e * cuts + i)),
            pl.BlockSpec((rows, width), lambda e, i: (0, e)),
            pl.BlockSpec((rows, hidden // cuts), lambda e, i: (0, e * cuts + i)),
            pl.BlockSpec((rows, hidden), lambda e, i: (0, e)),
        ],
        out_specs=(
            pl.BlockSpec((1, width // cuts, hidden), lambda e, i: (e, i, 0)),
            pl.BlockSpec((1, hidden // cuts, width), lambda e, i: (e, i, 0)),
        ),
    )(in_hbm(ins), in_hbm(cots), in_hbm(act), in_hbm(pre))


def crossed_send(value, step, turn):
    pairs = []
    for z in range(ZL):
        for x in range(X):
            for y in range(Y):
                for h in range(ZH):
                    for c in range(CORE):
                        along_x = (c + turn) % 2 == 0
                        tx = (x + step) % X if along_x else x
                        ty = y if along_x else (y + step) % Y
                        here = ((z * X + x) * Y + y) * ZH + h
                        there = ((z * X + tx) * Y + ty) * ZH + h
                        pairs.append((here * CORE + c, there * CORE + c))
    return lax.ppermute(value, ("batch", "expert"), pairs)


def depth_swap(value, step):
    depth = ZL * ZH
    pairs = []
    for z in range(depth):
        to = (z + (step if z % 2 else -step)) % depth
        for x in range(X):
            for y in range(Y):
                for c in range(CORE):
                    here, there = (
                        ((k % ZL * X + x) * Y + y) * ZH * CORE + k // ZL * CORE + c for k in (z, to)
                    )
                    pairs.append((here, there))
    return lax.ppermute(value, ("batch", "expert"), pairs)


def sum_all(partial, beside):
    core = lax.axis_index("expert") % CORE
    half = partial.shape[0] // CORE
    keep = lax.dynamic_slice_in_dim(partial, core * half, half)
    give = lax.dynamic_slice_in_dim(partial, (1 - core) * half, half)
    total = add(keep, expert_send(give, 0, 0, 1))
    total = add(total, *[crossed_send(total, k, 0) for k in range(1, X)])
    total = add(total, *[crossed_send(total, k, 1) for k in range(1, X)])
    total = add(total, batch_send(total, 1, 0))
    total, beside = together(total, beside)
    total = add(total, depth_swap(total, 1))
    total = add(total, depth_swap(total, -3))
    other = expert_send(total, 0, 0, 1)
    first = jnp.where(core == 0, total, other)
    second = jnp.where(core == 0, other, total)
    return jnp.concatenate([first, second], axis=0).astype(F32), beside


def body(tokens, slot_params, weight_in, weight_out, output_grad):
    tokens, output_grad = tokens[0], output_grad[0]
    patches, width = tokens.shape
    slots = slot_params.shape[1]
    groups = lax.axis_size("expert")
    each = slots // groups
    tiles = width // LANES
    flat = groups * 2 * each * tiles
    params = slot_params.T
    flat_shape = jax.ShapeDtypeStruct((flat, LANES), BF16)
    square = pltpu.VMEM((slots, patches), F32)
    dot_flops = 2 * slots * patches * width
    rows, dispatch, combine = local_kernel(
        functools.partial(front_kernel, each),
        (flat_shape, square, square),
        [
            pltpu.VMEM((tiles, slots, LANES), F32),
            pltpu.VMEM((flat, LANES), F32),
            pltpu.VMEM((patches, width), BF16),
            pltpu.VMEM((patches, width), BF16),
            pltpu.VMEM((slots, width), BF16),
            pltpu.SemaphoreType.DMA((3, PIECES)),
        ],
        3 * dot_flops,
        4 * patches * width + 2 * flat * LANES,
        "front",
        in_specs=[in_hbm_spec] * 3,
        out_specs=(in_vmem_spec,) * 3,
    )(in_hbm(tokens), in_hbm(output_grad), in_hbm(params))
    routed = lax.all_to_all(
        rows.reshape(groups, 2 * each * tiles, LANES), "expert", split_axis=0, concat_axis=0,
        tiled=True,
    ).reshape(flat, LANES)
    half_shape = jax.ShapeDtypeStruct((groups, each * width), BF16)
    ins, cots = local_kernel(
        unpack_kernel,
        (half_shape, half_shape),
        [pltpu.VMEM((flat, LANES), F32)],
        0,
        4 * flat * LANES,
        "unpack",
    )(routed)
    hidden = weight_in.shape[2]
    near_a = gather_near(ins)
    near_b = gather_near(cots)
    near_a = together(*near_a)
    next_a = gather_next(near_a)
    next_a, near_b = together(next_a, near_b)
    far_a = gather_far(next_a, 0)
    next_b = gather_next(near_b)
    blocks_a = by_offset(ins, near_a, next_a, far_a)
    parts_a, slope, rows_a, act = expert_step(
        forward_kernel, "expert_forward", blocks_a, [], 1, weight_in, weight_out, hidden, 1
    )
    next_b, parts_a = together(next_b, parts_a)
    far_b = gather_far(next_b, 1)
    blocks_b = by_offset(cots, near_b, next_b, far_b)
    first_a = scatter_first(parts_a)
    parts_b, rows_b, pre = expert_step(
        backward_kernel, "expert_backward", blocks_b, [slope], 0, weight_out, weight_in, hidden, 0
    )
    first_b = scatter_first(parts_b)
    first_a, parts_a, pre = together(first_a, parts_a, pre)
    second_a = scatter_second(parts_a, first_a, 0)
    first_b, parts_b = together(first_b, parts_b)
    second_b = scatter_second(parts_b, first_b, 1)
    second_a = together(*second_a)
    third_a = scatter_third(parts_a, second_a[0], 0)
    second_b = together(*second_b)
    third_b = scatter_third(parts_b, second_b[0], 1)
    share = (parts_a[0], *second_a[1:], third_a, parts_b[0], *second_b[1:], third_b)
    packed = local_kernel(
        pack_sum_kernel,
        flat_shape,
        [pltpu.VMEM((flat, LANES), F32)],
        0,
        10 * flat * LANES,
        "pack_sum",
    )(*share)
    packed, act, pre = together(packed, act, pre)
    back = lax.all_to_all(
        packed.reshape(groups, 2 * each * tiles, LANES), "expert", split_axis=0, concat_axis=0,
        tiled=True,
    ).reshape(flat, LANES)
    weight_grads = weight_gradients(rows_a, rows_b, act, pre, each)
    back, weight_grads = lax.optimization_barrier((back, weight_grads))
    row_shape = jax.ShapeDtypeStruct((slots, width), BF16)
    slot_in_grad, logits_grad, local_params = local_kernel(
        functools.partial(final_kernel, each),
        (row_shape, jax.ShapeDtypeStruct((slots, patches), BF16), row_shape),
        [
            pltpu.VMEM((flat, LANES), F32),
            pltpu.VMEM((tiles, slots, LANES), F32),
            pltpu.VMEM((tiles, slots, LANES), F32),
        ],
        3 * dot_flops,
        4 * patches * width + 2 * flat * LANES,
        "final",
    )(back, tokens, output_grad, dispatch, combine)
    tokens_grad = (
        jnp.einsum("sm,sd->md", dispatch.astype(BF16), slot_in_grad, preferred_element_type=F32)
        + jnp.einsum("sm,sd->md", logits_grad, params, preferred_element_type=F32)
    ).astype(BF16)
    total_images = lax.axis_size("batch") * groups
    params_sum, tokens_grad = sum_all(local_params, tokens_grad)
    params_grad = (params_sum / total_images).T
    return (tokens_grad[None], params_grad, *weight_grads)


def solution(mesh):
    in_specs = (
        P(("batch", "expert"), None, None),
        P(),
        P("expert", None, "batch"),
        P("expert", "batch", None),
        P(("batch", "expert"), None, None),
    )
    out_specs = (
        P(("batch", "expert"), None, None),
        P(),
        P("expert", None, "batch"),
        P("expert", "batch", None),
    )
    return jax.shard_map(body, mesh=mesh, in_specs=in_specs, out_specs=out_specs, check_vma=False)
```

```python
import functools
import math

import jax
import jax.numpy as jnp
from jax import lax
from jax.experimental import pallas as pl
from jax.experimental.pallas import tpu as pltpu
from jax.sharding import PartitionSpec as P

GELU_CUBIC = 0.044715
GELU_ROOT = math.sqrt(2.0 / math.pi)
BF16 = jnp.bfloat16
F32 = jnp.float32

X, ZL, Y, ZH, CORE = 4, 2, 4, 4, 2


def gelu_pair(pre_act):
    tanh_arg = GELU_ROOT * (pre_act + GELU_CUBIC * pre_act * pre_act * pre_act)
    tanh_value = jnp.tanh(tanh_arg)
    gelu_value = 0.5 * pre_act * (1.0 + tanh_value)
    gelu_slope = 0.5 * (1.0 + tanh_value) + 0.5 * pre_act * (
        1.0 - tanh_value * tanh_value
    ) * GELU_ROOT * (1.0 + 3.0 * GELU_CUBIC * pre_act * pre_act)
    return (gelu_value, gelu_slope)


def batch_send(value, dz, dx):
    pairs = [
        (z * X + x, ((z + dz) % ZL) * X + (x + dx) % X) for z in range(ZL) for x in range(X)
    ]
    return lax.ppermute(value, "batch", pairs)


def batch_fetch(value, dz, dx):
    return batch_send(value, -dz, -dx)


def expert_send(value, dy, dh, dc):
    pairs = []
    for y in range(Y):
        for h in range(ZH):
            for c in range(CORE):
                to = (((y + dy) % Y) * ZH + (h + dh) % ZH) * CORE + (c + dc) % CORE
                pairs.append(((y * ZH + h) * CORE + c, to))
    return lax.ppermute(value, "expert", pairs)


def add(*terms):
    total = terms[0].astype(F32)
    for term in terms[1:]:
        total = total + term.astype(F32)
    return total.astype(BF16)


def together(*values):
    return lax.optimization_barrier(values)


def gather_near(mine):
    return batch_fetch(mine, 0, 1), batch_fetch(mine, 0, 3), batch_fetch(mine, 1, 0)


def gather_next(near):
    b01, b03, b10 = near
    return batch_fetch(b01, 0, 1), batch_fetch(b10, 0, 3), batch_fetch(b01, 1, 0)


def gather_far(nexts, side):
    b02, b13, b11 = nexts
    return batch_fetch(b11, 0, 1) if side == 0 else batch_fetch(b13, 0, 3)


def by_offset(mine, near, nexts, far):
    return [mine, near[0], nexts[0], near[1], near[2], nexts[2], far, nexts[1]]


def scatter_first(parts):
    p00, p01, p02, p03, p10, p11, p12, p13 = parts
    return batch_send(p11, 0, 1), batch_send(p13, 0, 3), batch_send(p12, 1, 0)


def scatter_second(parts, got, side):
    p00, p01, p02, p03, p10, p11, p12, p13 = parts
    p10 = add(p10, got[0], got[1])
    p02 = add(p02, got[2])
    if side == 0:
        return batch_send(p02, 0, 1), batch_send(p03, 0, 3), batch_send(p10, 1, 0)
    return batch_send(p02, 0, 3), batch_send(p01, 0, 1), batch_send(p10, 1, 0)


def scatter_third(parts, got, side):
    if side == 0:
        return batch_send(add(parts[1], got), 0, 1)
    return batch_send(add(parts[3], got), 0, 3)


LANES = 128


PIECES = 4


def start_loads(source, target, sems):
    rows = source.shape[0] // PIECES
    copies = []
    for i in range(PIECES):
        part = pl.ds(i * rows, rows)
        copies.append(pltpu.make_async_copy(source.at[part], target.at[part], sems.at[i]))
        copies[-1].start()
    return copies


def wait_all(copies):
    for copy in copies:
        copy.wait()


in_vmem_spec = pl.BlockSpec(memory_space=pltpu.VMEM)
in_hbm_spec = pl.BlockSpec(memory_space=pltpu.HBM)


def in_hbm(value):
    return pltpu.with_memory_space_constraint(value, pltpu.HBM)


def local_kernel(kernel, outs, scratch, flops, moved, name, vmem=16, **specs):
    return pl.pallas_call(
        kernel,
        out_shape=outs,
        **specs,
        scratch_shapes=scratch,
        compiler_params=pltpu.CompilerParams(vmem_limit_bytes=vmem * 1024 * 1024),
        cost_estimate=pl.CostEstimate(flops=flops, bytes_accessed=moved, transcendentals=0),
        name=name,
    )


def nt(a, b):
    return lax.dot_general(a, b, (((1,), (1,)), ((), ())), preferred_element_type=F32)


PIECES = 4


def tn(a, b):
    return lax.dot_general(a, b, (((0,), (0,)), ((), ())), preferred_element_type=F32)


def front_kernel(
    each, tok_hbm, cot_hbm, par_hbm, rows_ref, disp_ref, comb_ref,
    slots_ref, flat_ref, tok_ref, cot_ref, par_ref, sems,
):
    par_loads = start_loads(par_hbm, par_ref, sems.at[0])
    tok_loads = start_loads(tok_hbm, tok_ref, sems.at[1])
    cot_loads = start_loads(cot_hbm, cot_ref, sems.at[2])
    wait_all(par_loads + tok_loads)
    tiles = slots_ref.shape[0]
    groups = slots_ref.shape[1] // each
    stride = 2 * each * tiles
    logits = nt(par_ref[...], tok_ref[...])
    raised = jnp.exp(logits - jnp.max(logits, axis=1, keepdims=True))
    dispatch = raised / jnp.sum(raised, axis=1, keepdims=True)
    raised = jnp.exp(logits - jnp.max(logits, axis=0, keepdims=True))
    combine = raised / jnp.sum(raised, axis=0, keepdims=True)
    disp_ref[...] = dispatch
    comb_ref[...] = combine
    for kind, (weights, values) in enumerate(((dispatch, tok_ref), (combine, cot_ref))):
        if kind == 1:
            wait_all(cot_loads)
        mixed = jnp.dot(weights.astype(BF16), values[...], preferred_element_type=F32)
        for k in range(tiles):
            slots_ref[k] = mixed[:, k * LANES : (k + 1) * LANES]
            for j in range(each):
                row = (kind * each + j) * tiles + k
                flat_ref[pl.ds(row, groups, stride=stride), :] = slots_ref[
                    k, pl.ds(j, groups, stride=each), :
                ]
    rows_ref[...] = flat_ref[...].astype(BF16)


def unpack_kernel(flat_in_ref, ins_ref, cots_ref, flat_ref):
    groups = ins_ref.shape[0]
    tiles = ins_ref.shape[1] // LANES
    flat_ref[...] = flat_in_ref[...].astype(F32)
    for kind, out_ref in enumerate((ins_ref, cots_ref)):
        for c in range(tiles):
            out_ref[:, c * LANES : (c + 1) * LANES] = flat_ref[
                pl.ds(kind * tiles + c, groups, stride=2 * tiles), :
            ].astype(BF16)


def pack_sum_kernel(*refs):
    out_ref, flat_ref = refs[-2:]
    groups = refs[0].shape[0]
    tiles = refs[0].shape[1] // LANES
    for kind in range(2):
        terms = refs[4 * kind : 4 * kind + 4]
        for c in range(tiles):
            cols = slice(c * LANES, (c + 1) * LANES)
            total = terms[0][:, cols].astype(F32)
            for term in terms[1:]:
                total = total + term[:, cols].astype(F32)
            flat_ref[pl.ds(kind * tiles + c, groups, stride=2 * tiles), :] = total
    out_ref[...] = flat_ref[...].astype(BF16)


def final_kernel(
    each, flat_in_ref, tok_ref, cot_ref, disp_ref, comb_ref, sig_ref, grad_ref, par_ref,
    flat_ref, out_f_ref, sig_f_ref,
):
    groups = sig_ref.shape[0] // each
    tiles = sig_ref.shape[1] // LANES
    stride = 2 * each * tiles
    flat_ref[...] = flat_in_ref[...].astype(F32)
    for kind, ref in enumerate((out_f_ref, sig_f_ref)):
        for j in range(each):
            for k in range(tiles):
                row = (kind * each + j) * tiles + k
                ref[k, pl.ds(j, groups, stride=each), :] = flat_ref[
                    pl.ds(row, groups, stride=stride), :
                ]
    slot_out = jnp.concatenate([out_f_ref[k].astype(BF16) for k in range(tiles)], axis=1)
    sig = jnp.concatenate([sig_f_ref[k].astype(BF16) for k in range(tiles)], axis=1)
    sig_ref[...] = sig
    combine_grad = nt(slot_out, cot_ref[...])
    dispatch_grad = nt(sig, tok_ref[...])
    combine = comb_ref[...]
    dispatch = disp_ref[...]
    combine_part = combine * (combine_grad - jnp.sum(combine * combine_grad, axis=0, keepdims=True))
    dispatch_part = dispatch * (
        dispatch_grad - jnp.sum(dispatch * dispatch_grad, axis=1, keepdims=True)
    )
    logits_grad = (combine_part + dispatch_part).astype(BF16)
    grad_ref[...] = logits_grad
    par_ref[...] = jnp.dot(logits_grad, tok_ref[...], preferred_element_type=F32).astype(BF16)


def gathered(blocks, j, width):
    return jnp.concatenate([b[:, j * width : (j + 1) * width] for b in blocks], axis=0)


def spread(parts, value, j, width):
    value = value.astype(BF16)
    groups = parts[0].shape[0]
    for i, part in enumerate(parts):
        part[:, j * width : (j + 1) * width] = value[i * groups : (i + 1) * groups]


def start_stores(sources, target, sems):
    rows = sources[0].shape[0]
    copies = []
    for i, source in enumerate(sources):
        part = target.at[pl.ds(i * rows, rows)]
        copies.append(pltpu.make_async_copy(source, part, sems.at[i]))
        copies[-1].start()
    return copies


def forward_kernel(count, each, *refs):
    blocks, (win_hbm, wout_hbm) = refs[:count], refs[count : count + 2]
    parts, (slope_ref, rows_hbm, act_hbm) = refs[count + 2 : 2 * count + 2], refs[-10:-7]
    win_ref, wout_ref, act_ref, sems, row_sems, kept_sems, win_sems = refs[-7:]
    width, hidden = win_ref.shape[1:]
    win_loads = [start_loads(win_hbm.at[j], win_ref.at[j], win_sems.at[j]) for j in range(each)]
    wout_loads = [start_loads(wout_hbm.at[j], wout_ref.at[j], sems.at[j]) for j in range(each)]
    stores = start_stores(blocks, rows_hbm, row_sems)
    for j in range(each):
        hid = slice(j * hidden, (j + 1) * hidden)
        wait_all(win_loads[j])
        pre_act = jnp.dot(gathered(blocks, j, width), win_ref[j], preferred_element_type=F32)
        gelu_value, slope_ref[:, hid] = gelu_pair(pre_act)
        act_ref[:, hid] = gelu_value.astype(BF16)
    stores += start_stores([act_ref], act_hbm, kept_sems)
    for j in range(each):
        hid = slice(j * hidden, (j + 1) * hidden)
        wait_all(wout_loads[j])
        spread(parts, jnp.dot(act_ref[:, hid], wout_ref[j], preferred_element_type=F32), j, width)
    wait_all(stores)


def backward_kernel(count, each, *refs):
    blocks, (slope_ref, wout_ref, win_hbm) = refs[:count], refs[count : count + 3]
    parts, (rows_hbm, pre_hbm) = refs[count + 3 : 2 * count + 3], refs[-7:-5]
    win_ref, pre_ref, sems, row_sems, kept_sems = refs[-5:]
    width, hidden = win_ref.shape[1:]
    win_loads = [start_loads(win_hbm.at[j], win_ref.at[j], sems.at[j]) for j in range(each)]
    stores = start_stores(blocks, rows_hbm, row_sems)
    for j in range(each):
        hid = slice(j * hidden, (j + 1) * hidden)
        act_grad = nt(gathered(blocks, j, width), wout_ref[j])
        pre_ref[:, hid] = (act_grad * slope_ref[:, hid]).astype(BF16)
    stores += start_stores([pre_ref], pre_hbm, kept_sems)
    for j in range(each):
        hid = slice(j * hidden, (j + 1) * hidden)
        wait_all(win_loads[j])
        spread(parts, nt(pre_ref[:, hid], win_ref[j]), j, width)
    wait_all(stores)


def expert_step(kernel, name, blocks, extra, in_place, first, second, hidden, load_first):
    count = len(blocks)
    each, width = first.shape[0], first.shape[1] * first.shape[2] // hidden
    rows = count * blocks[0].shape[0]
    kept = jax.ShapeDtypeStruct((rows, each * hidden), BF16)
    outs = local_kernel(
        functools.partial(kernel, count, each),
        [jax.ShapeDtypeStruct(b.shape, BF16) for b in blocks]
        + [jax.ShapeDtypeStruct((rows, each * hidden), F32)] * in_place
        + [pltpu.HBM((rows, each * width), BF16), pltpu.HBM(kept.shape, BF16)],
        [pltpu.VMEM(first.shape, BF16)] * load_first
        + [
            pltpu.VMEM(second.shape, BF16),
            pltpu.VMEM(kept.shape, BF16),
            pltpu.SemaphoreType.DMA((each, PIECES)),
            pltpu.SemaphoreType.DMA((count,)),
            pltpu.SemaphoreType.DMA((1,)),
        ]
        + [pltpu.SemaphoreType.DMA((each, PIECES))] * load_first,
        4 * rows * each * width * hidden,
        4 * each * width * hidden + 4 * rows * each * width,
        name,
        in_specs=[in_vmem_spec] * (count + len(extra) + 1 - load_first)
        + [in_hbm_spec] * (1 + load_first),
        out_specs=[in_vmem_spec] * (count + in_place) + [in_hbm_spec] * 2,
    )(*blocks, *extra, in_hbm(first) if load_first else first, in_hbm(second))
    return outs[:count], *outs[count:]


def weights_kernel(ins_ref, cots_ref, act_ref, pre_ref, gin_ref, gout_ref):
    gin_ref[0] = tn(ins_ref[...], pre_ref[...]).astype(BF16)
    gout_ref[0] = tn(act_ref[...], cots_ref[...]).astype(BF16)


def weight_gradients(ins, cots, act, pre, each):
    cuts = 2
    rows = ins.shape[0]
    width, hidden = ins.shape[1] // each, act.shape[1] // each
    return local_kernel(
        weights_kernel,
        (
            jax.ShapeDtypeStruct((each, width, hidden), BF16),
            jax.ShapeDtypeStruct((each, hidden, width), BF16),
        ),
        [],
        4 * rows * each * width * hidden,
        4 * each * width * hidden + 8 * rows * each * width,
        "weight_grads",
        grid=(each, cuts),
        in_specs=[
            pl.BlockSpec((rows, width // cuts), lambda e, i: (0, e * cuts + i)),
            pl.BlockSpec((rows, width), lambda e, i: (0, e)),
            pl.BlockSpec((rows, hidden // cuts), lambda e, i: (0, e * cuts + i)),
            pl.BlockSpec((rows, hidden), lambda e, i: (0, e)),
        ],
        out_specs=(
            pl.BlockSpec((1, width // cuts, hidden), lambda e, i: (e, i, 0)),
            pl.BlockSpec((1, hidden // cuts, width), lambda e, i: (e, i, 0)),
        ),
    )(in_hbm(ins), in_hbm(cots), in_hbm(act), in_hbm(pre))


def crossed_send(value, step, turn):
    pairs = []
    for z in range(ZL):
        for x in range(X):
            for y in range(Y):
                for h in range(ZH):
                    for c in range(CORE):
                        along_x = (c + turn) % 2 == 0
                        tx = (x + step) % X if along_x else x
                        ty = y if along_x else (y + step) % Y
                        here = ((z * X + x) * Y + y) * ZH + h
                        there = ((z * X + tx) * Y + ty) * ZH + h
                        pairs.append((here * CORE + c, there * CORE + c))
    return lax.ppermute(value, ("batch", "expert"), pairs)


def depth_swap(value, step):
    depth = ZL * ZH
    pairs = []
    for z in range(depth):
        to = (z + (step if z % 2 else -step)) % depth
        for x in range(X):
            for y in range(Y):
                for c in range(CORE):
                    here, there = (
                        ((k % ZL * X + x) * Y + y) * ZH * CORE + k // ZL * CORE + c for k in (z, to)
                    )
                    pairs.append((here, there))
    return lax.ppermute(value, ("batch", "expert"), pairs)


def sum_all(partial, beside):
    core = lax.axis_index("expert") % CORE
    half = partial.shape[0] // CORE
    keep = lax.dynamic_slice_in_dim(partial, core * half, half)
    give = lax.dynamic_slice_in_dim(partial, (1 - core) * half, half)
    total = add(keep, expert_send(give, 0, 0, 1))
    total = add(total, *[crossed_send(total, k, 0) for k in range(1, X)])
    total = add(total, *[crossed_send(total, k, 1) for k in range(1, X)])
    total = add(total, batch_send(total, 1, 0))
    total, beside = together(total, beside)
    total = add(total, depth_swap(total, 1))
    total = add(total, depth_swap(total, -3))
    other = expert_send(total, 0, 0, 1)
    first = jnp.where(core == 0, total, other)
    second = jnp.where(core == 0, other, total)
    return jnp.concatenate([first, second], axis=0).astype(F32), beside


def body(tokens, slot_params, weight_in, weight_out, output_grad):
    tokens, output_grad = tokens[0], output_grad[0]
    patches, width = tokens.shape
    slots = slot_params.shape[1]
    groups = lax.axis_size("expert")
    each = slots // groups
    tiles = width // LANES
    flat = groups * 2 * each * tiles
    params = slot_params.T
    flat_shape = jax.ShapeDtypeStruct((flat, LANES), BF16)
    square = pltpu.VMEM((slots, patches), F32)
    dot_flops = 2 * slots * patches * width
    rows, dispatch, combine = local_kernel(
        functools.partial(front_kernel, each),
        (flat_shape, square, square),
        [
            pltpu.VMEM((tiles, slots, LANES), F32),
            pltpu.VMEM((flat, LANES), F32),
            pltpu.VMEM((patches, width), BF16),
            pltpu.VMEM((patches, width), BF16),
            pltpu.VMEM((slots, width), BF16),
            pltpu.SemaphoreType.DMA((3, PIECES)),
        ],
        3 * dot_flops,
        4 * patches * width + 2 * flat * LANES,
        "front",
        in_specs=[in_hbm_spec] * 3,
        out_specs=(in_vmem_spec,) * 3,
    )(in_hbm(tokens), in_hbm(output_grad), in_hbm(params))
    routed = lax.all_to_all(
        rows.reshape(groups, 2 * each * tiles, LANES), "expert", split_axis=0, concat_axis=0,
        tiled=True,
    ).reshape(flat, LANES)
    half_shape = jax.ShapeDtypeStruct((groups, each * width), BF16)
    ins, cots = local_kernel(
        unpack_kernel,
        (half_shape, half_shape),
        [pltpu.VMEM((flat, LANES), F32)],
        0,
        4 * flat * LANES,
        "unpack",
    )(routed)
    hidden = weight_in.shape[2]
    near_a = gather_near(ins)
    near_b = gather_near(cots)
    near_a = together(*near_a)
    next_a = gather_next(near_a)
    near_b = together(*near_b)
    next_b = gather_next(near_b)
    next_a = together(*next_a)
    far_a = gather_far(next_a, 0)
    next_b = together(*next_b)
    far_b = gather_far(next_b, 1)
    blocks_a = by_offset(ins, near_a, next_a, far_a)
    blocks_b = by_offset(cots, near_b, next_b, far_b)
    parts_a, slope, rows_a, act = expert_step(
        forward_kernel, "expert_forward", blocks_a, [], 1, weight_in, weight_out, hidden, 1
    )
    first_a = scatter_first(parts_a)
    parts_b, rows_b, pre = expert_step(
        backward_kernel, "expert_backward", blocks_b, [slope], 0, weight_out, weight_in, hidden, 0
    )
    first_b = scatter_first(parts_b)
    first_a, parts_a, pre = together(first_a, parts_a, pre)
    second_a = scatter_second(parts_a, first_a, 0)
    first_b, parts_b = together(first_b, parts_b)
    second_b = scatter_second(parts_b, first_b, 1)
    second_a = together(*second_a)
    third_a = scatter_third(parts_a, second_a[0], 0)
    second_b = together(*second_b)
    third_b = scatter_third(parts_b, second_b[0], 1)
    share = (parts_a[0], *second_a[1:], third_a, parts_b[0], *second_b[1:], third_b)
    packed = local_kernel(
        pack_sum_kernel,
        flat_shape,
        [pltpu.VMEM((flat, LANES), F32)],
        0,
        10 * flat * LANES,
        "pack_sum",
    )(*share)
    packed, act, pre = together(packed, act, pre)
    back = lax.all_to_all(
        packed.reshape(groups, 2 * each * tiles, LANES), "expert", split_axis=0, concat_axis=0,
        tiled=True,
    ).reshape(flat, LANES)
    weight_grads = weight_gradients(rows_a, rows_b, act, pre, each)
    back, weight_grads = lax.optimization_barrier((back, weight_grads))
    row_shape = jax.ShapeDtypeStruct((slots, width), BF16)
    slot_in_grad, logits_grad, local_params = local_kernel(
        functools.partial(final_kernel, each),
        (row_shape, jax.ShapeDtypeStruct((slots, patches), BF16), row_shape),
        [
            pltpu.VMEM((flat, LANES), F32),
            pltpu.VMEM((tiles, slots, LANES), F32),
            pltpu.VMEM((tiles, slots, LANES), F32),
        ],
        3 * dot_flops,
        4 * patches * width + 2 * flat * LANES,
        "final",
    )(back, tokens, output_grad, dispatch, combine)
    tokens_grad = (
        jnp.einsum("sm,sd->md", dispatch.astype(BF16), slot_in_grad, preferred_element_type=F32)
        + jnp.einsum("sm,sd->md", logits_grad, params, preferred_element_type=F32)
    ).astype(BF16)
    total_images = lax.axis_size("batch") * groups
    params_sum, tokens_grad = sum_all(local_params, tokens_grad)
    params_grad = (params_sum / total_images).T
    return (tokens_grad[None], params_grad, *weight_grads)


def solution(mesh):
    in_specs = (
        P(("batch", "expert"), None, None),
        P(),
        P("expert", None, "batch"),
        P("expert", "batch", None),
        P(("batch", "expert"), None, None),
    )
    out_specs = (
        P(("batch", "expert"), None, None),
        P(),
        P("expert", None, "batch"),
        P("expert", "batch", None),
    )
    return jax.shard_map(body, mesh=mesh, in_specs=in_specs, out_specs=out_specs, check_vma=False)
```

```python
import functools
import math

import jax
import jax.numpy as jnp
from jax import lax
from jax.experimental import pallas as pl
from jax.experimental.pallas import tpu as pltpu
from jax.sharding import PartitionSpec as P

GELU_CUBIC = 0.044715
GELU_ROOT = math.sqrt(2.0 / math.pi)
BF16 = jnp.bfloat16
F32 = jnp.float32

X, ZL, Y, ZH, CORE = 4, 2, 4, 4, 2


def gelu_pair(pre_act):
    tanh_arg = GELU_ROOT * (pre_act + GELU_CUBIC * pre_act * pre_act * pre_act)
    tanh_value = jnp.tanh(tanh_arg)
    gelu_value = 0.5 * pre_act * (1.0 + tanh_value)
    gelu_slope = 0.5 * (1.0 + tanh_value) + 0.5 * pre_act * (
        1.0 - tanh_value * tanh_value
    ) * GELU_ROOT * (1.0 + 3.0 * GELU_CUBIC * pre_act * pre_act)
    return (gelu_value, gelu_slope)


def batch_send(value, dz, dx):
    pairs = [
        (z * X + x, ((z + dz) % ZL) * X + (x + dx) % X) for z in range(ZL) for x in range(X)
    ]
    return lax.ppermute(value, "batch", pairs)


def batch_fetch(value, dz, dx):
    return batch_send(value, -dz, -dx)


def expert_send(value, dy, dh, dc):
    pairs = []
    for y in range(Y):
        for h in range(ZH):
            for c in range(CORE):
                to = (((y + dy) % Y) * ZH + (h + dh) % ZH) * CORE + (c + dc) % CORE
                pairs.append(((y * ZH + h) * CORE + c, to))
    return lax.ppermute(value, "expert", pairs)


def add(*terms):
    total = terms[0].astype(F32)
    for term in terms[1:]:
        total = total + term.astype(F32)
    return total.astype(BF16)


def together(*values):
    return lax.optimization_barrier(values)


def gather_near(mine):
    return batch_fetch(mine, 0, 1), batch_fetch(mine, 0, 3), batch_fetch(mine, 1, 0)


def gather_next(near):
    b01, b03, b10 = near
    return batch_fetch(b01, 0, 1), batch_fetch(b10, 0, 3), batch_fetch(b01, 1, 0)


def gather_far(nexts, side):
    b02, b13, b11 = nexts
    return batch_fetch(b11, 0, 1) if side == 0 else batch_fetch(b13, 0, 3)


def by_offset(mine, near, nexts, far):
    return [mine, near[0], nexts[0], near[1], near[2], nexts[2], far, nexts[1]]


def scatter_first(parts):
    p00, p01, p02, p03, p10, p11, p12, p13 = parts
    return batch_send(p11, 0, 1), batch_send(p13, 0, 3), batch_send(p12, 1, 0)


def scatter_second(parts, got, side):
    p00, p01, p02, p03, p10, p11, p12, p13 = parts
    p10 = add(p10, got[0], got[1])
    p02 = add(p02, got[2])
    if side == 0:
        return batch_send(p02, 0, 1), batch_send(p03, 0, 3), batch_send(p10, 1, 0)
    return batch_send(p02, 0, 3), batch_send(p01, 0, 1), batch_send(p10, 1, 0)


def scatter_third(parts, got, side):
    if side == 0:
        return batch_send(add(parts[1], got), 0, 1)
    return batch_send(add(parts[3], got), 0, 3)


LANES = 128


PIECES = 4


def start_loads(source, target, sems):
    rows = source.shape[0] // PIECES
    copies = []
    for i in range(PIECES):
        part = pl.ds(i * rows, rows)
        copies.append(pltpu.make_async_copy(source.at[part], target.at[part], sems.at[i]))
        copies[-1].start()
    return copies


def wait_all(copies):
    for copy in copies:
        copy.wait()


in_vmem_spec = pl.BlockSpec(memory_space=pltpu.VMEM)
in_hbm_spec = pl.BlockSpec(memory_space=pltpu.HBM)


def in_hbm(value):
    return pltpu.with_memory_space_constraint(value, pltpu.HBM)


def local_kernel(kernel, outs, scratch, flops, moved, name, vmem=16, **specs):
    return pl.pallas_call(
        kernel,
        out_shape=outs,
        **specs,
        scratch_shapes=scratch,
        compiler_params=pltpu.CompilerParams(vmem_limit_bytes=vmem * 1024 * 1024),
        cost_estimate=pl.CostEstimate(flops=flops, bytes_accessed=moved, transcendentals=0),
        name=name,
    )


def nt(a, b):
    return lax.dot_general(a, b, (((1,), (1,)), ((), ())), preferred_element_type=F32)


PIECES = 4


def tn(a, b):
    return lax.dot_general(a, b, (((0,), (0,)), ((), ())), preferred_element_type=F32)


def front_kernel(
    each, tok_hbm, cot_hbm, par_hbm, rows_ref, disp_ref, comb_ref,
    slots_ref, flat_ref, tok_ref, cot_ref, par_ref, sems,
):
    par_loads = start_loads(par_hbm, par_ref, sems.at[0])
    tok_loads = start_loads(tok_hbm, tok_ref, sems.at[1])
    cot_loads = start_loads(cot_hbm, cot_ref, sems.at[2])
    wait_all(par_loads + tok_loads)
    tiles = slots_ref.shape[0]
    groups = slots_ref.shape[1] // each
    stride = 2 * each * tiles
    logits = nt(par_ref[...], tok_ref[...])
    raised = jnp.exp(logits - jnp.max(logits, axis=1, keepdims=True))
    dispatch = raised / jnp.sum(raised, axis=1, keepdims=True)
    raised = jnp.exp(logits - jnp.max(logits, axis=0, keepdims=True))
    combine = raised / jnp.sum(raised, axis=0, keepdims=True)
    disp_ref[...] = dispatch
    comb_ref[...] = combine
    for kind, (weights, values) in enumerate(((dispatch, tok_ref), (combine, cot_ref))):
        if kind == 1:
            wait_all(cot_loads)
        mixed = jnp.dot(weights.astype(BF16), values[...], preferred_element_type=F32)
        for k in range(tiles):
            slots_ref[k] = mixed[:, k * LANES : (k + 1) * LANES]
            for j in range(each):
                row = (kind * each + j) * tiles + k
                flat_ref[pl.ds(row, groups, stride=stride), :] = slots_ref[
                    k, pl.ds(j, groups, stride=each), :
                ]
    rows_ref[...] = flat_ref[...].astype(BF16)


def unpack_kernel(flat_in_ref, ins_ref, cots_ref, flat_ref):
    groups = ins_ref.shape[0]
    tiles = ins_ref.shape[1] // LANES
    flat_ref[...] = flat_in_ref[...].astype(F32)
    for kind, out_ref in enumerate((ins_ref, cots_ref)):
        for c in range(tiles):
            out_ref[:, c * LANES : (c + 1) * LANES] = flat_ref[
                pl.ds(kind * tiles + c, groups, stride=2 * tiles), :
            ].astype(BF16)


def pack_sum_kernel(*refs):
    out_ref, flat_ref = refs[-2:]
    groups = refs[0].shape[0]
    tiles = refs[0].shape[1] // LANES
    for kind in range(2):
        terms = refs[4 * kind : 4 * kind + 4]
        for c in range(tiles):
            cols = slice(c * LANES, (c + 1) * LANES)
            total = terms[0][:, cols].astype(F32)
            for term in terms[1:]:
                total = total + term[:, cols].astype(F32)
            flat_ref[pl.ds(kind * tiles + c, groups, stride=2 * tiles), :] = total
    out_ref[...] = flat_ref[...].astype(BF16)


def final_kernel(
    each, flat_in_ref, tok_ref, cot_ref, disp_ref, comb_ref, sig_ref, grad_ref, par_ref,
    flat_ref, out_f_ref, sig_f_ref,
):
    groups = sig_ref.shape[0] // each
    tiles = sig_ref.shape[1] // LANES
    stride = 2 * each * tiles
    flat_ref[...] = flat_in_ref[...].astype(F32)
    for kind, ref in enumerate((out_f_ref, sig_f_ref)):
        for j in range(each):
            for k in range(tiles):
                row = (kind * each + j) * tiles + k
                ref[k, pl.ds(j, groups, stride=each), :] = flat_ref[
                    pl.ds(row, groups, stride=stride), :
                ]
    slot_out = jnp.concatenate([out_f_ref[k].astype(BF16) for k in range(tiles)], axis=1)
    sig = jnp.concatenate([sig_f_ref[k].astype(BF16) for k in range(tiles)], axis=1)
    sig_ref[...] = sig
    combine_grad = nt(slot_out, cot_ref[...])
    dispatch_grad = nt(sig, tok_ref[...])
    combine = comb_ref[...]
    dispatch = disp_ref[...]
    combine_part = combine * (combine_grad - jnp.sum(combine * combine_grad, axis=0, keepdims=True))
    dispatch_part = dispatch * (
        dispatch_grad - jnp.sum(dispatch * dispatch_grad, axis=1, keepdims=True)
    )
    logits_grad = (combine_part + dispatch_part).astype(BF16)
    grad_ref[...] = logits_grad
    par_ref[...] = jnp.dot(logits_grad, tok_ref[...], preferred_element_type=F32).astype(BF16)


def gathered(blocks, j, width):
    return jnp.concatenate([b[:, j * width : (j + 1) * width] for b in blocks], axis=0)


def spread(parts, value, j, width):
    value = value.astype(BF16)
    groups = parts[0].shape[0]
    for i, part in enumerate(parts):
        part[:, j * width : (j + 1) * width] = value[i * groups : (i + 1) * groups]


def start_stores(sources, target, sems):
    rows = sources[0].shape[0]
    copies = []
    for i, source in enumerate(sources):
        part = target.at[pl.ds(i * rows, rows)]
        copies.append(pltpu.make_async_copy(source, part, sems.at[i]))
        copies[-1].start()
    return copies


def forward_kernel(count, each, *refs):
    blocks, (win_hbm, wout_hbm) = refs[:count], refs[count : count + 2]
    parts, (slope_ref, rows_hbm, act_hbm) = refs[count + 2 : 2 * count + 2], refs[-10:-7]
    win_ref, wout_ref, act_ref, sems, row_sems, kept_sems, win_sems = refs[-7:]
    width, hidden = win_ref.shape[1:]
    win_loads = [start_loads(win_hbm.at[j], win_ref.at[j], win_sems.at[j]) for j in range(each)]
    wout_loads = [start_loads(wout_hbm.at[j], wout_ref.at[j], sems.at[j]) for j in range(each)]
    stores = start_stores(blocks, rows_hbm, row_sems)
    for j in range(each):
        hid = slice(j * hidden, (j + 1) * hidden)
        wait_all(win_loads[j])
        pre_act = jnp.dot(gathered(blocks, j, width), win_ref[j], preferred_element_type=F32)
        gelu_value, slope_ref[:, hid] = gelu_pair(pre_act)
        act_ref[:, hid] = gelu_value.astype(BF16)
    stores += start_stores([act_ref], act_hbm, kept_sems)
    for j in range(each):
        hid = slice(j * hidden, (j + 1) * hidden)
        wait_all(wout_loads[j])
        spread(parts, jnp.dot(act_ref[:, hid], wout_ref[j], preferred_element_type=F32), j, width)
    wait_all(stores)


def backward_kernel(count, each, *refs):
    blocks, (slope_ref, wout_ref, win_hbm) = refs[:count], refs[count : count + 3]
    parts, (rows_hbm, pre_hbm) = refs[count + 3 : 2 * count + 3], refs[-7:-5]
    win_ref, pre_ref, sems, row_sems, kept_sems = refs[-5:]
    width, hidden = win_ref.shape[1:]
    win_loads = [start_loads(win_hbm.at[j], win_ref.at[j], sems.at[j]) for j in range(each)]
    stores = start_stores(blocks, rows_hbm, row_sems)
    for j in range(each):
        hid = slice(j * hidden, (j + 1) * hidden)
        act_grad = nt(gathered(blocks, j, width), wout_ref[j])
        pre_ref[:, hid] = (act_grad * slope_ref[:, hid]).astype(BF16)
    stores += start_stores([pre_ref], pre_hbm, kept_sems)
    for j in range(each):
        hid = slice(j * hidden, (j + 1) * hidden)
        wait_all(win_loads[j])
        spread(parts, nt(pre_ref[:, hid], win_ref[j]), j, width)
    wait_all(stores)


def expert_step(kernel, name, blocks, extra, in_place, first, second, hidden, load_first):
    count = len(blocks)
    each, width = first.shape[0], first.shape[1] * first.shape[2] // hidden
    rows = count * blocks[0].shape[0]
    kept = jax.ShapeDtypeStruct((rows, each * hidden), BF16)
    outs = local_kernel(
        functools.partial(kernel, count, each),
        [jax.ShapeDtypeStruct(b.shape, BF16) for b in blocks]
        + [jax.ShapeDtypeStruct((rows, each * hidden), F32)] * in_place
        + [pltpu.HBM((rows, each * width), BF16), pltpu.HBM(kept.shape, BF16)],
        [pltpu.VMEM(first.shape, BF16)] * load_first
        + [
            pltpu.VMEM(second.shape, BF16),
            pltpu.VMEM(kept.shape, BF16),
            pltpu.SemaphoreType.DMA((each, PIECES)),
            pltpu.SemaphoreType.DMA((count,)),
            pltpu.SemaphoreType.DMA((1,)),
        ]
        + [pltpu.SemaphoreType.DMA((each, PIECES))] * load_first,
        4 * rows * each * width * hidden,
        4 * each * width * hidden + 4 * rows * each * width,
        name,
        in_specs=[in_vmem_spec] * (count + len(extra) + 1 - load_first)
        + [in_hbm_spec] * (1 + load_first),
        out_specs=[in_vmem_spec] * (count + in_place) + [in_hbm_spec] * 2,
    )(*blocks, *extra, in_hbm(first) if load_first else first, in_hbm(second))
    return outs[:count], *outs[count:]


def weights_kernel(ins_ref, cots_ref, act_ref, pre_ref, gin_ref, gout_ref):
    gin_ref[0] = tn(ins_ref[...], pre_ref[...]).astype(BF16)
    gout_ref[0] = tn(act_ref[...], cots_ref[...]).astype(BF16)


def weight_gradients(ins, cots, act, pre, each):
    cuts = 2
    rows = ins.shape[0]
    width, hidden = ins.shape[1] // each, act.shape[1] // each
    return local_kernel(
        weights_kernel,
        (
            jax.ShapeDtypeStruct((each, width, hidden), BF16),
            jax.ShapeDtypeStruct((each, hidden, width), BF16),
        ),
        [],
        4 * rows * each * width * hidden,
        4 * each * width * hidden + 8 * rows * each * width,
        "weight_grads",
        grid=(each, cuts),
        in_specs=[
            pl.BlockSpec((rows, width // cuts), lambda e, i: (0, e * cuts + i)),
            pl.BlockSpec((rows, width), lambda e, i: (0, e)),
            pl.BlockSpec((rows, hidden // cuts), lambda e, i: (0, e * cuts + i)),
            pl.BlockSpec((rows, hidden), lambda e, i: (0, e)),
        ],
        out_specs=(
            pl.BlockSpec((1, width // cuts, hidden), lambda e, i: (e, i, 0)),
            pl.BlockSpec((1, hidden // cuts, width), lambda e, i: (e, i, 0)),
        ),
    )(in_hbm(ins), in_hbm(cots), in_hbm(act), in_hbm(pre))


def crossed_send(value, step, turn):
    pairs = []
    for z in range(ZL):
        for x in range(X):
            for y in range(Y):
                for h in range(ZH):
                    for c in range(CORE):
                        along_x = (c + turn) % 2 == 0
                        tx = (x + step) % X if along_x else x
                        ty = y if along_x else (y + step) % Y
                        here = ((z * X + x) * Y + y) * ZH + h
                        there = ((z * X + tx) * Y + ty) * ZH + h
                        pairs.append((here * CORE + c, there * CORE + c))
    return lax.ppermute(value, ("batch", "expert"), pairs)


def depth_swap(value, step):
    depth = ZL * ZH
    pairs = []
    for z in range(depth):
        to = (z + (step if z % 2 else -step)) % depth
        for x in range(X):
            for y in range(Y):
                for c in range(CORE):
                    here, there = (
                        ((k % ZL * X + x) * Y + y) * ZH * CORE + k // ZL * CORE + c for k in (z, to)
                    )
                    pairs.append((here, there))
    return lax.ppermute(value, ("batch", "expert"), pairs)


def sum_all(partial, beside):
    core = lax.axis_index("expert") % CORE
    half = partial.shape[0] // CORE
    keep = lax.dynamic_slice_in_dim(partial, core * half, half)
    give = lax.dynamic_slice_in_dim(partial, (1 - core) * half, half)
    total = add(keep, expert_send(give, 0, 0, 1))
    total = add(total, *[crossed_send(total, k, 0) for k in range(1, X)])
    total = add(total, *[crossed_send(total, k, 1) for k in range(1, X)])
    total = add(total, batch_send(total, 1, 0))
    total, beside = together(total, beside)
    total = add(total, depth_swap(total, 1))
    total = add(total, depth_swap(total, -3))
    other = expert_send(total, 0, 0, 1)
    first = jnp.where(core == 0, total, other)
    second = jnp.where(core == 0, other, total)
    return jnp.concatenate([first, second], axis=0).astype(F32), beside


def body(tokens, slot_params, weight_in, weight_out, output_grad):
    tokens, output_grad = tokens[0], output_grad[0]
    patches, width = tokens.shape
    slots = slot_params.shape[1]
    groups = lax.axis_size("expert")
    each = slots // groups
    tiles = width // LANES
    flat = groups * 2 * each * tiles
    params = slot_params.T
    flat_shape = jax.ShapeDtypeStruct((flat, LANES), BF16)
    square = pltpu.VMEM((slots, patches), F32)
    dot_flops = 2 * slots * patches * width
    rows, dispatch, combine = local_kernel(
        functools.partial(front_kernel, each),
        (flat_shape, square, square),
        [
            pltpu.VMEM((tiles, slots, LANES), F32),
            pltpu.VMEM((flat, LANES), F32),
            pltpu.VMEM((patches, width), BF16),
            pltpu.VMEM((patches, width), BF16),
            pltpu.VMEM((slots, width), BF16),
            pltpu.SemaphoreType.DMA((3, PIECES)),
        ],
        3 * dot_flops,
        4 * patches * width + 2 * flat * LANES,
        "front",
        in_specs=[in_hbm_spec] * 3,
        out_specs=(in_vmem_spec,) * 3,
    )(in_hbm(tokens), in_hbm(output_grad), in_hbm(params))
    routed = lax.all_to_all(
        rows.reshape(groups, 2 * each * tiles, LANES), "expert", split_axis=0, concat_axis=0,
        tiled=True,
    ).reshape(flat, LANES)
    half_shape = jax.ShapeDtypeStruct((groups, each * width), BF16)
    ins, cots = local_kernel(
        unpack_kernel,
        (half_shape, half_shape),
        [pltpu.VMEM((flat, LANES), F32)],
        0,
        4 * flat * LANES,
        "unpack",
    )(routed)
    hidden = weight_in.shape[2]
    near_a = gather_near(ins)
    near_b = gather_near(cots)
    near_a = together(*near_a)
    next_a = gather_next(near_a)
    near_b = together(*near_b)
    next_b = gather_next(near_b)
    next_a = together(*next_a)
    far_a = gather_far(next_a, 0)
    next_b = together(*next_b)
    far_b = gather_far(next_b, 1)
    blocks_a = by_offset(ins, near_a, next_a, far_a)
    blocks_b = by_offset(cots, near_b, next_b, far_b)
    parts_a, slope, rows_a, act = expert_step(
        forward_kernel, "expert_forward", blocks_a, [], 1, weight_in, weight_out, hidden, 1
    )
    sent_a = batch_send(parts_a[5], 0, 1), batch_send(parts_a[6], 1, 0)
    parts_b, rows_b, pre = expert_step(
        backward_kernel, "expert_backward", blocks_b, [slope], 0, weight_out, weight_in, hidden, 0
    )
    first_b = scatter_first(parts_b)
    parts_a, pre = together(parts_a, pre)
    first_a = sent_a[0], batch_send(parts_a[7], 0, 3), sent_a[1]
    first_a, parts_a = together(first_a, parts_a)
    second_a = scatter_second(parts_a, first_a, 0)
    first_b, parts_b = together(first_b, parts_b)
    second_b = scatter_second(parts_b, first_b, 1)
    second_a = together(*second_a)
    third_a = scatter_third(parts_a, second_a[0], 0)
    second_b = together(*second_b)
    third_b = scatter_third(parts_b, second_b[0], 1)
    share = (parts_a[0], *second_a[1:], third_a, parts_b[0], *second_b[1:], third_b)
    packed = local_kernel(
        pack_sum_kernel,
        flat_shape,
        [pltpu.VMEM((flat, LANES), F32)],
        0,
        10 * flat * LANES,
        "pack_sum",
    )(*share)
    packed, act, pre = together(packed, act, pre)
    back = lax.all_to_all(
        packed.reshape(groups, 2 * each * tiles, LANES), "expert", split_axis=0, concat_axis=0,
        tiled=True,
    ).reshape(flat, LANES)
    weight_grads = weight_gradients(rows_a, rows_b, act, pre, each)
    back, weight_grads = lax.optimization_barrier((back, weight_grads))
    row_shape = jax.ShapeDtypeStruct((slots, width), BF16)
    slot_in_grad, logits_grad, local_params = local_kernel(
        functools.partial(final_kernel, each),
        (row_shape, jax.ShapeDtypeStruct((slots, patches), BF16), row_shape),
        [
            pltpu.VMEM((flat, LANES), F32),
            pltpu.VMEM((tiles, slots, LANES), F32),
            pltpu.VMEM((tiles, slots, LANES), F32),
        ],
        3 * dot_flops,
        4 * patches * width + 2 * flat * LANES,
        "final",
    )(back, tokens, output_grad, dispatch, combine)
    tokens_grad = (
        jnp.einsum("sm,sd->md", dispatch.astype(BF16), slot_in_grad, preferred_element_type=F32)
        + jnp.einsum("sm,sd->md", logits_grad, params, preferred_element_type=F32)
    ).astype(BF16)
    total_images = lax.axis_size("batch") * groups
    params_sum, tokens_grad = sum_all(local_params, tokens_grad)
    params_grad = (params_sum / total_images).T
    return (tokens_grad[None], params_grad, *weight_grads)


def solution(mesh):
    in_specs = (
        P(("batch", "expert"), None, None),
        P(),
        P("expert", None, "batch"),
        P("expert", "batch", None),
        P(("batch", "expert"), None, None),
    )
    out_specs = (
        P(("batch", "expert"), None, None),
        P(),
        P("expert", None, "batch"),
        P("expert", "batch", None),
    )
    return jax.shard_map(body, mesh=mesh, in_specs=in_specs, out_specs=out_specs, check_vma=False)
```

```python
import functools
import math

import jax
import jax.numpy as jnp
from jax import lax
from jax.experimental import pallas as pl
from jax.experimental.pallas import tpu as pltpu
from jax.sharding import PartitionSpec as P

GELU_CUBIC = 0.044715
GELU_ROOT = math.sqrt(2.0 / math.pi)
BF16 = jnp.bfloat16
F32 = jnp.float32

X, ZL, Y, ZH, CORE = 4, 2, 4, 4, 2


def gelu_pair(pre_act):
    tanh_arg = GELU_ROOT * (pre_act + GELU_CUBIC * pre_act * pre_act * pre_act)
    tanh_value = jnp.tanh(tanh_arg)
    gelu_value = 0.5 * pre_act * (1.0 + tanh_value)
    gelu_slope = 0.5 * (1.0 + tanh_value) + 0.5 * pre_act * (
        1.0 - tanh_value * tanh_value
    ) * GELU_ROOT * (1.0 + 3.0 * GELU_CUBIC * pre_act * pre_act)
    return (gelu_value, gelu_slope)


def batch_send(value, dz, dx):
    pairs = [
        (z * X + x, ((z + dz) % ZL) * X + (x + dx) % X) for z in range(ZL) for x in range(X)
    ]
    return lax.ppermute(value, "batch", pairs)


def batch_fetch(value, dz, dx):
    return batch_send(value, -dz, -dx)


def expert_send(value, dy, dh, dc):
    pairs = []
    for y in range(Y):
        for h in range(ZH):
            for c in range(CORE):
                to = (((y + dy) % Y) * ZH + (h + dh) % ZH) * CORE + (c + dc) % CORE
                pairs.append(((y * ZH + h) * CORE + c, to))
    return lax.ppermute(value, "expert", pairs)


def add(*terms):
    total = terms[0].astype(F32)
    for term in terms[1:]:
        total = total + term.astype(F32)
    return total.astype(BF16)


def together(*values):
    return lax.optimization_barrier(values)


def gather_near(mine):
    return batch_fetch(mine, 0, 1), batch_fetch(mine, 0, 3), batch_fetch(mine, 1, 0)


def gather_next(near):
    b01, b03, b10 = near
    return batch_fetch(b01, 0, 1), batch_fetch(b10, 0, 3), batch_fetch(b01, 1, 0)


def gather_far(nexts, side):
    b02, b13, b11 = nexts
    return batch_fetch(b11, 0, 1) if side == 0 else batch_fetch(b13, 0, 3)


def by_offset(mine, near, nexts, far):
    return [mine, near[0], nexts[0], near[1], near[2], nexts[2], far, nexts[1]]


def scatter_first(parts):
    p00, p01, p02, p03, p10, p11, p12, p13 = parts
    return batch_send(p11, 0, 1), batch_send(p13, 0, 3), batch_send(p12, 1, 0)


def scatter_second(parts, got, side):
    p00, p01, p02, p03, p10, p11, p12, p13 = parts
    p10 = add(p10, got[0], got[1])
    p02 = add(p02, got[2])
    if side == 0:
        return batch_send(p02, 0, 1), batch_send(p03, 0, 3), batch_send(p10, 1, 0)
    return batch_send(p02, 0, 3), batch_send(p01, 0, 1), batch_send(p10, 1, 0)


def scatter_third(parts, got, side):
    if side == 0:
        return batch_send(add(parts[1], got), 0, 1)
    return batch_send(add(parts[3], got), 0, 3)


LANES = 128


PIECES = 8


def start_loads(source, target, sems):
    pieces = min(PIECES, source.shape[0] // 16)
    rows = source.shape[0] // pieces
    copies = []
    for i in range(pieces):
        part = pl.ds(i * rows, rows)
        copies.append(pltpu.make_async_copy(source.at[part], target.at[part], sems.at[i]))
        copies[-1].start()
    return copies


def wait_all(copies):
    for copy in copies:
        copy.wait()


in_vmem_spec = pl.BlockSpec(memory_space=pltpu.VMEM)
in_hbm_spec = pl.BlockSpec(memory_space=pltpu.HBM)


def in_hbm(value):
    return pltpu.with_memory_space_constraint(value, pltpu.HBM)


def local_kernel(kernel, outs, scratch, flops, moved, name, vmem=16, **specs):
    return pl.pallas_call(
        kernel,
        out_shape=outs,
        **specs,
        scratch_shapes=scratch,
        compiler_params=pltpu.CompilerParams(vmem_limit_bytes=vmem * 1024 * 1024),
        cost_estimate=pl.CostEstimate(flops=flops, bytes_accessed=moved, transcendentals=0),
        name=name,
    )


def nt(a, b):
    return lax.dot_general(a, b, (((1,), (1,)), ((), ())), preferred_element_type=F32)


PIECES = 8


def tn(a, b):
    return lax.dot_general(a, b, (((0,), (0,)), ((), ())), preferred_element_type=F32)


def front_kernel(
    each, tok_hbm, cot_hbm, par_hbm, rows_ref, disp_ref, comb_ref,
    slots_ref, flat_ref, tok_ref, cot_ref, par_ref, sems,
):
    par_loads = start_loads(par_hbm, par_ref, sems.at[0])
    tok_loads = start_loads(tok_hbm, tok_ref, sems.at[1])
    cot_loads = start_loads(cot_hbm, cot_ref, sems.at[2])
    wait_all(par_loads + tok_loads)
    tiles = slots_ref.shape[0]
    groups = slots_ref.shape[1] // each
    stride = 2 * each * tiles
    logits = nt(par_ref[...], tok_ref[...])
    raised = jnp.exp(logits - jnp.max(logits, axis=1, keepdims=True))
    dispatch = raised / jnp.sum(raised, axis=1, keepdims=True)
    raised = jnp.exp(logits - jnp.max(logits, axis=0, keepdims=True))
    combine = raised / jnp.sum(raised, axis=0, keepdims=True)
    disp_ref[...] = dispatch
    comb_ref[...] = combine
    for kind, (weights, values) in enumerate(((dispatch, tok_ref), (combine, cot_ref))):
        if kind == 1:
            wait_all(cot_loads)
        mixed = jnp.dot(weights.astype(BF16), values[...], preferred_element_type=F32)
        for k in range(tiles):
            slots_ref[k] = mixed[:, k * LANES : (k + 1) * LANES]
            for j in range(each):
                row = (kind * each + j) * tiles + k
                flat_ref[pl.ds(row, groups, stride=stride), :] = slots_ref[
                    k, pl.ds(j, groups, stride=each), :
                ]
    rows_ref[...] = flat_ref[...].astype(BF16)


def unpack_kernel(flat_in_ref, ins_ref, cots_ref, flat_ref):
    groups = ins_ref.shape[0]
    tiles = ins_ref.shape[1] // LANES
    flat_ref[...] = flat_in_ref[...].astype(F32)
    for kind, out_ref in enumerate((ins_ref, cots_ref)):
        for c in range(tiles):
            out_ref[:, c * LANES : (c + 1) * LANES] = flat_ref[
                pl.ds(kind * tiles + c, groups, stride=2 * tiles), :
            ].astype(BF16)


def pack_sum_kernel(*refs):
    out_ref, flat_ref = refs[-2:]
    groups = refs[0].shape[0]
    tiles = refs[0].shape[1] // LANES
    for kind in range(2):
        terms = refs[4 * kind : 4 * kind + 4]
        for c in range(tiles):
            cols = slice(c * LANES, (c + 1) * LANES)
            total = terms[0][:, cols].astype(F32)
            for term in terms[1:]:
                total = total + term[:, cols].astype(F32)
            flat_ref[pl.ds(kind * tiles + c, groups, stride=2 * tiles), :] = total
    out_ref[...] = flat_ref[...].astype(BF16)


def final_kernel(
    each, flat_in_ref, tok_ref, cot_ref, disp_ref, comb_ref, sig_ref, grad_ref, par_ref,
    flat_ref, out_f_ref, sig_f_ref,
):
    groups = sig_ref.shape[0] // each
    tiles = sig_ref.shape[1] // LANES
    stride = 2 * each * tiles
    flat_ref[...] = flat_in_ref[...].astype(F32)
    for kind, ref in enumerate((out_f_ref, sig_f_ref)):
        for j in range(each):
            for k in range(tiles):
                row = (kind * each + j) * tiles + k
                ref[k, pl.ds(j, groups, stride=each), :] = flat_ref[
                    pl.ds(row, groups, stride=stride), :
                ]
    slot_out = jnp.concatenate([out_f_ref[k].astype(BF16) for k in range(tiles)], axis=1)
    sig = jnp.concatenate([sig_f_ref[k].astype(BF16) for k in range(tiles)], axis=1)
    sig_ref[...] = sig
    combine_grad = nt(slot_out, cot_ref[...])
    dispatch_grad = nt(sig, tok_ref[...])
    combine = comb_ref[...]
    dispatch = disp_ref[...]
    combine_part = combine * (combine_grad - jnp.sum(combine * combine_grad, axis=0, keepdims=True))
    dispatch_part = dispatch * (
        dispatch_grad - jnp.sum(dispatch * dispatch_grad, axis=1, keepdims=True)
    )
    logits_grad = (combine_part + dispatch_part).astype(BF16)
    grad_ref[...] = logits_grad
    par_ref[...] = jnp.dot(logits_grad, tok_ref[...], preferred_element_type=F32).astype(BF16)


def gathered(blocks, j, width):
    return jnp.concatenate([b[:, j * width : (j + 1) * width] for b in blocks], axis=0)


def spread(parts, value, j, width):
    value = value.astype(BF16)
    groups = parts[0].shape[0]
    for i, part in enumerate(parts):
        part[:, j * width : (j + 1) * width] = value[i * groups : (i + 1) * groups]


def start_stores(sources, target, sems):
    rows = sources[0].shape[0]
    copies = []
    for i, source in enumerate(sources):
        part = target.at[pl.ds(i * rows, rows)]
        copies.append(pltpu.make_async_copy(source, part, sems.at[i]))
        copies[-1].start()
    return copies


def forward_kernel(count, each, *refs):
    blocks, (win_hbm, wout_hbm) = refs[:count], refs[count : count + 2]
    parts, (slope_ref, rows_hbm, act_hbm) = refs[count + 2 : 2 * count + 2], refs[-10:-7]
    win_ref, wout_ref, act_ref, sems, row_sems, kept_sems, win_sems = refs[-7:]
    width, hidden = win_ref.shape[1:]
    win_loads = [start_loads(win_hbm.at[j], win_ref.at[j], win_sems.at[j]) for j in range(each)]
    wout_loads = [start_loads(wout_hbm.at[j], wout_ref.at[j], sems.at[j]) for j in range(each)]
    stores = start_stores(blocks, rows_hbm, row_sems)
    for j in range(each):
        hid = slice(j * hidden, (j + 1) * hidden)
        wait_all(win_loads[j])
        pre_act = jnp.dot(gathered(blocks, j, width), win_ref[j], preferred_element_type=F32)
        gelu_value, slope_ref[:, hid] = gelu_pair(pre_act)
        act_ref[:, hid] = gelu_value.astype(BF16)
    stores += start_stores([act_ref], act_hbm, kept_sems)
    for j in range(each):
        hid = slice(j * hidden, (j + 1) * hidden)
        wait_all(wout_loads[j])
        spread(parts, jnp.dot(act_ref[:, hid], wout_ref[j], preferred_element_type=F32), j, width)
    wait_all(stores)


def backward_kernel(count, each, *refs):
    blocks, (slope_ref, wout_ref, win_hbm) = refs[:count], refs[count : count + 3]
    parts, (rows_hbm, pre_hbm) = refs[count + 3 : 2 * count + 3], refs[-7:-5]
    win_ref, pre_ref, sems, row_sems, kept_sems = refs[-5:]
    width, hidden = win_ref.shape[1:]
    win_loads = [start_loads(win_hbm.at[j], win_ref.at[j], sems.at[j]) for j in range(each)]
    stores = start_stores(blocks, rows_hbm, row_sems)
    for j in range(each):
        hid = slice(j * hidden, (j + 1) * hidden)
        act_grad = nt(gathered(blocks, j, width), wout_ref[j])
        pre_ref[:, hid] = (act_grad * slope_ref[:, hid]).astype(BF16)
    stores += start_stores([pre_ref], pre_hbm, kept_sems)
    for j in range(each):
        hid = slice(j * hidden, (j + 1) * hidden)
        wait_all(win_loads[j])
        spread(parts, nt(pre_ref[:, hid], win_ref[j]), j, width)
    wait_all(stores)


def expert_step(kernel, name, blocks, extra, in_place, first, second, hidden, load_first):
    count = len(blocks)
    each, width = first.shape[0], first.shape[1] * first.shape[2] // hidden
    rows = count * blocks[0].shape[0]
    kept = jax.ShapeDtypeStruct((rows, each * hidden), BF16)
    outs = local_kernel(
        functools.partial(kernel, count, each),
        [jax.ShapeDtypeStruct(b.shape, BF16) for b in blocks]
        + [jax.ShapeDtypeStruct((rows, each * hidden), F32)] * in_place
        + [pltpu.HBM((rows, each * width), BF16), pltpu.HBM(kept.shape, BF16)],
        [pltpu.VMEM(first.shape, BF16)] * load_first
        + [
            pltpu.VMEM(second.shape, BF16),
            pltpu.VMEM(kept.shape, BF16),
            pltpu.SemaphoreType.DMA((each, PIECES)),
            pltpu.SemaphoreType.DMA((count,)),
            pltpu.SemaphoreType.DMA((1,)),
        ]
        + [pltpu.SemaphoreType.DMA((each, PIECES))] * load_first,
        4 * rows * each * width * hidden,
        4 * each * width * hidden + 4 * rows * each * width,
        name,
        in_specs=[in_vmem_spec] * (count + len(extra) + 1 - load_first)
        + [in_hbm_spec] * (1 + load_first),
        out_specs=[in_vmem_spec] * (count + in_place) + [in_hbm_spec] * 2,
    )(*blocks, *extra, in_hbm(first) if load_first else first, in_hbm(second))
    return outs[:count], *outs[count:]


def weights_kernel(ins_ref, cots_ref, act_ref, pre_ref, gin_ref, gout_ref):
    gin_ref[0] = tn(ins_ref[...], pre_ref[...]).astype(BF16)
    gout_ref[0] = tn(act_ref[...], cots_ref[...]).astype(BF16)


def weight_gradients(ins, cots, act, pre, each):
    cuts = 2
    rows = ins.shape[0]
    width, hidden = ins.shape[1] // each, act.shape[1] // each
    return local_kernel(
        weights_kernel,
        (
            jax.ShapeDtypeStruct((each, width, hidden), BF16),
            jax.ShapeDtypeStruct((each, hidden, width), BF16),
        ),
        [],
        4 * rows * each * width * hidden,
        4 * each * width * hidden + 8 * rows * each * width,
        "weight_grads",
        grid=(each, cuts),
        in_specs=[
            pl.BlockSpec((rows, width // cuts), lambda e, i: (0, e * cuts + i)),
            pl.BlockSpec((rows, width), lambda e, i: (0, e)),
            pl.BlockSpec((rows, hidden // cuts), lambda e, i: (0, e * cuts + i)),
            pl.BlockSpec((rows, hidden), lambda e, i: (0, e)),
        ],
        out_specs=(
            pl.BlockSpec((1, width // cuts, hidden), lambda e, i: (e, i, 0)),
            pl.BlockSpec((1, hidden // cuts, width), lambda e, i: (e, i, 0)),
        ),
    )(in_hbm(ins), in_hbm(cots), in_hbm(act), in_hbm(pre))


def crossed_send(value, step, turn):
    pairs = []
    for z in range(ZL):
        for x in range(X):
            for y in range(Y):
                for h in range(ZH):
                    for c in range(CORE):
                        along_x = (c + turn) % 2 == 0
                        tx = (x + step) % X if along_x else x
                        ty = y if along_x else (y + step) % Y
                        here = ((z * X + x) * Y + y) * ZH + h
                        there = ((z * X + tx) * Y + ty) * ZH + h
                        pairs.append((here * CORE + c, there * CORE + c))
    return lax.ppermute(value, ("batch", "expert"), pairs)


def depth_swap(value, step):
    depth = ZL * ZH
    pairs = []
    for z in range(depth):
        to = (z + (step if z % 2 else -step)) % depth
        for x in range(X):
            for y in range(Y):
                for c in range(CORE):
                    here, there = (
                        ((k % ZL * X + x) * Y + y) * ZH * CORE + k // ZL * CORE + c for k in (z, to)
                    )
                    pairs.append((here, there))
    return lax.ppermute(value, ("batch", "expert"), pairs)


def sum_all(partial, beside):
    core = lax.axis_index("expert") % CORE
    half = partial.shape[0] // CORE
    keep = lax.dynamic_slice_in_dim(partial, core * half, half)
    give = lax.dynamic_slice_in_dim(partial, (1 - core) * half, half)
    total = add(keep, expert_send(give, 0, 0, 1))
    total = add(total, *[crossed_send(total, k, 0) for k in range(1, X)])
    total = add(total, *[crossed_send(total, k, 1) for k in range(1, X)])
    total = add(total, batch_send(total, 1, 0))
    total, beside = together(total, beside)
    total = add(total, depth_swap(total, 1))
    total = add(total, depth_swap(total, -3))
    other = expert_send(total, 0, 0, 1)
    first = jnp.where(core == 0, total, other)
    second = jnp.where(core == 0, other, total)
    return jnp.concatenate([first, second], axis=0).astype(F32), beside


def body(tokens, slot_params, weight_in, weight_out, output_grad):
    tokens, output_grad = tokens[0], output_grad[0]
    patches, width = tokens.shape
    slots = slot_params.shape[1]
    groups = lax.axis_size("expert")
    each = slots // groups
    tiles = width // LANES
    flat = groups * 2 * each * tiles
    params = slot_params.T
    flat_shape = jax.ShapeDtypeStruct((flat, LANES), BF16)
    square = pltpu.VMEM((slots, patches), F32)
    dot_flops = 2 * slots * patches * width
    rows, dispatch, combine = local_kernel(
        functools.partial(front_kernel, each),
        (flat_shape, square, square),
        [
            pltpu.VMEM((tiles, slots, LANES), F32),
            pltpu.VMEM((flat, LANES), F32),
            pltpu.VMEM((patches, width), BF16),
            pltpu.VMEM((patches, width), BF16),
            pltpu.VMEM((slots, width), BF16),
            pltpu.SemaphoreType.DMA((3, PIECES)),
        ],
        3 * dot_flops,
        4 * patches * width + 2 * flat * LANES,
        "front",
        in_specs=[in_hbm_spec] * 3,
        out_specs=(in_vmem_spec,) * 3,
    )(in_hbm(tokens), in_hbm(output_grad), in_hbm(params))
    routed = lax.all_to_all(
        rows.reshape(groups, 2 * each * tiles, LANES), "expert", split_axis=0, concat_axis=0,
        tiled=True,
    ).reshape(flat, LANES)
    half_shape = jax.ShapeDtypeStruct((groups, each * width), BF16)
    ins, cots = local_kernel(
        unpack_kernel,
        (half_shape, half_shape),
        [pltpu.VMEM((flat, LANES), F32)],
        0,
        4 * flat * LANES,
        "unpack",
    )(routed)
    hidden = weight_in.shape[2]
    near_a = gather_near(ins)
    near_b = gather_near(cots)
    near_a = together(*near_a)
    next_a = gather_next(near_a)
    near_b = together(*near_b)
    next_b = gather_next(near_b)
    next_a = together(*next_a)
    far_a = gather_far(next_a, 0)
    next_b = together(*next_b)
    far_b = gather_far(next_b, 1)
    blocks_a = by_offset(ins, near_a, next_a, far_a)
    blocks_b = by_offset(cots, near_b, next_b, far_b)
    parts_a, slope, rows_a, act = expert_step(
        forward_kernel, "expert_forward", blocks_a, [], 1, weight_in, weight_out, hidden, 1
    )
    first_a = scatter_first(parts_a)
    parts_b, rows_b, pre = expert_step(
        backward_kernel, "expert_backward", blocks_b, [slope], 0, weight_out, weight_in, hidden, 0
    )
    first_b = scatter_first(parts_b)
    first_a, parts_a, pre = together(first_a, parts_a, pre)
    second_a = scatter_second(parts_a, first_a, 0)
    first_b, parts_b = together(first_b, parts_b)
    second_b = scatter_second(parts_b, first_b, 1)
    second_a = together(*second_a)
    third_a = scatter_third(parts_a, second_a[0], 0)
    second_b = together(*second_b)
    third_b = scatter_third(parts_b, second_b[0], 1)
    share = (parts_a[0], *second_a[1:], third_a, parts_b[0], *second_b[1:], third_b)
    packed = local_kernel(
        pack_sum_kernel,
        flat_shape,
        [pltpu.VMEM((flat, LANES), F32)],
        0,
        10 * flat * LANES,
        "pack_sum",
    )(*share)
    packed, act, pre = together(packed, act, pre)
    back = lax.all_to_all(
        packed.reshape(groups, 2 * each * tiles, LANES), "expert", split_axis=0, concat_axis=0,
        tiled=True,
    ).reshape(flat, LANES)
    weight_grads = weight_gradients(rows_a, rows_b, act, pre, each)
    back, weight_grads = lax.optimization_barrier((back, weight_grads))
    row_shape = jax.ShapeDtypeStruct((slots, width), BF16)
    slot_in_grad, logits_grad, local_params = local_kernel(
        functools.partial(final_kernel, each),
        (row_shape, jax.ShapeDtypeStruct((slots, patches), BF16), row_shape),
        [
            pltpu.VMEM((flat, LANES), F32),
            pltpu.VMEM((tiles, slots, LANES), F32),
            pltpu.VMEM((tiles, slots, LANES), F32),
        ],
        3 * dot_flops,
        4 * patches * width + 2 * flat * LANES,
        "final",
    )(back, tokens, output_grad, dispatch, combine)
    tokens_grad = (
        jnp.einsum("sm,sd->md", dispatch.astype(BF16), slot_in_grad, preferred_element_type=F32)
        + jnp.einsum("sm,sd->md", logits_grad, params, preferred_element_type=F32)
    ).astype(BF16)
    total_images = lax.axis_size("batch") * groups
    params_sum, tokens_grad = sum_all(local_params, tokens_grad)
    params_grad = (params_sum / total_images).T
    return (tokens_grad[None], params_grad, *weight_grads)


def solution(mesh):
    in_specs = (
        P(("batch", "expert"), None, None),
        P(),
        P("expert", None, "batch"),
        P("expert", "batch", None),
        P(("batch", "expert"), None, None),
    )
    out_specs = (
        P(("batch", "expert"), None, None),
        P(),
        P("expert", None, "batch"),
        P("expert", "batch", None),
    )
    return jax.shard_map(body, mesh=mesh, in_specs=in_specs, out_specs=out_specs, check_vma=False)
```
